256 devices in a mesh: batch: 16 (over y, x), proto: 16 (over z, core).
Axes of the slice: x: 4, y: 4, z: 8, core: 2. Of those that a mesh axis runs over, the one named last changes fastest.
Arguments:
- teacher_emb: bfloat16 [256, 8192], P('proto', 'batch'), may hold values from -22 to 22
- student_emb: bfloat16 [256, 8192], P('proto', 'batch'), may hold values from -6 to 6
- prototypes: bfloat16 [256, 65536], P('batch', 'proto'), may hold values from -16 to 16
Outputs:
- grad_proto: float32 [256, 65536], P('batch', 'proto')
- grad_student: float32 [256, 8192], P('proto', 'batch')
- loss: float32 [], replicated
The draws below stay inside these ranges and needn't reach their ends.
All inputs are finite; a program needn't handle non-finite values.
Results may differ from the reference program's by a relative error of at most 0.00055.
The reference program's roundings to bfloat16 on the way (of `proto_unit` and `grad_logit`) count: a program that leaves them out, or rounds other values in their place, can miss the bound.
Values may be sent and summed in bfloat16 or wider, within the bound.
A program may use at most 64 MiB of HBM per device.

```python
import jax
import jax.numpy as jnp
from jax import lax

K = 256
PROTOS = 65536
ROWS_DEV = 512
ITERS = 3
CROPS = 8192


def common_axis(key):
    return jnp.clip(jax.random.normal(jax.random.fold_in(key, 7), (K, 1), jnp.float32), -4.0, 4.0)


def draw_teacher_emb(key, part):
    direction = common_axis(key)
    noise = jnp.clip(jax.random.normal(jax.random.fold_in(key, 1), (K, CROPS), jnp.float32), -6.0, 6.0)
    reach = 3.0
    trend = reach * jnp.arange(CROPS, dtype=jnp.float32) / CROPS
    return (noise + trend[None, :] * direction).astype(jnp.bfloat16)


def draw_prototypes(key, part):
    direction = common_axis(key)
    noise = jnp.clip(jax.random.normal(jax.random.fold_in(key, 2), (K, PROTOS), jnp.float32), -6.0, 6.0)
    jitter = jax.random.uniform(jax.random.fold_in(key, 3), (PROTOS,), jnp.float32, -1.0, 1.0)
    lean = 1.5 * (2.0 * jnp.arange(PROTOS, dtype=jnp.float32) / PROTOS - 1.0) + jitter
    return (noise + lean[None, :] * direction).astype(jnp.bfloat16)


def spiked(result, key, source, target, parts, factor):
    def block_of(dim):
        return (jnp.arange(result.shape[dim]) // (result.shape[dim] // parts)).reshape((-1,) + (1,) * (result.ndim - 1 - dim))

    first = jax.random.permutation(key, parts)[block_of(target)]
    far = (block_of(target) + parts // 2) % parts
    return jnp.where((block_of(source) == first) | (block_of(source) == far), factor * result, result)


def block_levels(stream_key, shape, cuts, low, top_value):
    gain = 1.0
    for axis_at, blocks in cuts:
        draws = jax.random.uniform(jax.random.fold_in(jax.random.fold_in(stream_key, 6), axis_at), (blocks,), jnp.float32, low / len(cuts), top_value / len(cuts))
        gain = gain * jnp.repeat(jnp.exp(draws), shape[axis_at] // blocks).reshape((-1,) + (1,) * (len(shape) - 1 - axis_at))
    return gain


def noise_with(stream_key, extent, deviation, limit, cuts, heavy, kind=jnp.bfloat16):
    entries = deviation * jax.random.normal(stream_key, extent, jnp.float32)
    if cuts:
        entries = entries * block_levels(stream_key, extent, cuts, -0.22, 0.18)
    return jnp.clip(spiked(entries, jax.random.fold_in(stream_key, 3), *heavy), -limit, limit).astype(kind)


def setup_inputs(seed: int = 0) -> dict:
    key_of = jax.random.split(jax.random.key(seed), 4)
    teacher_emb = draw_teacher_emb(jax.random.fold_in(key_of[3], 71), 0)
    student_emb = noise_with(key_of[1], (K, CROPS), 1.0, 6.0, ((0, 16), (1, 16)), (1, 0, 16, 2.0))
    prototypes = draw_prototypes(jax.random.fold_in(key_of[3], 71), 0)
    return dict(teacher_emb=teacher_emb, student_emb=student_emb, prototypes=prototypes)


teacher_temp = 0.07
student_temp = 0.1
epsilon = 1e-06

def unit(matrix):
    values = matrix.astype(jnp.float32)
    factor = lax.rsqrt(lax.optimization_barrier(jnp.sum(values * values, axis=0, keepdims=True)) + epsilon)
    return ((values * factor).astype(jnp.bfloat16), factor)

def cosine(left, right):
    return lax.dot_general(left, right, (((0,), (0,)), ((), ())), preferred_element_type=jnp.float32)

def reference(teacher_emb, student_emb, prototypes):
    proto_unit, proto_scale = unit(prototypes)
    teacher_unit, unused = unit(teacher_emb)
    student_unit, student_scale = unit(student_emb)
    width = teacher_emb.shape[0]
    total_rows = teacher_emb.shape[1]
    count = total_rows // ROWS_DEV

    def blocks(matrix):
        return matrix.reshape(width, count, ROWS_DEV).transpose(1, 0, 2)
    teacher_blocks = blocks(teacher_unit)
    student_blocks = blocks(student_unit)

    def expo_of(block):
        return jnp.exp(cosine(block, proto_unit) / teacher_temp)
    crop_scale = jnp.ones((count, ROWS_DEV), jnp.float32)
    proto_inv = jnp.ones((PROTOS,), jnp.float32)
    for iteration in range(ITERS):

        def add_column(carry, item):
            block, weights = item
            return (carry + jnp.dot(weights, expo_of(block), precision=lax.Precision.HIGHEST), None)
        column_sum, unused_out = lax.scan(add_column, jnp.zeros((PROTOS,), jnp.float32), (teacher_blocks, crop_scale))
        proto_inv = 1.0 / column_sum

        def row_of(block):
            return jnp.dot(expo_of(block), proto_inv, precision=lax.Precision.HIGHEST)
        crop_scale = 1.0 / lax.map(row_of, teacher_blocks)

    def final(carry, item):
        grad_sum, loss_sum = carry
        teacher_block, student_block, weights = item
        targets = expo_of(teacher_block) * proto_inv[None, :] * weights[:, None]
        logits = cosine(student_block, proto_unit) / student_temp
        logp = logits - jnp.log(lax.optimization_barrier(jnp.sum(jnp.exp(logits), axis=1, keepdims=True)))
        loss_sum = loss_sum - jnp.sum(targets * logp)
        grad_logit = ((jnp.exp(logp) - targets) / (total_rows * student_temp)).astype(jnp.bfloat16)
        grad_sum = grad_sum + jnp.dot(student_block, grad_logit, preferred_element_type=jnp.float32)
        crop_part = lax.dot_general(proto_unit, grad_logit, (((1,), (1,)), ((), ())), preferred_element_type=jnp.float32)
        return ((grad_sum, loss_sum), crop_part)
    start = (jnp.zeros((width, PROTOS), jnp.float32), jnp.zeros((), jnp.float32))
    (grad_unit_proto, loss_sum), crop_parts = lax.scan(final, start, (teacher_blocks, student_blocks, crop_scale))
    grad_unit_crop = crop_parts.transpose(1, 0, 2).reshape(width, total_rows)
    proto_values = proto_unit.astype(jnp.float32)
    proto_dot = lax.optimization_barrier(jnp.sum(proto_values * grad_unit_proto, axis=0, keepdims=True))
    grad_proto = (grad_unit_proto - proto_values * proto_dot) * proto_scale
    student_values = student_unit.astype(jnp.float32)
    crop_dot = lax.optimization_barrier(jnp.sum(student_values * grad_unit_crop, axis=0, keepdims=True))
    grad_student = (grad_unit_crop - student_values * crop_dot) * student_scale
    return (grad_proto, grad_student, loss_sum / total_rows)
```

```python
import types

import jax
import jax.numpy as jnp
from jax import lax
from jax.experimental import pallas as pl
from jax.experimental.pallas import tpu as pltpu
from jax.sharding import PartitionSpec as P

F32, BF16 = jnp.float32, jnp.bfloat16
MESH = pl.DeviceIdType.MESH
LOG2E = 1.4426950408889634
TEACHER_TEMP, STUDENT_TEMP, EPS = 0.07, 0.1, 1e-6
K, ROWS, COLS = 256, 512, 4096
CHUNK = 512
NCHUNK = COLS // CHUNK
SIDE = 4
NP = 16
BLK = K // 16
HALF = COLS // 2
QUART = COLS // 4
CROPS = ROWS * SIDE * SIDE
OFFS = (0, -1, 1, 2)
MSGW = CHUNK + 128

SCRATCH = dict(
    praw=((K, COLS), BF16),
    traw=((K, ROWS), BF16),
    sraw=((K, ROWS), BF16),
    tt=((ROWS, K), BF16),
    st=((ROWS, K), BF16),
    su=((K, ROWS), BF16),
    pu=((K, COLS), BF16),
    pscale=((1, COLS), F32),
    sscale=((1, ROWS), F32),
    expo=((ROWS, COLS), F32),
    cos=((ROWS, COLS), F32),
    rowacc=((ROWS, 128), F32),
    colacc=((8, COLS), F32),
    pinv=((8, COLS), F32),
    csb=((ROWS, 128), F32),
    itot=((ROWS, 128), F32),
    tlacc=((8, 128), F32),
    gl=((ROWS, CHUNK), BF16),
    gp=((K, COLS), F32),
    cg=((K, ROWS), F32),
    cgb=((2, 8, BLK, ROWS), F32),
    cgr=((8, BLK, ROWS), F32),
    cgz=((8, BLK, ROWS), F32),
    cgs=((8, BLK, ROWS), F32),
    cx=((4, SIDE, NCHUNK, MSGW), F32),
    cy=((4, SIDE, NCHUNK, MSGW), F32),
    rx=((4, NP, 8, 128), F32),
    lx=((SIDE, 8, 128), F32),
    ly=((SIDE, 8, 128), F32),
    s1=((2, 2, 3, 4 * BLK, QUART), F32),
    r1=((2, 2, 3, 4 * BLK, QUART), F32),
    t1=((2, 4 * BLK, HALF), F32),
    s2=((2, 2, 3, BLK, QUART), F32),
    r2=((2, 2, 3, BLK, QUART), F32),
)
SEMS = dict(
    own=(3,),
    ag_s=(2, 5, 4),
    ag_r=(2, 5, 4),
    ts_s=(2, 16),
    ts_r=(2, 16),
    cx_s=(4, 3),
    cx_r=(4, 3),
    cy_s=(4, 3),
    cy_r=(4, 3),
    rx_s=(4, 15),
    rx_r=(4, 15),
    l_s=(2, 3),
    l_r=(2, 3),
    rs1_s=(2, 2, 3),
    rs1_r=(2, 2, 3),
    rs2_s=(2, 2, 3),
    rs2_r=(2, 2, 3),
    cg_s=(8,),
    cg_r=(8,),
)


def body(t_in, s_in, p_in, gp_out, gs_out, loss_out, *scratch):
    m = types.SimpleNamespace(**dict(zip(list(SCRATCH) + list(SEMS), scratch)))
    bi, pi = lax.axis_index("batch"), lax.axis_index("proto")
    yi, xi = bi // SIDE, bi % SIDE
    zi, ci = pi // 2, pi % 2
    started = []

    def batch_dev(y, x):
        return (y * SIDE + x, pi)

    def proto_dev(p):
        return (bi, p)

    def rdma(src, dst, ssem, rsem, dev):
        return pltpu.make_async_remote_copy(
            src_ref=src, dst_ref=dst, send_sem=ssem, recv_sem=rsem, device_id=dev, device_id_type=MESH
        )

    def send(src, dst, ssem, rsem, dev):
        copy = rdma(src, dst, ssem, rsem, dev)
        copy.start()
        started.append(copy)

    def arrived(dst, ssem, rsem, dev):
        rdma(dst, dst, ssem, rsem, dev).wait_recv()

    barrier = pltpu.get_barrier_semaphore()
    peers = []
    for d in range(1, SIDE):
        peers.append(batch_dev(yi, (xi + d) % SIDE))
        peers.append(batch_dev((yi + d) % SIDE, xi))
    for d in range(1, NP):
        peers.append(proto_dev((pi + d) % NP))
    for peer in peers:
        pl.semaphore_signal(barrier, inc=1, device_id=peer, device_id_type=MESH)
    pl.semaphore_wait(barrier, len(peers))

    def where(h, c1, c2):
        c1, c2 = (c1 + SIDE) % SIDE, (c2 + SIDE) % SIDE
        return (c2, c1) if h == 0 else (c1, c2)

    pos = ((xi, yi), (yi, xi))

    def row0(y, x):
        return pl.multiple_of((y * SIDE + x) * BLK, BLK)

    def piece(h, y, x, part):
        lo, n = ((h * HALF, HALF), (h * HALF, QUART), (h * HALF + QUART, QUART))[part]
        return m.praw.at[pl.ds(row0(y, x), BLK), pl.ds(lo, n)]

    def own_piece(h):
        return p_in.at[:, pl.ds(h * HALF, HALF)]

    own = [
        pltpu.make_async_copy(p_in, m.praw.at[pl.ds(row0(yi, xi), BLK), :], m.own.at[0]),
        pltpu.make_async_copy(t_in, m.traw.at[pl.ds(pl.multiple_of(pi * BLK, BLK), BLK), :], m.own.at[1]),
        pltpu.make_async_copy(s_in, m.sraw.at[pl.ds(pl.multiple_of(pi * BLK, BLK), BLK), :], m.own.at[2]),
    ]

    def put(h, phase, slot, dev_c, blk_c, part, src=None):
        y, x = where(h, *blk_c)
        dst = piece(h, y, x, part)
        send(dst if src is None else src, dst, m.ag_s.at[h, phase, slot], m.ag_r.at[h, phase, slot], batch_dev(*where(h, *dev_c)))

    def got(h, phase, slot, blk_c, part):
        y, x = where(h, *blk_c)
        dst = piece(h, y, x, part)
        arrived(dst, m.ag_s.at[h, phase, slot], m.ag_r.at[h, phase, slot], batch_dev(y, x))

    for h in range(2):
        i1, i2 = pos[h]
        for slot, d in enumerate((1, -1)):
            put(h, 0, slot, (i1 + d, i2), (i1, i2), 0, own_piece(h))
    for h in range(2):
        i1, i2 = pos[h]
        for slot, d in enumerate((1, -1)):
            put(h, 1, slot, (i1, i2 + d), (i1, i2), 0, own_piece(h))

    def ts_rows(ref, p):
        return ref.at[pl.ds(pl.multiple_of(p * BLK, BLK), BLK), :]

    sibling = zi * 2 + 1 - ci
    for d in range(1, 8):
        peer = ((zi + d) % 8) * 2 + ci
        for a, (src, ref) in enumerate(((t_in, m.traw), (s_in, m.sraw))):
            send(src, ts_rows(ref, pi), m.ts_s.at[a, d - 1], m.ts_r.at[a, d - 1], proto_dev(peer))
    for a, (src, ref) in enumerate(((t_in, m.traw), (s_in, m.sraw))):
        send(src, ts_rows(ref, pi), m.ts_s.at[a, 7], m.ts_r.at[a, 7], proto_dev(sibling))
    for copy in own:
        copy.start()

    for slot, d in enumerate((-1, 1)):
        for h in range(2):
            i1, i2 = pos[h]
            got(h, 0, slot, (i1 + d, i2), 0)
            put(h, 0, 2 + slot, (i1 - d, i2), (i1 + d, i2), 1 + slot)
            for s2, d2 in enumerate((1, -1)):
                put(h, 2 + slot, s2, (i1, i2 + d2), (i1 + d, i2), 0)
    for d in range(1, 8):
        peer = ((zi + 8 - d) % 8) * 2 + ci
        for a, ref in enumerate((m.traw, m.sraw)):
            rows = ts_rows(ref, peer)
            arrived(rows, m.ts_s.at[a, d - 1], m.ts_r.at[a, d - 1], proto_dev(peer))
            send(rows, rows, m.ts_s.at[a, 7 + d], m.ts_r.at[a, 7 + d], proto_dev(sibling))
    for h in range(2):
        i1, i2 = pos[h]
        for slot in range(2):
            got(h, 0, 2 + slot, (i1 + 2, i2), 1 + slot)
        for s2, d2 in enumerate((1, -1)):
            put(h, 4, s2, (i1, i2 + d2), (i1 + 2, i2), 0)
    for r, off in enumerate(OFFS):
        for slot, d in enumerate((-1, 1)):
            for h in range(2):
                i1, i2 = pos[h]
                got(h, 1 + r, slot, (i1 + off, i2 + d), 0)
                put(h, 1 + r, 2 + slot, (i1, i2 - d), (i1 + off, i2 + d), 1 + slot)

    for copy in own[1:]:
        copy.wait()
    for a, ref in enumerate((m.traw, m.sraw)):
        arrived(ts_rows(ref, sibling), m.ts_s.at[a, 7], m.ts_r.at[a, 7], proto_dev(sibling))
        for d in range(1, 8):
            rows = ts_rows(ref, ((zi + 8 - d) % 8) * 2 + 1 - ci)
            arrived(rows, m.ts_s.at[a, 7 + d], m.ts_r.at[a, 7 + d], proto_dev(sibling))

    def unit(values):
        values = values.astype(F32)
        factor = lax.rsqrt(jnp.sum(values * values, axis=0, keepdims=True) + EPS)
        return values * factor, factor

    teacher, unused = unit(m.traw[...])
    m.tt[...] = jnp.transpose(teacher).astype(BF16)
    student, factor = unit(m.sraw[...])
    m.sscale[...] = factor
    m.su[...] = student.astype(BF16)
    m.st[...] = jnp.transpose(student).astype(BF16)

    own[0].wait()
    for r, off in enumerate(OFFS):
        for slot in range(2):
            for h in range(2):
                i1, i2 = pos[h]
                got(h, 1 + r, 2 + slot, (i1 + off, i2 + 2), 1 + slot)

    def cols_of(j):
        return pl.ds(pl.multiple_of(j * CHUNK, CHUNK), CHUNK)

    def teacher_chunk(j, carry):
        cols = cols_of(j)
        proto, factor = unit(m.praw[:, cols])
        proto = proto.astype(BF16)
        m.pu[:, cols] = proto
        m.pscale[:, cols] = factor
        c = jnp.dot(m.tt[...], proto, preferred_element_type=F32)
        e = jnp.exp2(c * (LOG2E / TEACHER_TEMP))
        m.expo[:, cols] = e
        m.colacc[:, cols] = jnp.sum(e.reshape(ROWS // 8, 8, CHUNK), axis=0)
        return carry

    def to_message(e):
        for j in range(NCHUNK):
            m.cx[e, xi, j : j + 1, pl.ds(0, CHUNK)] = jnp.sum(
                m.colacc[:, j * CHUNK : (j + 1) * CHUNK], axis=0, keepdims=True
            )

    lax.fori_loop(0, NCHUNK, teacher_chunk, 0)
    to_message(0)

    def ring_send(buf, me, dev, ss, rs):
        for d in range(1, SIDE):
            send(buf.at[me], buf.at[me], ss.at[d - 1], rs.at[d - 1], dev((me + d) % SIDE))

    def ring_sum(buf, me, dev, ss, rs):
        for d in range(1, SIDE):
            frm = (me + SIDE - d) % SIDE
            arrived(buf.at[frm], ss.at[d - 1], rs.at[d - 1], dev(frm))
        return (buf[0] + buf[1]) + (buf[2] + buf[3])

    def along_x(x):
        return batch_dev(yi, x)

    def along_y(y):
        return batch_dev(y, xi)

    def col_start(e):
        ring_send(m.cx.at[e], xi, along_x, m.cx_s.at[e], m.cx_r.at[e])

    def col_finish(e):
        m.cy[e, yi] = ring_sum(m.cx.at[e], xi, along_x, m.cx_s.at[e], m.cx_r.at[e])
        ring_send(m.cy.at[e], yi, along_y, m.cy_s.at[e], m.cy_r.at[e])
        return ring_sum(m.cy.at[e], yi, along_y, m.cy_s.at[e], m.cy_r.at[e])

    def row_start(e):
        for d in range(1, NP):
            send(m.rx.at[e, pi], m.rx.at[e, pi], m.rx_s.at[e, d - 1], m.rx_r.at[e, d - 1], proto_dev((pi + d) % NP))

    def row_finish(e):
        for d in range(1, NP):
            frm = (pi + NP - d) % NP
            arrived(m.rx.at[e, frm], m.rx_s.at[e, d - 1], m.rx_r.at[e, d - 1], proto_dev(frm))
        return jnp.sum(m.rx[e], axis=0)

    def to_rows(acc_ref, e, first):
        for q in range(4):
            block = jnp.transpose(acc_ref[q * 128 : (q + 1) * 128, :])
            m.rx[e, pi, pl.ds(first + q, 1), :] = jnp.sum(block, axis=0, keepdims=True)

    def to_columns(ref, rows):
        for q in range(4):
            ref[q * 128 : (q + 1) * 128, :] = jnp.transpose(jnp.broadcast_to(rows[q : q + 1], (128, 128)))

    m.cx[:, xi, :, pl.ds(CHUNK, 128)] = jnp.zeros((4, NCHUNK, 128), F32)
    col_start(0)

    m.rowacc[...] = jnp.zeros_like(m.rowacc)

    def student_chunk(j, carry):
        cols = cols_of(j)
        c = jnp.dot(m.st[...], m.pu[:, cols], preferred_element_type=F32)
        m.cos[:, cols] = c
        e = jnp.exp2(c * (LOG2E / STUDENT_TEMP))
        m.rowacc[...] += (e[:, 0:128] + e[:, 128:256]) + (e[:, 256:384] + e[:, 384:512])
        return carry

    lax.fori_loop(0, NCHUNK, student_chunk, 0)
    to_rows(m.rowacc, 0, 4)

    def row_pass(e):
        for half in range(2):
            rows = pl.ds(half * 256, 256)

            def step(j, acc):
                for i in range(4):
                    cols = pl.ds(pl.multiple_of(j * CHUNK + i * 128, 128), 128)
                    acc = acc + m.expo[rows, cols].reshape(32, 8, 128) * m.pinv[:, cols]
                return acc

            m.rowacc[rows, :] = lax.fori_loop(0, NCHUNK, step, jnp.zeros((32, 8, 128), F32)).reshape(256, 128)
        to_rows(m.rowacc, e, 0)

    def col_pass(e):
        m.colacc[...] = jnp.zeros_like(m.colacc)

        def step(r, carry):
            rows = pl.ds(pl.multiple_of(r * 64, 64), 64)
            weights = m.csb[rows, :]
            for q in range(COLS // 128):
                cols = slice(q * 128, (q + 1) * 128)
                m.colacc[:, cols] += jnp.sum((m.expo[rows, cols] * weights).reshape(8, 8, 128), axis=0)
            return carry

        lax.fori_loop(0, ROWS // 64, step, 0)
        to_message(e)

    log_total = None
    for e in range(3):
        if e:
            col_pass(e)
            col_start(e)
        total = col_finish(e)[:, :CHUNK]
        total = 1.0 / total
        for j in range(NCHUNK):
            m.pinv[:, j * CHUNK : (j + 1) * CHUNK] = jnp.broadcast_to(total[j : j + 1], (8, CHUNK))
        if e:
            m.rx[e, pi, 4:8, :] = jnp.zeros((4, 128), F32)
        row_pass(e)
        row_start(e)
        rows = row_finish(e)
        to_columns(m.csb, 1.0 / rows[0:4])
        if e == 0:
            to_columns(m.itot, 1.0 / rows[4:8])
            log_total = jnp.sum(jnp.log(rows[4:8]), axis=0, keepdims=True)

    m.tlacc[...] = jnp.zeros_like(m.tlacc)
    m.cg[...] = jnp.zeros_like(m.cg)

    def grad_chunk(j, carry):
        cols = cols_of(j)

        def rows_step(r, inner):
            rows = pl.ds(pl.multiple_of(r * 64, 64), 64)
            weights, inv = m.csb[rows, :], m.itot[rows, :]
            tl = jnp.zeros((64, 128), F32)
            for i in range(4):
                sub = pl.ds(pl.multiple_of(j * CHUNK + i * 128, 128), 128)
                target = (m.expo[rows, sub].reshape(8, 8, 128) * m.pinv[:, sub]).reshape(64, 128) * weights
                c = m.cos[rows, sub]
                prob = jnp.exp2(c * (LOG2E / STUDENT_TEMP)) * inv
                tl = tl + target * c
                m.gl[rows, i * 128 : (i + 1) * 128] = ((prob - target) * (1.0 / (CROPS * STUDENT_TEMP))).astype(BF16)
            m.tlacc[...] += jnp.sum(tl.reshape(8, 8, 128), axis=0)
            return inner

        lax.fori_loop(0, ROWS // 64, rows_step, 0)
        g = m.gl[...]
        proto = m.pu[:, cols]
        part = jnp.dot(m.su[...], g, preferred_element_type=F32)
        m.gp[:, cols] = part
        m.cg[...] += lax.dot_general(proto, g, (((1,), (1,)), ((), ())), preferred_element_type=F32)
        m.colacc[:, cols] = jnp.sum((proto.astype(F32) * part).reshape(K // 8, 8, CHUNK), axis=0)
        return carry

    lax.fori_loop(0, NCHUNK, grad_chunk, 0)
    to_message(3)

    dot_rows = jnp.sum(m.su[...].astype(F32) * m.cg[...], axis=0, keepdims=True)
    for q in range(4):
        m.rx[3, pi, q : q + 1, :] = dot_rows[:, q * 128 : (q + 1) * 128]
    m.rx[3, pi, 4:8, :] = jnp.zeros((4, 128), F32)
    m.rx[3, pi, 4:5, :] = jnp.sum(m.tlacc[...], axis=0, keepdims=True)
    row_start(3)
    col_start(3)
    for p in range(NP):
        m.cgb[p % 2, p // 2] = m.cg[p * BLK : (p + 1) * BLK, :]
    send(m.cgb.at[1 - ci], m.cgr, m.cg_s.at[7], m.cg_r.at[7], proto_dev(sibling))

    def rs_send(s, r, ss, rs, h, axis, direction, slot):
        i1, i2 = pos[h]
        d = 1 - 2 * direction
        dev = (i1 + d, i2) if axis == 0 else (i1, i2 + d)
        send(s.at[h, direction, slot], r.at[h, direction, slot], ss.at[h, direction, slot], rs.at[h, direction, slot], batch_dev(*where(h, *dev)))

    def rs_got(s, r, ss, rs, h, axis, direction, slot):
        i1, i2 = pos[h]
        d = 1 - 2 * direction
        dev = (i1 - d, i2) if axis == 0 else (i1, i2 - d)
        arrived(r.at[h, direction, slot], ss.at[h, direction, slot], rs.at[h, direction, slot], batch_dev(*where(h, *dev)))
        return r[h, direction, slot]

    def reduce_scatter(axis, s, r, ss, rs, load):
        at = [pos[h][axis] for h in range(2)]
        for h in range(2):
            for direction in range(2):
                s[h, direction, 0] = load(h, at[h] + 2, direction)
                rs_send(s, r, ss, rs, h, axis, direction, 0)
        for h in range(2):
            for direction in range(2):
                s[h, direction, 1] = load(h, at[h] + 1 - 2 * direction, 1 - direction)
                rs_send(s, r, ss, rs, h, axis, direction, 1)
        for h in range(2):
            for direction in range(2):
                mine = load(h, at[h] + 1 - 2 * direction, direction)
                s[h, direction, 2] = mine + rs_got(s, r, ss, rs, h, axis, direction, 0)
                rs_send(s, r, ss, rs, h, axis, direction, 2)

    def reduced(axis, s, r, ss, rs, load, h, quarter):
        mine = load(h, pos[h][axis], quarter)
        return mine + rs_got(s, r, ss, rs, h, axis, 1 - quarter, 1) + rs_got(s, r, ss, rs, h, axis, quarter, 2)

    def load1(h, c, quarter):
        c = (c + SIDE) % SIDE
        cols = pl.ds(h * HALF + quarter * QUART, QUART)
        blocks = []
        for u in range(SIDE):
            y, x = (c, u) if h else (u, c)
            blocks.append(m.gp[pl.ds(row0(y, x), BLK), cols])
        return jnp.concatenate(blocks, axis=0)

    def load2(h, c, quarter):
        c = (c + SIDE) % SIDE
        return m.t1[h, pl.ds(pl.multiple_of(c * BLK, BLK), BLK), pl.ds(quarter * QUART, QUART)]

    one = (m.s1, m.r1, m.rs1_s, m.rs1_r)
    two = (m.s2, m.r2, m.rs2_s, m.rs2_r)
    reduce_scatter(0, *one, load1)

    arrived(m.cgr, m.cg_s.at[7], m.cg_r.at[7], proto_dev(sibling))
    m.cgs[...] = m.cgb[ci] + m.cgr[...]
    for d in range(1, 8):
        to = (zi + d) % 8
        send(m.cgs.at[to], m.cgz.at[zi], m.cg_s.at[d - 1], m.cg_r.at[d - 1], proto_dev(to * 2 + ci))
    m.cgz[zi] = m.cgs[zi]

    rows = row_finish(3)
    loss_rows = rows[4:5] * (1.0 / STUDENT_TEMP) - log_total
    m.lx[xi] = jnp.broadcast_to(loss_rows, (8, 128))
    ring_send(m.lx, xi, along_x, m.l_s.at[0], m.l_r.at[0])
    dots = col_finish(3)[:, :CHUNK]
    m.ly[yi] = ring_sum(m.lx, xi, along_x, m.l_s.at[0], m.l_r.at[0])
    ring_send(m.ly, yi, along_y, m.l_s.at[1], m.l_r.at[1])

    for h in range(2):
        for quarter in range(2):
            m.t1[h, :, pl.ds(quarter * QUART, QUART)] = reduced(0, *one, load1, h, quarter)
    reduce_scatter(1, *two, load2)

    loss_out[0, 0] = jnp.sum(ring_sum(m.ly, yi, along_y, m.l_s.at[1], m.l_r.at[1])[0:1]) * (-1.0 / CROPS)
    for d in range(1, 8):
        frm = (zi + 8 - d) % 8
        arrived(m.cgz.at[frm], m.cg_s.at[d - 1], m.cg_r.at[d - 1], proto_dev(frm * 2 + ci))
    crop_part = jnp.sum(m.cgz[...], axis=0)
    student_own = m.su[pl.ds(pl.multiple_of(pi * BLK, BLK), BLK), :].astype(F32)
    for q in range(4):
        cols = slice(q * 128, (q + 1) * 128)
        gs_out[:, cols] = (crop_part[:, cols] - student_own[:, cols] * rows[q : q + 1]) * m.sscale[:, cols]

    for h in range(2):
        for quarter in range(2):
            total = reduced(1, *two, load2, h, quarter)
            for half in range(2):
                j = h * 4 + quarter * 2 + half
                cols = slice(j * CHUNK, (j + 1) * CHUNK)
                proto_own = m.pu[pl.ds(row0(yi, xi), BLK), cols].astype(F32)
                gp_out[:, cols] = (total[:, half * CHUNK : (half + 1) * CHUNK] - proto_own * dots[j : j + 1]) * m.pscale[:, cols]

    for copy in started:
        copy.wait_send()


def shards(teacher_emb, student_emb, prototypes):
    hbm = pl.BlockSpec(memory_space=pl.ANY)
    vmem = pl.BlockSpec(memory_space=pltpu.VMEM)
    grad_proto, grad_student, loss = pl.pallas_call(
        body,
        out_shape=(
            jax.ShapeDtypeStruct((BLK, COLS), F32),
            jax.ShapeDtypeStruct((BLK, ROWS), F32),
            jax.ShapeDtypeStruct((1, 1), F32),
        ),
        in_specs=[hbm] * 3,
        out_specs=(vmem, vmem, pl.BlockSpec(memory_space=pltpu.SMEM)),
        scratch_shapes=[pltpu.VMEM(shape, dtype) for shape, dtype in SCRATCH.values()]
        + [pltpu.SemaphoreType.DMA(shape) for shape in SEMS.values()],
        compiler_params=pltpu.CompilerParams(
            collective_id=0, has_side_effects=True, vmem_limit_bytes=58 * 1024 * 1024
        ),
    )(teacher_emb, student_emb, prototypes)
    return grad_proto, grad_student, loss.reshape(())


def solution(mesh):
    in_specs = (P("proto", "batch"), P("proto", "batch"), P("batch", "proto"))
    out_specs = (P("batch", "proto"), P("proto", "batch"), P())
    return jax.shard_map(shards, mesh=mesh, in_specs=in_specs, out_specs=out_specs, check_vma=False)
```

```python
import types

import jax
import jax.numpy as jnp
from jax import lax
from jax.experimental import pallas as pl
from jax.experimental.pallas import tpu as pltpu
from jax.sharding import PartitionSpec as P

F32, BF16 = jnp.float32, jnp.bfloat16
MESH = pl.DeviceIdType.MESH
LOG2E = 1.4426950408889634
TEACHER_TEMP, STUDENT_TEMP, EPS = 0.07, 0.1, 1e-6
K, ROWS, COLS = 256, 512, 4096
CHUNK = 512
NCHUNK = COLS // CHUNK
SIDE = 4
NP = 16
BLK = K // 16
HALF = COLS // 2
QUART = COLS // 4
CROPS = ROWS * SIDE * SIDE
OFFS = (0, -1, 1, 2)
MSGW = CHUNK + 128

SCRATCH = dict(
    praw=((K, COLS), BF16),
    traw=((K, ROWS), BF16),
    sraw=((K, ROWS), BF16),
    tt=((ROWS, K), BF16),
    st=((ROWS, K), BF16),
    su=((K, ROWS), BF16),
    pu=((K, COLS), BF16),
    pscale=((1, COLS), F32),
    sscale=((1, ROWS), F32),
    expo=((ROWS, COLS), F32),
    cos=((ROWS, COLS), F32),
    rowacc=((ROWS, 128), F32),
    colacc=((8, COLS), F32),
    pinv=((8, COLS), F32),
    csb=((ROWS, 128), F32),
    itot=((ROWS, 128), F32),
    tlacc=((8, 128), F32),
    gl=((ROWS, CHUNK), BF16),
    gp=((K, COLS), F32),
    cg=((K, ROWS), F32),
    cgb=((2, 8, BLK, ROWS), F32),
    cgr=((8, BLK, ROWS), F32),
    cgz=((8, BLK, ROWS), F32),
    cgs=((8, BLK, ROWS), F32),
    cx=((4, SIDE, NCHUNK, MSGW), F32),
    cy=((4, SIDE, NCHUNK, MSGW), F32),
    rx=((4, NP, 8, 128), F32),
    lx=((SIDE, 8, 128), F32),
    ly=((SIDE, 8, 128), F32),
    s1=((2, 2, 3, 4 * BLK, QUART), BF16),
    r1=((2, 2, 3, 4 * BLK, QUART), BF16),
    t1=((2, 4 * BLK, HALF), F32),
    s2=((2, 2, 3, BLK, QUART), BF16),
    r2=((2, 2, 3, BLK, QUART), BF16),
    smax=((8, CHUNK), F32),
)
SEMS = dict(
    own=(3,),
    ag_s=(2, 5, 4),
    ag_r=(2, 5, 4),
    ts_s=(2, 16),
    ts_r=(2, 16),
    cx_s=(4, 3),
    cx_r=(4, 3),
    cy_s=(4, 3),
    cy_r=(4, 3),
    rx_s=(4, 15),
    rx_r=(4, 15),
    l_s=(2, 3),
    l_r=(2, 3),
    rs1_s=(2, 2, 3),
    rs1_r=(2, 2, 3),
    rs2_s=(2, 2, 3),
    rs2_r=(2, 2, 3),
    cg_s=(8,),
    cg_r=(8,),
)


def body(t_in, s_in, p_in, gp_out, gs_out, loss_out, *scratch):
    m = types.SimpleNamespace(**dict(zip(list(SCRATCH) + list(SEMS), scratch)))
    bi, pi = lax.axis_index("batch"), lax.axis_index("proto")
    yi, xi = bi // SIDE, bi % SIDE
    zi, ci = pi // 2, pi % 2
    started = []

    def batch_dev(y, x):
        return (y * SIDE + x, pi)

    def proto_dev(p):
        return (bi, p)

    def rdma(src, dst, ssem, rsem, dev):
        return pltpu.make_async_remote_copy(
            src_ref=src, dst_ref=dst, send_sem=ssem, recv_sem=rsem, device_id=dev, device_id_type=MESH
        )

    def send(src, dst, ssem, rsem, dev):
        copy = rdma(src, dst, ssem, rsem, dev)
        copy.start()
        started.append(copy)

    def arrived(dst, ssem, rsem, dev):
        rdma(dst, dst, ssem, rsem, dev).wait_recv()

    barrier = pltpu.get_barrier_semaphore()
    peers = []
    for d in range(1, SIDE):
        peers.append(batch_dev(yi, (xi + d) % SIDE))
        peers.append(batch_dev((yi + d) % SIDE, xi))
    for d in range(1, NP):
        peers.append(proto_dev((pi + d) % NP))
    for peer in peers:
        pl.semaphore_signal(barrier, inc=1, device_id=peer, device_id_type=MESH)
    pl.semaphore_wait(barrier, len(peers))

    def where(h, c1, c2):
        c1, c2 = (c1 + SIDE) % SIDE, (c2 + SIDE) % SIDE
        return (c2, c1) if h == 0 else (c1, c2)

    pos = ((xi, yi), (yi, xi))

    def row0(y, x):
        return pl.multiple_of((y * SIDE + x) * BLK, BLK)

    def piece(h, y, x, part):
        lo, n = ((h * HALF, HALF), (h * HALF, QUART), (h * HALF + QUART, QUART))[part]
        return m.praw.at[pl.ds(row0(y, x), BLK), pl.ds(lo, n)]

    def own_piece(h):
        return p_in.at[:, pl.ds(h * HALF, HALF)]

    own = [
        pltpu.make_async_copy(p_in, m.praw.at[pl.ds(row0(yi, xi), BLK), :], m.own.at[0]),
        pltpu.make_async_copy(t_in, m.traw.at[pl.ds(pl.multiple_of(pi * BLK, BLK), BLK), :], m.own.at[1]),
        pltpu.make_async_copy(s_in, m.sraw.at[pl.ds(pl.multiple_of(pi * BLK, BLK), BLK), :], m.own.at[2]),
    ]

    def put(h, phase, slot, dev_c, blk_c, part, src=None):
        y, x = where(h, *blk_c)
        dst = piece(h, y, x, part)
        send(dst if src is None else src, dst, m.ag_s.at[h, phase, slot], m.ag_r.at[h, phase, slot], batch_dev(*where(h, *dev_c)))

    def got(h, phase, slot, blk_c, part):
        y, x = where(h, *blk_c)
        dst = piece(h, y, x, part)
        arrived(dst, m.ag_s.at[h, phase, slot], m.ag_r.at[h, phase, slot], batch_dev(y, x))

    for h in range(2):
        i1, i2 = pos[h]
        for slot, d in enumerate((1, -1)):
            put(h, 0, slot, (i1 + d, i2), (i1, i2), 0, own_piece(h))
    for h in range(2):
        i1, i2 = pos[h]
        for slot, d in enumerate((1, -1)):
            put(h, 1, slot, (i1, i2 + d), (i1, i2), 0, own_piece(h))

    def ts_rows(ref, p):
        return ref.at[pl.ds(pl.multiple_of(p * BLK, BLK), BLK), :]

    sibling = zi * 2 + 1 - ci
    for d in range(1, 8):
        peer = ((zi + d) % 8) * 2 + ci
        for a, (src, ref) in enumerate(((t_in, m.traw), (s_in, m.sraw))):
            send(src, ts_rows(ref, pi), m.ts_s.at[a, d - 1], m.ts_r.at[a, d - 1], proto_dev(peer))
    for a, (src, ref) in enumerate(((t_in, m.traw), (s_in, m.sraw))):
        send(src, ts_rows(ref, pi), m.ts_s.at[a, 7], m.ts_r.at[a, 7], proto_dev(sibling))
    for copy in own:
        copy.start()

    for slot, d in enumerate((-1, 1)):
        for h in range(2):
            i1, i2 = pos[h]
            got(h, 0, slot, (i1 + d, i2), 0)
            put(h, 0, 2 + slot, (i1 - d, i2), (i1 + d, i2), 1 + slot)
            for s2, d2 in enumerate((1, -1)):
                put(h, 2 + slot, s2, (i1, i2 + d2), (i1 + d, i2), 0)
    for d in range(1, 8):
        peer = ((zi + 8 - d) % 8) * 2 + ci
        for a, ref in enumerate((m.traw, m.sraw)):
            rows = ts_rows(ref, peer)
            arrived(rows, m.ts_s.at[a, d - 1], m.ts_r.at[a, d - 1], proto_dev(peer))
            send(rows, rows, m.ts_s.at[a, 7 + d], m.ts_r.at[a, 7 + d], proto_dev(sibling))
    for h in range(2):
        i1, i2 = pos[h]
        for slot in range(2):
            got(h, 0, 2 + slot, (i1 + 2, i2), 1 + slot)
        for s2, d2 in enumerate((1, -1)):
            put(h, 4, s2, (i1, i2 + d2), (i1 + 2, i2), 0)
    for r, off in enumerate(OFFS):
        for slot, d in enumerate((-1, 1)):
            for h in range(2):
                i1, i2 = pos[h]
                got(h, 1 + r, slot, (i1 + off, i2 + d), 0)
                put(h, 1 + r, 2 + slot, (i1, i2 - d), (i1 + off, i2 + d), 1 + slot)

    for copy in own[1:]:
        copy.wait()
    for a, ref in enumerate((m.traw, m.sraw)):
        arrived(ts_rows(ref, sibling), m.ts_s.at[a, 7], m.ts_r.at[a, 7], proto_dev(sibling))
        for d in range(1, 8):
            rows = ts_rows(ref, ((zi + 8 - d) % 8) * 2 + 1 - ci)
            arrived(rows, m.ts_s.at[a, 7 + d], m.ts_r.at[a, 7 + d], proto_dev(sibling))

    def unit(values):
        values = values.astype(F32)
        factor = lax.rsqrt(jnp.sum(values * values, axis=0, keepdims=True) + EPS)
        return values * factor, factor

    teacher, unused = unit(m.traw[...])
    m.tt[...] = jnp.transpose(teacher).astype(BF16)
    student, factor = unit(m.sraw[...])
    m.sscale[...] = factor
    m.su[...] = student.astype(BF16)
    m.st[...] = jnp.transpose(student).astype(BF16)

    own[0].wait()
    for r, off in enumerate(OFFS):
        for slot in range(2):
            for h in range(2):
                i1, i2 = pos[h]
                got(h, 1 + r, 2 + slot, (i1 + off, i2 + 2), 1 + slot)

    def cols_of(j):
        return pl.ds(pl.multiple_of(j * CHUNK, CHUNK), CHUNK)

    def teacher_chunk(j, carry):
        cols = cols_of(j)
        proto, factor = unit(m.praw[:, cols])
        proto = proto.astype(BF16)
        m.pu[:, cols] = proto
        m.pscale[:, cols] = factor
        c = jnp.dot(m.tt[...], proto, preferred_element_type=F32)
        e = jnp.exp2(c * (LOG2E / TEACHER_TEMP))
        m.expo[:, cols] = e
        m.colacc[:, cols] = jnp.sum(e.reshape(ROWS // 8, 8, CHUNK), axis=0)
        return carry

    def to_message(e):
        for j in range(NCHUNK):
            m.cx[e, xi, j : j + 1, pl.ds(0, CHUNK)] = jnp.sum(
                m.colacc[:, j * CHUNK : (j + 1) * CHUNK], axis=0, keepdims=True
            )

    lax.fori_loop(0, NCHUNK, teacher_chunk, 0)
    to_message(0)

    def ring_send(buf, me, dev, ss, rs):
        for d in range(1, SIDE):
            send(buf.at[me], buf.at[me], ss.at[d - 1], rs.at[d - 1], dev((me + d) % SIDE))

    def ring_sum(buf, me, dev, ss, rs):
        for d in range(1, SIDE):
            frm = (me + SIDE - d) % SIDE
            arrived(buf.at[frm], ss.at[d - 1], rs.at[d - 1], dev(frm))
        return (buf[0] + buf[1]) + (buf[2] + buf[3])

    def along_x(x):
        return batch_dev(yi, x)

    def along_y(y):
        return batch_dev(y, xi)

    def col_start(e):
        ring_send(m.cx.at[e], xi, along_x, m.cx_s.at[e], m.cx_r.at[e])

    def col_finish(e):
        m.cy[e, yi] = ring_sum(m.cx.at[e], xi, along_x, m.cx_s.at[e], m.cx_r.at[e])
        ring_send(m.cy.at[e], yi, along_y, m.cy_s.at[e], m.cy_r.at[e])
        return ring_sum(m.cy.at[e], yi, along_y, m.cy_s.at[e], m.cy_r.at[e])

    def row_start(e):
        for d in range(1, NP):
            send(m.rx.at[e, pi], m.rx.at[e, pi], m.rx_s.at[e, d - 1], m.rx_r.at[e, d - 1], proto_dev((pi + d) % NP))

    def row_finish(e):
        for d in range(1, NP):
            frm = (pi + NP - d) % NP
            arrived(m.rx.at[e, frm], m.rx_s.at[e, d - 1], m.rx_r.at[e, d - 1], proto_dev(frm))
        return jnp.sum(m.rx[e], axis=0)

    def to_rows(acc_ref, e, first):
        for q in range(4):
            block = jnp.transpose(acc_ref[q * 128 : (q + 1) * 128, :])
            m.rx[e, pi, pl.ds(first + q, 1), :] = jnp.sum(block, axis=0, keepdims=True)

    def to_columns(ref, rows):
        for q in range(4):
            ref[q * 128 : (q + 1) * 128, :] = jnp.transpose(jnp.broadcast_to(rows[q : q + 1], (128, 128)))

    m.cx[:, xi, :, pl.ds(CHUNK, 128)] = jnp.zeros((4, NCHUNK, 128), F32)
    col_start(0)

    m.rowacc[...] = jnp.zeros_like(m.rowacc)
    m.smax[...] = jnp.zeros_like(m.smax)

    def student_chunk(j, carry):
        cols = cols_of(j)
        c = jnp.dot(m.st[...], m.pu[:, cols], preferred_element_type=F32)
        m.cos[:, cols] = c
        e = jnp.exp2(c * (LOG2E / STUDENT_TEMP))
        m.smax[...] = jnp.maximum(m.smax[...], jnp.sum(e.reshape(ROWS // 8, 8, CHUNK), axis=0))
        m.rowacc[...] += (e[:, 0:128] + e[:, 128:256]) + (e[:, 256:384] + e[:, 384:512])
        return carry

    lax.fori_loop(0, NCHUNK, student_chunk, 0)
    to_rows(m.rowacc, 0, 4)

    def row_pass(e):
        for half in range(2):
            rows = pl.ds(half * 256, 256)

            def step(j, acc):
                for i in range(4):
                    cols = pl.ds(pl.multiple_of(j * CHUNK + i * 128, 128), 128)
                    acc = acc + m.expo[rows, cols].reshape(32, 8, 128) * m.pinv[:, cols]
                return acc

            m.rowacc[rows, :] = lax.fori_loop(0, NCHUNK, step, jnp.zeros((32, 8, 128), F32)).reshape(256, 128)
        to_rows(m.rowacc, e, 0)

    def col_pass(e):
        m.colacc[...] = jnp.zeros_like(m.colacc)

        def step(r, carry):
            rows = pl.ds(pl.multiple_of(r * 64, 64), 64)
            weights = m.csb[rows, :]
            for q in range(COLS // 128):
                cols = slice(q * 128, (q + 1) * 128)
                m.colacc[:, cols] += jnp.sum((m.expo[rows, cols] * weights).reshape(8, 8, 128), axis=0)
            return carry

        lax.fori_loop(0, ROWS // 64, step, 0)
        to_message(e)

    log_total = None
    for e in range(3):
        if e:
            col_pass(e)
            col_start(e)
        message = col_finish(e)
        total = message[:, :CHUNK]
        if e == 1:
            mass = message[0:2, CHUNK:]
        if e == 2:
            growth = jnp.max(total * inverse)
        inverse = 1.0 / total
        for j in range(NCHUNK):
            m.pinv[:, j * CHUNK : (j + 1) * CHUNK] = jnp.broadcast_to(inverse[j : j + 1], (8, CHUNK))
        if e == 1:
            m.rx[1, pi, 4:8, :] = jnp.zeros((4, 128), F32)
        if e == 2:
            m.rx[2, pi, 4:6, :] = jnp.zeros((2, 128), F32) + growth
            m.rx[2, pi, 6:8, :] = mass
        row_pass(e)
        row_start(e)
        rows = row_finish(e)
        to_columns(m.csb, 1.0 / rows[0:4])
        if e == 0:
            to_columns(m.itot, 1.0 / rows[4:8])
            log_total = jnp.sum(jnp.log(rows[4:8]), axis=0, keepdims=True)
            bound = jnp.max(jnp.sum(m.smax[...], axis=0, keepdims=True)) * jnp.max(1.0 / rows[4:8])
            m.cx[1, xi, :, pl.ds(CHUNK, 128)] = jnp.zeros((NCHUNK, 128), F32) + bound

    bound = (jnp.max(m.rx[2][:, 4:6, :]) + jnp.max(m.rx[2][:, 6:8, :])) * (1.05 / (CROPS * STUDENT_TEMP))
    wire_scale, wire_unscale = 131072.0 / bound, bound * (1.0 / 131072.0)

    def encode(values):
        values = values * wire_scale
        square = values * values
        return ((values * square) * (square * square)).astype(BF16)

    def decode(coded):
        coded = coded.astype(F32)
        root = jnp.exp2(jnp.log(jnp.maximum(jnp.abs(coded), 1e-37)) * (-6.0 / 7.0 * LOG2E))
        return (coded * root) * wire_unscale

    m.tlacc[...] = jnp.zeros_like(m.tlacc)
    m.cg[...] = jnp.zeros_like(m.cg)

    def grad_chunk(j, carry):
        cols = cols_of(j)

        def rows_step(r, inner):
            rows = pl.ds(pl.multiple_of(r * 64, 64), 64)
            weights, inv = m.csb[rows, :], m.itot[rows, :]
            tl = jnp.zeros((64, 128), F32)
            for i in range(4):
                sub = pl.ds(pl.multiple_of(j * CHUNK + i * 128, 128), 128)
                target = (m.expo[rows, sub].reshape(8, 8, 128) * m.pinv[:, sub]).reshape(64, 128) * weights
                c = m.cos[rows, sub]
                prob = jnp.exp2(c * (LOG2E / STUDENT_TEMP)) * inv
                tl = tl + target * c
                m.gl[rows, i * 128 : (i + 1) * 128] = ((prob - target) * (1.0 / (CROPS * STUDENT_TEMP))).astype(BF16)
            m.tlacc[...] += jnp.sum(tl.reshape(8, 8, 128), axis=0)
            return inner

        lax.fori_loop(0, ROWS // 64, rows_step, 0)
        g = m.gl[...]
        proto = m.pu[:, cols]
        part = jnp.dot(m.su[...], g, preferred_element_type=F32)
        m.gp[:, cols] = part
        m.cg[...] += lax.dot_general(proto, g, (((1,), (1,)), ((), ())), preferred_element_type=F32)
        m.colacc[:, cols] = jnp.sum((proto.astype(F32) * part).reshape(K // 8, 8, CHUNK), axis=0)
        return carry

    def rs_send(lane, h, axis, direction, slot):
        i1, i2 = pos[h]
        d = 1 - 2 * direction
        dev = (i1 + d, i2) if axis == 0 else (i1, i2 + d)
        src, dst, ss, rs = (r.at[h, direction, slot] for r in lane)
        send(src, dst, ss, rs, batch_dev(*where(h, *dev)))

    def rs_got(lane, h, axis, direction, slot):
        i1, i2 = pos[h]
        d = 1 - 2 * direction
        dev = (i1 - d, i2) if axis == 0 else (i1, i2 - d)
        unused, dst, ss, rs = (r.at[h, direction, slot] for r in lane)
        arrived(dst, ss, rs, batch_dev(*where(h, *dev)))
        return decode(dst[...])

    def load1(h, c, quarter):
        c = (c + SIDE) % SIDE
        cols = pl.ds(h * HALF + quarter * QUART, QUART)
        blocks = []
        for u in range(SIDE):
            y, x = (c, u) if h else (u, c)
            blocks.append(m.gp[pl.ds(row0(y, x), BLK), cols])
        return jnp.concatenate(blocks, axis=0)

    def load2(h, c, quarter):
        c = (c + SIDE) % SIDE
        return m.t1[h, pl.ds(pl.multiple_of(c * BLK, BLK), BLK), pl.ds(quarter * QUART, QUART)]

    lanes = ((m.s1, m.r1, m.rs1_s, m.rs1_r), (m.s2, m.r2, m.rs2_s, m.rs2_r))
    loads = (load1, load2)

    def rs_first(axis, h, quarter):
        at, lane, load = pos[h][axis], lanes[axis], loads[axis]
        lane[0][h, quarter, 0] = encode(load(h, at + 2, quarter))
        rs_send(lane, h, axis, quarter, 0)
        lane[0][h, 1 - quarter, 1] = encode(load(h, at - 1 + 2 * quarter, quarter))
        rs_send(lane, h, axis, 1 - quarter, 1)

    def rs_second(axis, h, quarter):
        at, lane, load = pos[h][axis], lanes[axis], loads[axis]
        lane[0][h, quarter, 2] = encode(load(h, at + 1 - 2 * quarter, quarter) + rs_got(lane, h, axis, quarter, 0))
        rs_send(lane, h, axis, quarter, 2)

    def rs_third(axis, h, quarter):
        at, lane, load = pos[h][axis], lanes[axis], loads[axis]
        return load(h, at, quarter) + rs_got(lane, h, axis, 1 - quarter, 1) + rs_got(lane, h, axis, quarter, 2)

    quarters = ((0, 0), (1, 0), (0, 1), (1, 1))
    for n, (h, quarter) in enumerate(quarters):
        first = h * 4 + quarter * 2
        lax.fori_loop(first, first + 2, grad_chunk, 0)
        rs_first(0, h, quarter)
        if n == 2:
            rs_second(0, *quarters[0])
    to_message(3)

    dot_rows = jnp.sum(m.su[...].astype(F32) * m.cg[...], axis=0, keepdims=True)
    for q in range(4):
        m.rx[3, pi, q : q + 1, :] = dot_rows[:, q * 128 : (q + 1) * 128]
    m.rx[3, pi, 4:8, :] = jnp.zeros((4, 128), F32)
    m.rx[3, pi, 4:5, :] = jnp.sum(m.tlacc[...], axis=0, keepdims=True)
    row_start(3)
    col_start(3)
    for p in range(NP):
        m.cgb[p % 2, p // 2] = m.cg[p * BLK : (p + 1) * BLK, :]
    send(m.cgb.at[1 - ci], m.cgr, m.cg_s.at[7], m.cg_r.at[7], proto_dev(sibling))

    for h, quarter in quarters[1:]:
        rs_second(0, h, quarter)

    arrived(m.cgr, m.cg_s.at[7], m.cg_r.at[7], proto_dev(sibling))
    m.cgs[...] = m.cgb[ci] + m.cgr[...]
    for d in range(1, 8):
        to = (zi + d) % 8
        send(m.cgs.at[to], m.cgz.at[zi], m.cg_s.at[d - 1], m.cg_r.at[d - 1], proto_dev(to * 2 + ci))
    m.cgz[zi] = m.cgs[zi]

    rows = row_finish(3)
    loss_rows = rows[4:5] * (1.0 / STUDENT_TEMP) - log_total
    m.lx[xi] = jnp.broadcast_to(loss_rows, (8, 128))
    ring_send(m.lx, xi, along_x, m.l_s.at[0], m.l_r.at[0])
    dots = col_finish(3)[:, :CHUNK]
    m.ly[yi] = ring_sum(m.lx, xi, along_x, m.l_s.at[0], m.l_r.at[0])
    ring_send(m.ly, yi, along_y, m.l_s.at[1], m.l_r.at[1])

    for h, quarter in quarters:
        m.t1[h, :, pl.ds(quarter * QUART, QUART)] = rs_third(0, h, quarter)
        rs_first(1, h, quarter)
    for h, quarter in quarters:
        rs_second(1, h, quarter)

    loss_out[0, 0] = jnp.sum(ring_sum(m.ly, yi, along_y, m.l_s.at[1], m.l_r.at[1])[0:1]) * (-1.0 / CROPS)
    for d in range(1, 8):
        frm = (zi + 8 - d) % 8
        arrived(m.cgz.at[frm], m.cg_s.at[d - 1], m.cg_r.at[d - 1], proto_dev(frm * 2 + ci))
    crop_part = jnp.sum(m.cgz[...], axis=0)
    student_own = m.su[pl.ds(pl.multiple_of(pi * BLK, BLK), BLK), :].astype(F32)
    for q in range(4):
        cols = slice(q * 128, (q + 1) * 128)
        gs_out[:, cols] = (crop_part[:, cols] - student_own[:, cols] * rows[q : q + 1]) * m.sscale[:, cols]

    for h, quarter in quarters:
        total = rs_third(1, h, quarter)
        for half in range(2):
            j = h * 4 + quarter * 2 + half
            cols = slice(j * CHUNK, (j + 1) * CHUNK)
            proto_own = m.pu[pl.ds(row0(yi, xi), BLK), cols].astype(F32)
            gp_out[:, cols] = (total[:, half * CHUNK : (half + 1) * CHUNK] - proto_own * dots[j : j + 1]) * m.pscale[:, cols]

    for copy in started:
        copy.wait_send()


def shards(teacher_emb, student_emb, prototypes):
    hbm = pl.BlockSpec(memory_space=pl.ANY)
    vmem = pl.BlockSpec(memory_space=pltpu.VMEM)
    grad_proto, grad_student, loss = pl.pallas_call(
        body,
        out_shape=(
            jax.ShapeDtypeStruct((BLK, COLS), F32),
            jax.ShapeDtypeStruct((BLK, ROWS), F32),
            jax.ShapeDtypeStruct((1, 1), F32),
        ),
        in_specs=[hbm] * 3,
        out_specs=(vmem, vmem, pl.BlockSpec(memory_space=pltpu.SMEM)),
        scratch_shapes=[pltpu.VMEM(shape, dtype) for shape, dtype in SCRATCH.values()]
        + [pltpu.SemaphoreType.DMA(shape) for shape in SEMS.values()],
        compiler_params=pltpu.CompilerParams(
            collective_id=0, has_side_effects=True, vmem_limit_bytes=58 * 1024 * 1024
        ),
    )(teacher_emb, student_emb, prototypes)
    return grad_proto, grad_student, loss.reshape(())


def solution(mesh):
    in_specs = (P("proto", "batch"), P("proto", "batch"), P("batch", "proto"))
    out_specs = (P("batch", "proto"), P("proto", "batch"), P())
    return jax.shard_map(shards, mesh=mesh, in_specs=in_specs, out_specs=out_specs, check_vma=False)
```

```python
import types

import jax
import jax.numpy as jnp
from jax import lax
from jax.experimental import pallas as pl
from jax.experimental.pallas import tpu as pltpu
from jax.sharding import PartitionSpec as P

F32, BF16 = jnp.float32, jnp.bfloat16
MESH = pl.DeviceIdType.MESH
LOG2E = 1.4426950408889634
TEACHER_TEMP, STUDENT_TEMP, EPS = 0.07, 0.1, 1e-6
K, ROWS, COLS = 256, 512, 4096
CHUNK = 512
NCHUNK = COLS // CHUNK
SIDE = 4
NP = 16
BLK = K // 16
QUART = COLS // 4
NEAR = (2, 1, 3)
LAG = 5
CROPS = ROWS * SIDE * SIDE
MSGW = CHUNK + 128

SCRATCH = dict(
    praw=((K, COLS), BF16),
    traw=((K, ROWS), BF16),
    sraw=((K, ROWS), BF16),
    tt=((ROWS, K), BF16),
    st=((ROWS, K), BF16),
    su=((K, ROWS), BF16),
    pu=((K, COLS), BF16),
    pscale=((1, COLS), F32),
    sscale=((1, ROWS), F32),
    expo=((ROWS, COLS), F32),
    cos=((ROWS, COLS), F32),
    rowacc=((ROWS, 128), F32),
    colacc=((8, COLS), F32),
    pinv=((8, COLS), F32),
    csb=((ROWS, 128), F32),
    itot=((ROWS, 128), F32),
    tlacc=((8, 128), F32),
    gl=((ROWS, CHUNK), BF16),
    gp=((K, COLS), F32),
    cg=((K, ROWS), F32),
    cgb=((2, 8, BLK, ROWS), F32),
    cgr=((8, BLK, ROWS), F32),
    cgz=((8, BLK, ROWS), F32),
    cgs=((8, BLK, ROWS), F32),
    cx=((3, SIDE * SIDE, NCHUNK, MSGW), F32),
    dx=((SIDE, NCHUNK, CHUNK), F32),
    dy=((SIDE, NCHUNK, CHUNK), F32),
    rx=((4, NP, 8, 128), F32),
    lx=((SIDE * SIDE, 8, 128), F32),
    s1=((NCHUNK, 3, SIDE * BLK, CHUNK), BF16),
    r1=((NCHUNK, 3, SIDE * BLK, CHUNK), BF16),
    t1=((NCHUNK, SIDE * BLK, CHUNK), F32),
    s2=((NCHUNK, 3, BLK, CHUNK), BF16),
    r2=((NCHUNK, 3, BLK, CHUNK), BF16),
    smax=((8, CHUNK), F32),
)
SEMS = dict(
    own=(3,),
    ag1_s=(4, 3),
    ag1_r=(4, 3),
    ag2_s=(4, 4, 3),
    ag2_r=(4, 4, 3),
    ts_s=(2, 16),
    ts_r=(2, 16),
    cx_s=(3, 15),
    cx_r=(3, 15),
    d_s=(2, 3),
    d_r=(2, 3),
    rx_s=(4, 15),
    rx_r=(4, 15),
    l_s=(15,),
    l_r=(15,),
    rs1_s=(NCHUNK, 3),
    rs1_r=(NCHUNK, 3),
    rs2_s=(NCHUNK, 3),
    rs2_r=(NCHUNK, 3),
    cg_s=(8,),
    cg_r=(8,),
)


def body(t_in, s_in, p_in, gp_out, gs_out, loss_out, *scratch):
    m = types.SimpleNamespace(**dict(zip(list(SCRATCH) + list(SEMS), scratch)))
    bi, pi = lax.axis_index("batch"), lax.axis_index("proto")
    yi, xi = bi // SIDE, bi % SIDE
    zi, ci = pi // 2, pi % 2
    started = []

    def batch_dev(y, x):
        return (y * SIDE + x, pi)

    def proto_dev(p):
        return (bi, p)

    def rdma(src, dst, ssem, rsem, dev):
        return pltpu.make_async_remote_copy(
            src_ref=src, dst_ref=dst, send_sem=ssem, recv_sem=rsem, device_id=dev, device_id_type=MESH
        )

    def send(src, dst, ssem, rsem, dev):
        copy = rdma(src, dst, ssem, rsem, dev)
        copy.start()
        started.append(copy)

    def arrived(dst, ssem, rsem, dev):
        rdma(dst, dst, ssem, rsem, dev).wait_recv()

    barrier = pltpu.get_barrier_semaphore()
    peers = []
    for d in range(1, NP):
        peers.append(((bi + d) % NP, pi))
        peers.append(proto_dev((pi + d) % NP))
    for peer in peers:
        pl.semaphore_signal(barrier, inc=1, device_id=peer, device_id_type=MESH)
    pl.semaphore_wait(barrier, len(peers))

    def where(h, c1, c2):
        c1, c2 = (c1 + SIDE) % SIDE, (c2 + SIDE) % SIDE
        return (c2, c1) if h == 0 else (c1, c2)

    pos = ((xi, yi), (yi, xi))

    def row0(y, x):
        return pl.multiple_of((y * SIDE + x) * BLK, BLK)

    def piece(k, y, x):
        return m.praw.at[pl.ds(row0(y, x), BLK), pl.ds(k * QUART, QUART)]

    own = [
        pltpu.make_async_copy(p_in, m.praw.at[pl.ds(row0(yi, xi), BLK), :], m.own.at[0]),
        pltpu.make_async_copy(t_in, m.traw.at[pl.ds(pl.multiple_of(pi * BLK, BLK), BLK), :], m.own.at[1]),
        pltpu.make_async_copy(s_in, m.sraw.at[pl.ds(pl.multiple_of(pi * BLK, BLK), BLK), :], m.own.at[2]),
    ]

    for k in range(4):
        i1, i2 = pos[k % 2]
        for d in NEAR:
            to = batch_dev(*where(k % 2, i1 + d, i2))
            send(p_in.at[:, pl.ds(k * QUART, QUART)], piece(k, yi, xi), m.ag1_s.at[k, d - 1], m.ag1_r.at[k, d - 1], to)
    for k in range(4):
        i1, i2 = pos[k % 2]
        for d in NEAR:
            to = batch_dev(*where(k % 2, i1, i2 + d))
            send(p_in.at[:, pl.ds(k * QUART, QUART)], piece(k, yi, xi), m.ag2_s.at[k, 0, d - 1], m.ag2_r.at[k, 0, d - 1], to)

    def ts_rows(ref, p):
        return ref.at[pl.ds(pl.multiple_of(p * BLK, BLK), BLK), :]

    sibling = zi * 2 + 1 - ci
    embeddings = ((t_in, m.traw), (s_in, m.sraw))
    for a, (src, ref) in enumerate(embeddings):
        for d in (4, 3, 5, 2, 6, 1, 7):
            peer = ((zi + d) % 8) * 2 + ci
            send(src, ts_rows(ref, pi), m.ts_s.at[a, d - 1], m.ts_r.at[a, d - 1], proto_dev(peer))
        send(src, ts_rows(ref, pi), m.ts_s.at[a, 7], m.ts_r.at[a, 7], proto_dev(sibling))
    for copy in own:
        copy.start()

    for k in range(4):
        h = k % 2
        i1, i2 = pos[h]
        for d in (1, 3, 2):
            y, x = where(h, i1 - d, i2)
            block = piece(k, y, x)
            arrived(block, m.ag1_s.at[k, d - 1], m.ag1_r.at[k, d - 1], batch_dev(y, x))
            for d2 in NEAR:
                send(block, block, m.ag2_s.at[k, d, d2 - 1], m.ag2_r.at[k, d, d2 - 1], batch_dev(*where(h, i1, i2 + d2)))

    def ts_forward(a):
        ref = embeddings[a][1]
        for d in (1, 7, 2, 6, 3, 5, 4):
            peer = ((zi + 8 - d) % 8) * 2 + ci
            rows = ts_rows(ref, peer)
            arrived(rows, m.ts_s.at[a, d - 1], m.ts_r.at[a, d - 1], proto_dev(peer))
            send(rows, rows, m.ts_s.at[a, 7 + d], m.ts_r.at[a, 7 + d], proto_dev(sibling))

    def ts_finish(a):
        ref = embeddings[a][1]
        own[1 + a].wait()
        arrived(ts_rows(ref, sibling), m.ts_s.at[a, 7], m.ts_r.at[a, 7], proto_dev(sibling))
        for d in range(1, 8):
            rows = ts_rows(ref, ((zi + 8 - d) % 8) * 2 + 1 - ci)
            arrived(rows, m.ts_s.at[a, 7 + d], m.ts_r.at[a, 7 + d], proto_dev(sibling))

    ts_forward(0)
    ts_forward(1)

    def unit(values):
        values = values.astype(F32)
        factor = lax.rsqrt(jnp.sum(values * values, axis=0, keepdims=True) + EPS)
        return values * factor, factor

    ts_finish(0)
    teacher, unused = unit(m.traw[...])
    m.tt[...] = jnp.transpose(teacher).astype(BF16)
    ts_finish(1)
    student, factor = unit(m.sraw[...])
    m.sscale[...] = factor
    m.su[...] = student.astype(BF16)
    m.st[...] = jnp.transpose(student).astype(BF16)
    own[0].wait()

    def cols_of(j):
        return pl.ds(j * CHUNK if isinstance(j, int) else pl.multiple_of(j * CHUNK, CHUNK), CHUNK)

    def teacher_chunk(j, carry):
        cols = cols_of(j)
        proto, factor = unit(m.praw[:, cols])
        proto = proto.astype(BF16)
        m.pu[:, cols] = proto
        m.pscale[:, cols] = factor
        c = jnp.dot(m.tt[...], proto, preferred_element_type=F32)
        e = jnp.exp2(c * (LOG2E / TEACHER_TEMP))
        m.expo[:, cols] = e
        m.colacc[:, cols] = jnp.sum(e.reshape(ROWS // 8, 8, CHUNK), axis=0)
        return carry

    def to_message(ref):
        for j in range(NCHUNK):
            ref[j : j + 1, pl.ds(0, CHUNK)] = jnp.sum(m.colacc[:, j * CHUNK : (j + 1) * CHUNK], axis=0, keepdims=True)

    for k in range(4):
        h = k % 2
        i1, i2 = pos[h]
        for r in range(4):
            for d in (1, 3, 2):
                y, x = where(h, i1 - r, i2 - d)
                arrived(piece(k, y, x), m.ag2_s.at[k, r, d - 1], m.ag2_r.at[k, r, d - 1], batch_dev(y, x))
        lax.fori_loop(2 * k, 2 * k + 2, teacher_chunk, 0)
    to_message(m.cx.at[0, bi])

    def all_send(buf, ss, rs):
        for d in range(1, NP):
            send(buf.at[bi], buf.at[bi], ss.at[d - 1], rs.at[d - 1], ((bi + d) % NP, pi))

    def all_sum(buf, ss, rs):
        for d in range(1, NP):
            frm = (bi + NP - d) % NP
            arrived(buf.at[frm], ss.at[d - 1], rs.at[d - 1], (frm, pi))
        return jnp.sum(buf[...], axis=0)

    def message(e):
        return m.cx.at[e] if e == 1 else m.cx.at[e, :, :, pl.ds(0, CHUNK)]

    def col_start(e):
        all_send(message(e), m.cx_s.at[e], m.cx_r.at[e])

    def col_finish(e):
        return all_sum(message(e), m.cx_s.at[e], m.cx_r.at[e])

    def ring_send(buf, me, dev, ss, rs):
        for d in NEAR:
            send(buf.at[me], buf.at[me], ss.at[d - 1], rs.at[d - 1], dev((me + d) % SIDE))

    def ring_sum(buf, me, dev, ss, rs):
        for d in range(1, SIDE):
            frm = (me + SIDE - d) % SIDE
            arrived(buf.at[frm], ss.at[d - 1], rs.at[d - 1], dev(frm))
        return (buf[0] + buf[1]) + (buf[2] + buf[3])

    def along_x(x):
        return batch_dev(yi, x)

    def along_y(y):
        return batch_dev(y, xi)

    def row_start(e):
        for d in range(1, NP):
            send(m.rx.at[e, pi], m.rx.at[e, pi], m.rx_s.at[e, d - 1], m.rx_r.at[e, d - 1], proto_dev((pi + d) % NP))

    def row_finish(e):
        for d in range(1, NP):
            frm = (pi + NP - d) % NP
            arrived(m.rx.at[e, frm], m.rx_s.at[e, d - 1], m.rx_r.at[e, d - 1], proto_dev(frm))
        return jnp.sum(m.rx[e], axis=0)

    def to_rows(acc_ref, e, first):
        for q in range(4):
            block = jnp.transpose(acc_ref[q * 128 : (q + 1) * 128, :])
            m.rx[e, pi, pl.ds(first + q, 1), :] = jnp.sum(block, axis=0, keepdims=True)

    def to_columns(ref, rows):
        for q in range(4):
            ref[q * 128 : (q + 1) * 128, :] = jnp.transpose(jnp.broadcast_to(rows[q : q + 1], (128, 128)))

    col_start(0)

    m.rowacc[...] = jnp.zeros_like(m.rowacc)
    m.smax[...] = jnp.zeros_like(m.smax)

    def student_chunk(j, carry):
        cols = cols_of(j)
        c = jnp.dot(m.st[...], m.pu[:, cols], preferred_element_type=F32)
        m.cos[:, cols] = c
        e = jnp.exp2(c * (LOG2E / STUDENT_TEMP))
        m.smax[...] = jnp.maximum(m.smax[...], jnp.sum(e.reshape(ROWS // 8, 8, CHUNK), axis=0))
        m.rowacc[...] += (e[:, 0:128] + e[:, 128:256]) + (e[:, 256:384] + e[:, 384:512])
        return carry

    lax.fori_loop(0, NCHUNK, student_chunk, 0)
    to_rows(m.rowacc, 0, 4)

    def row_pass(e):
        for half in range(2):
            rows = pl.ds(half * 256, 256)

            def step(j, acc):
                for i in range(4):
                    cols = pl.ds(pl.multiple_of(j * CHUNK + i * 128, 128), 128)
                    acc = acc + m.expo[rows, cols].reshape(32, 8, 128) * m.pinv[:, cols]
                return acc

            m.rowacc[rows, :] = lax.fori_loop(0, NCHUNK, step, jnp.zeros((32, 8, 128), F32)).reshape(256, 128)
        to_rows(m.rowacc, e, 0)

    def col_pass(e):
        m.colacc[...] = jnp.zeros_like(m.colacc)

        def step(r, carry):
            rows = pl.ds(pl.multiple_of(r * 64, 64), 64)
            weights = m.csb[rows, :]
            for q in range(COLS // 128):
                cols = slice(q * 128, (q + 1) * 128)
                m.colacc[:, cols] += jnp.sum((m.expo[rows, cols] * weights).reshape(8, 8, 128), axis=0)
            return carry

        lax.fori_loop(0, ROWS // 64, step, 0)
        to_message(m.cx.at[e, bi])

    log_total = None
    for e in range(3):
        if e:
            col_pass(e)
            col_start(e)
        sums = col_finish(e)
        total = sums[:, :CHUNK]
        if e == 1:
            mass = sums[0:2, CHUNK:]
        if e == 2:
            growth = jnp.max(total * inverse)
        inverse = 1.0 / total
        for j in range(NCHUNK):
            m.pinv[:, j * CHUNK : (j + 1) * CHUNK] = jnp.broadcast_to(inverse[j : j + 1], (8, CHUNK))
        if e == 1:
            m.rx[1, pi, 4:8, :] = jnp.zeros((4, 128), F32)
        if e == 2:
            m.rx[2, pi, 4:6, :] = jnp.zeros((2, 128), F32) + growth
            m.rx[2, pi, 6:8, :] = mass
        row_pass(e)
        row_start(e)
        rows = row_finish(e)
        to_columns(m.csb, 1.0 / rows[0:4])
        if e == 0:
            to_columns(m.itot, 1.0 / rows[4:8])
            log_total = jnp.sum(jnp.log(rows[4:8]), axis=0, keepdims=True)
            bound = jnp.max(jnp.sum(m.smax[...], axis=0, keepdims=True)) * jnp.max(1.0 / rows[4:8])
            m.cx[1, bi, :, pl.ds(CHUNK, 128)] = jnp.zeros((NCHUNK, 128), F32) + bound

    bound = (jnp.max(m.rx[2][:, 4:6, :]) + jnp.max(m.rx[2][:, 6:8, :])) * (1.05 / (CROPS * STUDENT_TEMP))
    wire_scale, wire_unscale = 8192.0 / bound, bound * (1.0 / 8192.0)

    def encode(values):
        values = values * wire_scale
        square = values * values
        e8 = square * square
        return (values * (e8 * e8)).astype(BF16)

    def decode(coded):
        coded = coded.astype(F32)
        root = jnp.exp2(jnp.log(jnp.maximum(jnp.abs(coded), 1e-37)) * (-8.0 / 9.0 * LOG2E))
        return (coded * root) * wire_unscale

    m.tlacc[...] = jnp.zeros_like(m.tlacc)
    m.cg[...] = jnp.zeros_like(m.cg)

    def grad_chunk(j, carry):
        cols = cols_of(j)

        def rows_step(r, inner):
            rows = pl.ds(pl.multiple_of(r * 64, 64), 64)
            weights, inv = m.csb[rows, :], m.itot[rows, :]
            tl = jnp.zeros((64, 128), F32)
            for i in range(4):
                sub = pl.ds(j * CHUNK + i * 128, 128)
                target = (m.expo[rows, sub].reshape(8, 8, 128) * m.pinv[:, sub]).reshape(64, 128) * weights
                c = m.cos[rows, sub]
                prob = jnp.exp2(c * (LOG2E / STUDENT_TEMP)) * inv
                tl = tl + target * c
                m.gl[rows, i * 128 : (i + 1) * 128] = ((prob - target) * (1.0 / (CROPS * STUDENT_TEMP))).astype(BF16)
            m.tlacc[...] += jnp.sum(tl.reshape(8, 8, 128), axis=0)
            return inner

        lax.fori_loop(0, ROWS // 64, rows_step, 0)
        g = m.gl[...]
        proto = m.pu[:, cols]
        part = jnp.dot(m.su[...], g, preferred_element_type=F32)
        m.gp[:, cols] = part
        m.cg[...] += lax.dot_general(proto, g, (((1,), (1,)), ((), ())), preferred_element_type=F32)
        m.colacc[:, cols] = jnp.sum((proto.astype(F32) * part).reshape(K // 8, 8, CHUNK), axis=0)
        return carry

    def first_rows(h, c, cols):
        c = (c + SIDE) % SIDE
        blocks = []
        for u in range(SIDE):
            y, x = (c, u) if h else (u, c)
            blocks.append(m.gp[pl.ds(row0(y, x), BLK), cols])
        return jnp.concatenate(blocks, axis=0)

    def second_rows(j, c):
        return m.t1[j, pl.ds(pl.multiple_of(((c + SIDE) % SIDE) * BLK, BLK), BLK), :]

    def first_send(j):
        h = j % 2
        i1, i2 = pos[h]
        for d in NEAR:
            m.s1[j, d - 1] = encode(first_rows(h, i1 + d, slice(j * CHUNK, (j + 1) * CHUNK)))
            to = batch_dev(*where(h, i1 + d, i2))
            send(m.s1.at[j, d - 1], m.r1.at[j, d - 1], m.rs1_s.at[j, d - 1], m.rs1_r.at[j, d - 1], to)

    def second_send(j):
        h = j % 2
        i1, i2 = pos[h]
        total = first_rows(h, i1, slice(j * CHUNK, (j + 1) * CHUNK))
        for d in range(1, SIDE):
            arrived(m.r1.at[j, d - 1], m.rs1_s.at[j, d - 1], m.rs1_r.at[j, d - 1], batch_dev(*where(h, i1 - d, i2)))
            total = total + decode(m.r1[j, d - 1])
        m.t1[j] = total
        for d in NEAR:
            m.s2[j, d - 1] = encode(second_rows(j, i2 + d))
            to = batch_dev(*where(h, i1, i2 + d))
            send(m.s2.at[j, d - 1], m.r2.at[j, d - 1], m.rs2_s.at[j, d - 1], m.rs2_r.at[j, d - 1], to)

    def reduced(j):
        h = j % 2
        i1, i2 = pos[h]
        total = second_rows(j, i2)
        for d in range(1, SIDE):
            arrived(m.r2.at[j, d - 1], m.rs2_s.at[j, d - 1], m.rs2_r.at[j, d - 1], batch_dev(*where(h, i1, i2 - d)))
            total = total + decode(m.r2[j, d - 1])
        return total

    for j in range(NCHUNK):
        grad_chunk(j, 0)
        first_send(j)
        if j >= LAG:
            second_send(j - LAG)
    for p in range(NP):
        m.cgb[p % 2, p // 2] = m.cg[p * BLK : (p + 1) * BLK, :]
    send(m.cgb.at[1 - ci], m.cgr, m.cg_s.at[7], m.cg_r.at[7], proto_dev(sibling))
    dot_rows = jnp.sum(m.su[...].astype(F32) * m.cg[...], axis=0, keepdims=True)
    for q in range(4):
        m.rx[3, pi, q : q + 1, :] = dot_rows[:, q * 128 : (q + 1) * 128]
    m.rx[3, pi, 4:8, :] = jnp.zeros((4, 128), F32)
    m.rx[3, pi, 4:5, :] = jnp.sum(m.tlacc[...], axis=0, keepdims=True)
    row_start(3)
    to_message(m.dx.at[xi])
    ring_send(m.dx, xi, along_x, m.d_s.at[0], m.d_r.at[0])

    arrived(m.cgr, m.cg_s.at[7], m.cg_r.at[7], proto_dev(sibling))
    m.cgs[...] = m.cgb[ci] + m.cgr[...]
    for d in range(1, 8):
        to = (zi + d) % 8
        send(m.cgs.at[to], m.cgz.at[zi], m.cg_s.at[d - 1], m.cg_r.at[d - 1], proto_dev(to * 2 + ci))
    m.cgz[zi] = m.cgs[zi]

    second_send(NCHUNK - LAG)
    m.dy[yi] = ring_sum(m.dx, xi, along_x, m.d_s.at[0], m.d_r.at[0])
    ring_send(m.dy, yi, along_y, m.d_s.at[1], m.d_r.at[1])
    second_send(NCHUNK - LAG + 1)

    rows = row_finish(3)
    loss_rows = rows[4:5] * (1.0 / STUDENT_TEMP) - log_total
    m.lx[bi] = jnp.broadcast_to(loss_rows, (8, 128))
    all_send(m.lx, m.l_s, m.l_r)
    for j in range(NCHUNK - LAG + 2, NCHUNK):
        second_send(j)
    dots = ring_sum(m.dy, yi, along_y, m.d_s.at[1], m.d_r.at[1])

    loss_out[0, 0] = jnp.sum(all_sum(m.lx, m.l_s, m.l_r)[0:1]) * (-1.0 / CROPS)
    for d in range(1, 8):
        frm = (zi + 8 - d) % 8
        arrived(m.cgz.at[frm], m.cg_s.at[d - 1], m.cg_r.at[d - 1], proto_dev(frm * 2 + ci))
    crop_part = jnp.sum(m.cgz[...], axis=0)
    student_own = m.su[pl.ds(pl.multiple_of(pi * BLK, BLK), BLK), :].astype(F32)
    for q in range(4):
        cols = slice(q * 128, (q + 1) * 128)
        gs_out[:, cols] = (crop_part[:, cols] - student_own[:, cols] * rows[q : q + 1]) * m.sscale[:, cols]

    proto_rows = pl.ds(row0(yi, xi), BLK)
    for j in range(NCHUNK):
        cols = slice(j * CHUNK, (j + 1) * CHUNK)
        proto_own = m.pu[proto_rows, cols].astype(F32)
        gp_out[:, cols] = (reduced(j) - proto_own * dots[j : j + 1]) * m.pscale[:, cols]

    for copy in started:
        copy.wait_send()


def shards(teacher_emb, student_emb, prototypes):
    hbm = pl.BlockSpec(memory_space=pl.ANY)
    vmem = pl.BlockSpec(memory_space=pltpu.VMEM)
    grad_proto, grad_student, loss = pl.pallas_call(
        body,
        out_shape=(
            jax.ShapeDtypeStruct((BLK, COLS), F32),
            jax.ShapeDtypeStruct((BLK, ROWS), F32),
            jax.ShapeDtypeStruct((1, 1), F32),
        ),
        in_specs=[hbm] * 3,
        out_specs=(vmem, vmem, pl.BlockSpec(memory_space=pltpu.SMEM)),
        scratch_shapes=[pltpu.VMEM(shape, dtype) for shape, dtype in SCRATCH.values()]
        + [pltpu.SemaphoreType.DMA(shape) for shape in SEMS.values()],
        compiler_params=pltpu.CompilerParams(
            collective_id=0, has_side_effects=True, vmem_limit_bytes=58 * 1024 * 1024
        ),
    )(teacher_emb, student_emb, prototypes)
    return grad_proto, grad_student, loss.reshape(())


def solution(mesh):
    in_specs = (P("proto", "batch"), P("proto", "batch"), P("batch", "proto"))
    out_specs = (P("batch", "proto"), P("proto", "batch"), P())
    return jax.shard_map(shards, mesh=mesh, in_specs=in_specs, out_specs=out_specs, check_vma=False)
```

```python
import types

import jax
import jax.numpy as jnp
from jax import lax
from jax.experimental import pallas as pl
from jax.experimental.pallas import tpu as pltpu
from jax.sharding import PartitionSpec as P

F32, BF16 = jnp.float32, jnp.bfloat16
MESH = pl.DeviceIdType.MESH
LOG2E = 1.4426950408889634
TEACHER_TEMP, STUDENT_TEMP, EPS = 0.07, 0.1, 1e-6
K, ROWS, COLS = 256, 512, 4096
CHUNK = 512
NCHUNK = COLS // CHUNK
SIDE = 4
NP = 16
BLK = K // 16
QUART = COLS // 4
NEAR = (2, 1, 3)
LAG = 5
CROPS = ROWS * SIDE * SIDE
WIRE_TOP = 8192.0
CROP_SCALE = WIRE_TOP * (CROPS * STUDENT_TEMP) / 2.1
MSGW = CHUNK + 128

SCRATCH = dict(
    praw=((K, COLS), BF16),
    traw=((K, ROWS), BF16),
    sraw=((K, ROWS), BF16),
    tt=((ROWS, K), BF16),
    st=((ROWS, K), BF16),
    su=((K, ROWS), BF16),
    pu=((K, COLS), BF16),
    pscale=((1, COLS), F32),
    sscale=((1, ROWS), F32),
    expo=((ROWS, COLS), F32),
    cos=((ROWS, COLS), F32),
    rowacc=((ROWS, 128), F32),
    colacc=((8, COLS), F32),
    pinv=((8, COLS), F32),
    csb=((ROWS, 128), F32),
    itot=((ROWS, 128), F32),
    tlacc=((8, 128), F32),
    gl=((ROWS, CHUNK), BF16),
    gp=((K, COLS), F32),
    cg=((K, ROWS), F32),
    cgb=((2, 8, BLK, ROWS), F32),
    cgr=((8, BLK, ROWS), F32),
    cgz=((8, BLK, ROWS), BF16),
    cgs=((8, BLK, ROWS), BF16),
    cgm=((8, BLK, ROWS), F32),
    cx=((3, SIDE * SIDE, NCHUNK, MSGW), F32),
    dx=((SIDE, NCHUNK, CHUNK), F32),
    dy=((SIDE, NCHUNK, CHUNK), F32),
    rx=((4, NP, 8, 128), F32),
    lx=((SIDE * SIDE, 8, 128), F32),
    s1=((NCHUNK, 3, SIDE * BLK, CHUNK), BF16),
    r1=((NCHUNK, 3, SIDE * BLK, CHUNK), BF16),
    t1=((NCHUNK, SIDE * BLK, CHUNK), F32),
    s2=((NCHUNK, 3, BLK, CHUNK), BF16),
    r2=((NCHUNK, 3, BLK, CHUNK), BF16),
    smax=((8, CHUNK), F32),
)
SEMS = dict(
    own=(3,),
    ag1_s=(4, 3),
    ag1_r=(4, 3),
    ag2_s=(4, 4, 3),
    ag2_r=(4, 4, 3),
    ts_s=(2, 16),
    ts_r=(2, 16),
    cx_s=(3, 15),
    cx_r=(3, 15),
    d_s=(2, 3),
    d_r=(2, 3),
    rx_s=(4, 15),
    rx_r=(4, 15),
    l_s=(15,),
    l_r=(15,),
    rs1_s=(NCHUNK, 3),
    rs1_r=(NCHUNK, 3),
    rs2_s=(NCHUNK, 3),
    rs2_r=(NCHUNK, 3),
    cg_s=(8,),
    cg_r=(8,),
)


def body(t_in, s_in, p_in, gp_out, gs_out, loss_out, *scratch):
    m = types.SimpleNamespace(**dict(zip(list(SCRATCH) + list(SEMS), scratch)))
    bi, pi = lax.axis_index("batch"), lax.axis_index("proto")
    yi, xi = bi // SIDE, bi % SIDE
    zi, ci = pi // 2, pi % 2
    started = []

    def batch_dev(y, x):
        return (y * SIDE + x, pi)

    def proto_dev(p):
        return (bi, p)

    def rdma(src, dst, ssem, rsem, dev):
        return pltpu.make_async_remote_copy(
            src_ref=src, dst_ref=dst, send_sem=ssem, recv_sem=rsem, device_id=dev, device_id_type=MESH
        )

    def send(src, dst, ssem, rsem, dev):
        copy = rdma(src, dst, ssem, rsem, dev)
        copy.start()
        started.append(copy)

    def arrived(dst, ssem, rsem, dev):
        rdma(dst, dst, ssem, rsem, dev).wait_recv()

    barrier = pltpu.get_barrier_semaphore()
    peers = []
    for d in (8, 9, 7, 6, 10, 11, 5, 4, 12, 13, 3, 2, 14, 15, 1):
        peers.append(proto_dev((pi + d) % NP))
    for d in (10, 9, 11, 6, 14, 8, 2, 5, 7, 13, 15, 1, 3, 4, 12):
        peers.append(((bi + d) % NP, pi))
    for peer in peers:
        pl.semaphore_signal(barrier, inc=1, device_id=peer, device_id_type=MESH)
    pl.semaphore_wait(barrier, len(peers))

    def where(h, c1, c2):
        c1, c2 = (c1 + SIDE) % SIDE, (c2 + SIDE) % SIDE
        return (c2, c1) if h == 0 else (c1, c2)

    pos = ((xi, yi), (yi, xi))

    def row0(y, x):
        return pl.multiple_of((y * SIDE + x) * BLK, BLK)

    def piece(k, y, x):
        return m.praw.at[pl.ds(row0(y, x), BLK), pl.ds(k * QUART, QUART)]

    own = [
        pltpu.make_async_copy(p_in, m.praw.at[pl.ds(row0(yi, xi), BLK), :], m.own.at[0]),
        pltpu.make_async_copy(t_in, m.traw.at[pl.ds(pl.multiple_of(pi * BLK, BLK), BLK), :], m.own.at[1]),
        pltpu.make_async_copy(s_in, m.sraw.at[pl.ds(pl.multiple_of(pi * BLK, BLK), BLK), :], m.own.at[2]),
    ]

    for k in range(4):
        i1, i2 = pos[k % 2]
        for d in NEAR:
            to = batch_dev(*where(k % 2, i1 + d, i2))
            send(p_in.at[:, pl.ds(k * QUART, QUART)], piece(k, yi, xi), m.ag1_s.at[k, d - 1], m.ag1_r.at[k, d - 1], to)
    for k in range(4):
        i1, i2 = pos[k % 2]
        for d in NEAR:
            to = batch_dev(*where(k % 2, i1, i2 + d))
            send(p_in.at[:, pl.ds(k * QUART, QUART)], piece(k, yi, xi), m.ag2_s.at[k, 0, d - 1], m.ag2_r.at[k, 0, d - 1], to)

    def ts_rows(ref, p):
        return ref.at[pl.ds(pl.multiple_of(p * BLK, BLK), BLK), :]

    sibling = zi * 2 + 1 - ci
    embeddings = ((t_in, m.traw), (s_in, m.sraw))
    for a, (src, ref) in enumerate(embeddings):
        for d in (4, 3, 5, 2, 6, 1, 7):
            peer = ((zi + d) % 8) * 2 + ci
            send(src, ts_rows(ref, pi), m.ts_s.at[a, d - 1], m.ts_r.at[a, d - 1], proto_dev(peer))
        send(src, ts_rows(ref, pi), m.ts_s.at[a, 7], m.ts_r.at[a, 7], proto_dev(sibling))
    for copy in own:
        copy.start()

    for k in range(4):
        h = k % 2
        i1, i2 = pos[h]
        for d in (1, 3, 2):
            y, x = where(h, i1 - d, i2)
            block = piece(k, y, x)
            arrived(block, m.ag1_s.at[k, d - 1], m.ag1_r.at[k, d - 1], batch_dev(y, x))
            for d2 in NEAR:
                send(block, block, m.ag2_s.at[k, d, d2 - 1], m.ag2_r.at[k, d, d2 - 1], batch_dev(*where(h, i1, i2 + d2)))

    def ts_forward(a):
        ref = embeddings[a][1]
        for d in (1, 7, 2, 6, 3, 5, 4):
            peer = ((zi + 8 - d) % 8) * 2 + ci
            rows = ts_rows(ref, peer)
            arrived(rows, m.ts_s.at[a, d - 1], m.ts_r.at[a, d - 1], proto_dev(peer))
            send(rows, rows, m.ts_s.at[a, 7 + d], m.ts_r.at[a, 7 + d], proto_dev(sibling))

    def ts_finish(a):
        ref = embeddings[a][1]
        own[1 + a].wait()
        arrived(ts_rows(ref, sibling), m.ts_s.at[a, 7], m.ts_r.at[a, 7], proto_dev(sibling))
        for d in range(1, 8):
            rows = ts_rows(ref, ((zi + 8 - d) % 8) * 2 + 1 - ci)
            arrived(rows, m.ts_s.at[a, 7 + d], m.ts_r.at[a, 7 + d], proto_dev(sibling))

    ts_forward(0)
    ts_forward(1)

    def unit(values):
        values = values.astype(F32)
        factor = lax.rsqrt(jnp.sum(values * values, axis=0, keepdims=True) + EPS)
        return values * factor, factor

    ts_finish(0)
    teacher, unused = unit(m.traw[...])
    m.tt[...] = jnp.transpose(teacher).astype(BF16)
    ts_finish(1)
    student, factor = unit(m.sraw[...])
    m.sscale[...] = factor
    m.su[...] = student.astype(BF16)
    m.st[...] = jnp.transpose(student).astype(BF16)
    own[0].wait()

    def cols_of(j):
        return pl.ds(j * CHUNK if isinstance(j, int) else pl.multiple_of(j * CHUNK, CHUNK), CHUNK)

    def teacher_chunk(j, carry):
        cols = cols_of(j)
        proto, factor = unit(m.praw[:, cols])
        proto = proto.astype(BF16)
        m.pu[:, cols] = proto
        m.pscale[:, cols] = factor
        c = jnp.dot(m.tt[...], proto, preferred_element_type=F32)
        e = jnp.exp2(c * (LOG2E / TEACHER_TEMP))
        m.expo[:, cols] = e
        m.colacc[:, cols] = jnp.sum(e.reshape(ROWS // 8, 8, CHUNK), axis=0)
        return carry

    def to_message(ref):
        for j in range(NCHUNK):
            ref[j : j + 1, pl.ds(0, CHUNK)] = jnp.sum(m.colacc[:, j * CHUNK : (j + 1) * CHUNK], axis=0, keepdims=True)

    for k in range(4):
        h = k % 2
        i1, i2 = pos[h]
        for r in range(4):
            for d in (1, 3, 2):
                y, x = where(h, i1 - r, i2 - d)
                arrived(piece(k, y, x), m.ag2_s.at[k, r, d - 1], m.ag2_r.at[k, r, d - 1], batch_dev(y, x))
        lax.fori_loop(2 * k, 2 * k + 2, teacher_chunk, 0)
    to_message(m.cx.at[0, bi])

    def all_send(buf, ss, rs):
        for d in range(1, NP):
            send(buf.at[bi], buf.at[bi], ss.at[d - 1], rs.at[d - 1], ((bi + d) % NP, pi))

    def all_sum(buf, ss, rs):
        for d in range(1, NP):
            frm = (bi + NP - d) % NP
            arrived(buf.at[frm], ss.at[d - 1], rs.at[d - 1], (frm, pi))
        return jnp.sum(buf[...], axis=0)

    def message(e):
        return m.cx.at[e] if e == 1 else m.cx.at[e, :, :, pl.ds(0, CHUNK)]

    def col_start(e):
        all_send(message(e), m.cx_s.at[e], m.cx_r.at[e])

    def col_finish(e):
        return all_sum(message(e), m.cx_s.at[e], m.cx_r.at[e])

    def ring_send(buf, me, dev, ss, rs):
        for d in NEAR:
            send(buf.at[me], buf.at[me], ss.at[d - 1], rs.at[d - 1], dev((me + d) % SIDE))

    def ring_sum(buf, me, dev, ss, rs):
        for d in range(1, SIDE):
            frm = (me + SIDE - d) % SIDE
            arrived(buf.at[frm], ss.at[d - 1], rs.at[d - 1], dev(frm))
        return (buf[0] + buf[1]) + (buf[2] + buf[3])

    def along_x(x):
        return batch_dev(yi, x)

    def along_y(y):
        return batch_dev(y, xi)

    def row_start(e):
        for d in range(1, NP):
            send(m.rx.at[e, pi], m.rx.at[e, pi], m.rx_s.at[e, d - 1], m.rx_r.at[e, d - 1], proto_dev((pi + d) % NP))

    def row_finish(e):
        for d in range(1, NP):
            frm = (pi + NP - d) % NP
            arrived(m.rx.at[e, frm], m.rx_s.at[e, d - 1], m.rx_r.at[e, d - 1], proto_dev(frm))
        return jnp.sum(m.rx[e], axis=0)

    def to_rows(acc_ref, e, first):
        for q in range(4):
            block = jnp.transpose(acc_ref[q * 128 : (q + 1) * 128, :])
            m.rx[e, pi, pl.ds(first + q, 1), :] = jnp.sum(block, axis=0, keepdims=True)

    def to_columns(ref, rows):
        for q in range(4):
            ref[q * 128 : (q + 1) * 128, :] = jnp.transpose(jnp.broadcast_to(rows[q : q + 1], (128, 128)))

    col_start(0)

    m.rowacc[...] = jnp.zeros_like(m.rowacc)
    m.smax[...] = jnp.zeros_like(m.smax)

    def student_chunk(j, carry):
        cols = cols_of(j)
        c = jnp.dot(m.st[...], m.pu[:, cols], preferred_element_type=F32)
        m.cos[:, cols] = c
        e = jnp.exp2(c * (LOG2E / STUDENT_TEMP))
        m.smax[...] = jnp.maximum(m.smax[...], jnp.sum(e.reshape(ROWS // 8, 8, CHUNK), axis=0))
        m.rowacc[...] += (e[:, 0:128] + e[:, 128:256]) + (e[:, 256:384] + e[:, 384:512])
        return carry

    lax.fori_loop(0, NCHUNK, student_chunk, 0)
    to_rows(m.rowacc, 0, 4)

    def row_pass(e):
        def step(r, carry):
            rows = pl.ds(pl.multiple_of(r * 64, 64), 64)
            acc = jnp.zeros((8, 8, 128), F32)
            for q in range(COLS // 128):
                cols = slice(q * 128, (q + 1) * 128)
                acc = acc + m.expo[rows, cols].reshape(8, 8, 128) * m.pinv[:, cols]
            m.rowacc[rows, :] = acc.reshape(64, 128)
            return carry

        lax.fori_loop(0, ROWS // 64, step, 0)
        to_rows(m.rowacc, e, 0)

    def col_pass(e):
        m.colacc[...] = jnp.zeros_like(m.colacc)

        def step(r, carry):
            rows = pl.ds(pl.multiple_of(r * 64, 64), 64)
            weights = m.csb[rows, :]
            for q in range(COLS // 128):
                cols = slice(q * 128, (q + 1) * 128)
                m.colacc[:, cols] += jnp.sum((m.expo[rows, cols] * weights).reshape(8, 8, 128), axis=0)
            return carry

        lax.fori_loop(0, ROWS // 64, step, 0)
        to_message(m.cx.at[e, bi])

    log_total = None
    for e in range(3):
        if e:
            col_pass(e)
            col_start(e)
        sums = col_finish(e)
        total = sums[:, :CHUNK]
        if e == 1:
            mass = sums[0:2, CHUNK:]
        if e == 2:
            growth = jnp.max(total * inverse)
        inverse = 1.0 / total
        for j in range(NCHUNK):
            m.pinv[:, j * CHUNK : (j + 1) * CHUNK] = jnp.broadcast_to(inverse[j : j + 1], (8, CHUNK))
        if e == 1:
            m.rx[1, pi, 4:8, :] = jnp.zeros((4, 128), F32)
        if e == 2:
            m.rx[2, pi, 4:6, :] = jnp.zeros((2, 128), F32) + growth
            m.rx[2, pi, 6:8, :] = mass
        row_pass(e)
        row_start(e)
        rows = row_finish(e)
        to_columns(m.csb, 1.0 / rows[0:4])
        if e == 0:
            to_columns(m.itot, 1.0 / rows[4:8])
            log_total = jnp.sum(jnp.log(rows[4:8]), axis=0, keepdims=True)
            bound = jnp.max(jnp.sum(m.smax[...], axis=0, keepdims=True)) * jnp.max(1.0 / rows[4:8])
            m.cx[1, bi, :, pl.ds(CHUNK, 128)] = jnp.zeros((NCHUNK, 128), F32) + bound

    bound = (jnp.max(m.rx[2][:, 4:6, :]) + jnp.max(m.rx[2][:, 6:8, :])) * (1.05 / (CROPS * STUDENT_TEMP))
    wire_scale, wire_unscale = WIRE_TOP / bound, bound * (1.0 / WIRE_TOP)

    def encode(values, scale):
        values = values * scale
        square = values * values
        e8 = square * square
        return (values * (e8 * e8)).astype(BF16)

    def decode(coded, unscale):
        coded = coded.astype(F32)
        root = jnp.exp2(jnp.log(jnp.maximum(jnp.abs(coded), 1e-37)) * (-8.0 / 9.0 * LOG2E))
        return (coded * root) * unscale

    m.tlacc[...] = jnp.zeros_like(m.tlacc)
    m.cg[...] = jnp.zeros_like(m.cg)

    def grad_chunk(j, carry):
        cols = cols_of(j)

        def rows_step(r, inner):
            rows = pl.ds(pl.multiple_of(r * 64, 64), 64)
            weights, inv = m.csb[rows, :], m.itot[rows, :]
            tl = jnp.zeros((64, 128), F32)
            for i in range(4):
                sub = pl.ds(j * CHUNK + i * 128, 128)
                target = (m.expo[rows, sub].reshape(8, 8, 128) * m.pinv[:, sub]).reshape(64, 128) * weights
                c = m.cos[rows, sub]
                prob = jnp.exp2(c * (LOG2E / STUDENT_TEMP)) * inv
                tl = tl + target * c
                m.gl[rows, i * 128 : (i + 1) * 128] = ((prob - target) * (1.0 / (CROPS * STUDENT_TEMP))).astype(BF16)
            m.tlacc[...] += jnp.sum(tl.reshape(8, 8, 128), axis=0)
            return inner

        lax.fori_loop(0, ROWS // 64, rows_step, 0)
        g = m.gl[...]
        proto = m.pu[:, cols]
        part = jnp.dot(m.su[...], g, preferred_element_type=F32)
        m.gp[:, cols] = part
        m.cg[...] += lax.dot_general(proto, g, (((1,), (1,)), ((), ())), preferred_element_type=F32)
        m.colacc[:, cols] = jnp.sum((proto.astype(F32) * part).reshape(K // 8, 8, CHUNK), axis=0)
        return carry

    def first_rows(h, c, cols):
        c = (c + SIDE) % SIDE
        blocks = []
        for u in range(SIDE):
            y, x = (c, u) if h else (u, c)
            blocks.append(m.gp[pl.ds(row0(y, x), BLK), cols])
        return jnp.concatenate(blocks, axis=0)

    def second_rows(j, c):
        return m.t1[j, pl.ds(pl.multiple_of(((c + SIDE) % SIDE) * BLK, BLK), BLK), :]

    def first_send(j):
        h = j % 2
        i1, i2 = pos[h]
        for d in NEAR:
            m.s1[j, d - 1] = encode(first_rows(h, i1 + d, slice(j * CHUNK, (j + 1) * CHUNK)), wire_scale)
            to = batch_dev(*where(h, i1 + d, i2))
            send(m.s1.at[j, d - 1], m.r1.at[j, d - 1], m.rs1_s.at[j, d - 1], m.rs1_r.at[j, d - 1], to)

    def second_send(j):
        h = j % 2
        i1, i2 = pos[h]
        total = first_rows(h, i1, slice(j * CHUNK, (j + 1) * CHUNK))
        for d in range(1, SIDE):
            arrived(m.r1.at[j, d - 1], m.rs1_s.at[j, d - 1], m.rs1_r.at[j, d - 1], batch_dev(*where(h, i1 - d, i2)))
            total = total + decode(m.r1[j, d - 1], wire_unscale)
        m.t1[j] = total
        for d in NEAR:
            m.s2[j, d - 1] = encode(second_rows(j, i2 + d), wire_scale)
            to = batch_dev(*where(h, i1, i2 + d))
            send(m.s2.at[j, d - 1], m.r2.at[j, d - 1], m.rs2_s.at[j, d - 1], m.rs2_r.at[j, d - 1], to)

    def reduced(j):
        h = j % 2
        i1, i2 = pos[h]
        total = second_rows(j, i2)
        for d in range(1, SIDE):
            arrived(m.r2.at[j, d - 1], m.rs2_s.at[j, d - 1], m.rs2_r.at[j, d - 1], batch_dev(*where(h, i1, i2 - d)))
            total = total + decode(m.r2[j, d - 1], wire_unscale)
        return total

    for j in range(NCHUNK):
        grad_chunk(j, 0)
        first_send(j)
        if j >= LAG:
            second_send(j - LAG)
    for p in range(NP):
        m.cgb[p % 2, p // 2] = m.cg[p * BLK : (p + 1) * BLK, :]
    send(m.cgb.at[1 - ci], m.cgr, m.cg_s.at[7], m.cg_r.at[7], proto_dev(sibling))
    dot_rows = jnp.sum(m.su[...].astype(F32) * m.cg[...], axis=0, keepdims=True)
    for q in range(4):
        m.rx[3, pi, q : q + 1, :] = dot_rows[:, q * 128 : (q + 1) * 128]
    m.rx[3, pi, 4:8, :] = jnp.zeros((4, 128), F32)
    m.rx[3, pi, 4:5, :] = jnp.sum(m.tlacc[...], axis=0, keepdims=True)
    row_start(3)
    to_message(m.dx.at[xi])
    ring_send(m.dx, xi, along_x, m.d_s.at[0], m.d_r.at[0])

    arrived(m.cgr, m.cg_s.at[7], m.cg_r.at[7], proto_dev(sibling))
    m.cgm[...] = m.cgb[ci] + m.cgr[...]
    m.cgs[...] = encode(m.cgm[...], CROP_SCALE)
    for d in range(1, 8):
        to = (zi + d) % 8
        send(m.cgs.at[to], m.cgz.at[zi], m.cg_s.at[d - 1], m.cg_r.at[d - 1], proto_dev(to * 2 + ci))

    second_send(NCHUNK - LAG)
    m.dy[yi] = ring_sum(m.dx, xi, along_x, m.d_s.at[0], m.d_r.at[0])
    ring_send(m.dy, yi, along_y, m.d_s.at[1], m.d_r.at[1])
    second_send(NCHUNK - LAG + 1)

    rows = row_finish(3)
    loss_rows = rows[4:5] * (1.0 / STUDENT_TEMP) - log_total
    m.lx[bi] = jnp.broadcast_to(loss_rows, (8, 128))
    all_send(m.lx, m.l_s, m.l_r)
    for j in range(NCHUNK - LAG + 2, NCHUNK):
        second_send(j)
    dots = ring_sum(m.dy, yi, along_y, m.d_s.at[1], m.d_r.at[1])

    loss_out[0, 0] = jnp.sum(all_sum(m.lx, m.l_s, m.l_r)[0:1]) * (-1.0 / CROPS)
    crop_part = m.cgm[zi]
    for d in range(1, 8):
        frm = (zi + 8 - d) % 8
        arrived(m.cgz.at[frm], m.cg_s.at[d - 1], m.cg_r.at[d - 1], proto_dev(frm * 2 + ci))
        crop_part = crop_part + decode(m.cgz[frm], 1.0 / CROP_SCALE)
    student_own = m.su[pl.ds(pl.multiple_of(pi * BLK, BLK), BLK), :].astype(F32)
    for q in range(4):
        cols = slice(q * 128, (q + 1) * 128)
        gs_out[:, cols] = (crop_part[:, cols] - student_own[:, cols] * rows[q : q + 1]) * m.sscale[:, cols]

    proto_rows = pl.ds(row0(yi, xi), BLK)
    for j in range(NCHUNK):
        cols = slice(j * CHUNK, (j + 1) * CHUNK)
        proto_own = m.pu[proto_rows, cols].astype(F32)
        gp_out[:, cols] = (reduced(j) - proto_own * dots[j : j + 1]) * m.pscale[:, cols]

    for copy in started:
        copy.wait_send()


def shards(teacher_emb, student_emb, prototypes):
    hbm = pl.BlockSpec(memory_space=pl.ANY)
    vmem = pl.BlockSpec(memory_space=pltpu.VMEM)
    grad_proto, grad_student, loss = pl.pallas_call(
        body,
        out_shape=(
            pltpu.VMEM((BLK, COLS), F32),
            pltpu.VMEM((BLK, ROWS), F32),
            jax.ShapeDtypeStruct((1, 1), F32),
        ),
        in_specs=[hbm] * 3,
        out_specs=(vmem, vmem, pl.BlockSpec(memory_space=pltpu.SMEM)),
        scratch_shapes=[pltpu.VMEM(shape, dtype) for shape, dtype in SCRATCH.values()]
        + [pltpu.SemaphoreType.DMA(shape) for shape in SEMS.values()],
        compiler_params=pltpu.CompilerParams(
            collective_id=0, has_side_effects=True, vmem_limit_bytes=58 * 1024 * 1024
        ),
    )(teacher_emb, student_emb, prototypes)
    return grad_proto, grad_student, loss.reshape(())


def solution(mesh):
    in_specs = (P("proto", "batch"), P("proto", "batch"), P("batch", "proto"))
    out_specs = (P("batch", "proto"), P("proto", "batch"), P())
    return jax.shard_map(shards, mesh=mesh, in_specs=in_specs, out_specs=out_specs, check_vma=False)
```

```python
import types

import jax
import jax.numpy as jnp
from jax import lax
from jax.experimental import pallas as pl
from jax.experimental.pallas import tpu as pltpu
from jax.sharding import PartitionSpec as P

F32, BF16 = jnp.float32, jnp.bfloat16
MESH = pl.DeviceIdType.MESH
LOG2E = 1.4426950408889634
TEACHER_TEMP, STUDENT_TEMP, EPS = 0.07, 0.1, 1e-6
K, ROWS, COLS = 256, 512, 4096
CHUNK = 512
NCHUNK = COLS // CHUNK
SIDE = 4
NP = 16
BLK = K // 16
QUART = COLS // 4
NEAR = (2, 1, 3)
LAG = 5
RELAYED = (0, 1, 2)
CROPS = ROWS * SIDE * SIDE
WIRE_TOP = 8192.0
CROP_SCALE = WIRE_TOP * (CROPS * STUDENT_TEMP) / 2.1
MSGW = CHUNK + 128


def hops(step, size):
    return min(step, size - step)


BATCH_STEPS = sorted(
    ((dy, dx) for dy in range(SIDE) for dx in range(SIDE) if dy or dx), key=lambda s: -hops(s[0], SIDE) - hops(s[1], SIDE)
)
PROTO_STEPS = sorted(((dz, dc) for dz in range(8) for dc in range(2) if dz or dc), key=lambda s: -2 * hops(s[0], 8) - s[1])

SCRATCH = dict(
    praw=((K, COLS), BF16),
    traw=((K, ROWS), BF16),
    sraw=((K, ROWS), BF16),
    tt=((ROWS, K), BF16),
    st=((ROWS, K), BF16),
    su=((K, ROWS), BF16),
    pu=((K, COLS), BF16),
    pscale=((1, COLS), F32),
    sscale=((1, ROWS), F32),
    expo=((ROWS, COLS), F32),
    cos=((ROWS, COLS), F32),
    rowacc=((ROWS, 128), F32),
    colacc=((8, COLS), F32),
    pinv=((8, COLS), F32),
    csb=((ROWS, 128), F32),
    itot=((ROWS, 128), F32),
    tlacc=((8, 128), F32),
    gl=((ROWS, CHUNK), BF16),
    gp=((K, COLS), F32),
    cg=((K, ROWS), F32),
    cgb=((2, 8, BLK, ROWS), F32),
    cgr=((8, BLK, ROWS), F32),
    cgz=((8, BLK, ROWS), BF16),
    cgs=((8, BLK, ROWS), BF16),
    cgm=((8, BLK, ROWS), F32),
    cx=((3, SIDE * SIDE, NCHUNK, MSGW), F32),
    dx=((SIDE, NCHUNK, CHUNK), F32),
    dy=((SIDE, NCHUNK, CHUNK), F32),
    rx=((4, NP, 8, 128), F32),
    lx=((SIDE * SIDE, 8, 128), F32),
    s1=((NCHUNK, 3, SIDE * BLK, CHUNK), BF16),
    r1=((NCHUNK, 3, SIDE * BLK, CHUNK), BF16),
    t1=((NCHUNK, SIDE * BLK, CHUNK), F32),
    s2=((NCHUNK, 3, BLK, CHUNK), BF16),
    r2=((NCHUNK, 3, BLK, CHUNK), BF16),
    smax=((8, CHUNK), F32),
)
SEMS = dict(
    own=(3,),
    ag1_s=(4, 3),
    ag1_r=(4, 3),
    ag2_s=(4, 4, 4),
    ag2_r=(4, 4, 4),
    ts_s=(2, 16),
    ts_r=(2, 16),
    cx_s=(3, 15),
    cx_r=(3, 15),
    d_s=(2, 3),
    d_r=(2, 3),
    rx_s=(4, 15),
    rx_r=(4, 15),
    l_s=(15,),
    l_r=(15,),
    rs1_s=(NCHUNK, 3),
    rs1_r=(NCHUNK, 3),
    rs2_s=(NCHUNK, 3),
    rs2_r=(NCHUNK, 3),
    cg_s=(8,),
    cg_r=(8,),
)


def body(t_in, s_in, p_in, gp_out, gs_out, loss_out, *scratch):
    m = types.SimpleNamespace(**dict(zip(list(SCRATCH) + list(SEMS), scratch)))
    bi, pi = lax.axis_index("batch"), lax.axis_index("proto")
    yi, xi = bi // SIDE, bi % SIDE
    zi, ci = pi // 2, pi % 2
    started = []

    def batch_dev(y, x):
        return (y * SIDE + x, pi)

    def proto_dev(p):
        return (bi, p)

    def batch_peer(step, sign):
        return (yi + SIDE + sign * step[0]) % SIDE * SIDE + (xi + SIDE + sign * step[1]) % SIDE

    def proto_peer(step, sign):
        return (zi + 8 + sign * step[0]) % 8 * 2 + (ci + step[1]) % 2

    def rdma(src, dst, ssem, rsem, dev):
        return pltpu.make_async_remote_copy(
            src_ref=src, dst_ref=dst, send_sem=ssem, recv_sem=rsem, device_id=dev, device_id_type=MESH
        )

    def send(src, dst, ssem, rsem, dev):
        copy = rdma(src, dst, ssem, rsem, dev)
        copy.start()
        started.append(copy)

    def drain(count):
        for copy in started[:count]:
            copy.wait_send()
        del started[:count]

    def arrived(dst, ssem, rsem, dev):
        rdma(dst, dst, ssem, rsem, dev).wait_recv()

    barrier = pltpu.get_barrier_semaphore()
    peers = []
    for step in PROTO_STEPS:
        peers.append(proto_dev(proto_peer(step, 1)))
    for step in BATCH_STEPS:
        peers.append((batch_peer(step, 1), pi))
    for peer in peers:
        pl.semaphore_signal(barrier, inc=1, device_id=peer, device_id_type=MESH)
    pl.semaphore_wait(barrier, len(peers))

    def where(h, c1, c2):
        c1, c2 = (c1 + SIDE) % SIDE, (c2 + SIDE) % SIDE
        return (c2, c1) if h == 0 else (c1, c2)

    pos = ((xi, yi), (yi, xi))

    def row0(y, x):
        return pl.multiple_of((y * SIDE + x) * BLK, BLK)

    def piece(k, y, x):
        return m.praw.at[pl.ds(row0(y, x), BLK), pl.ds(k * QUART, QUART)]

    def half_piece(k, y, x, half):
        return m.praw.at[pl.ds(row0(y, x), BLK), pl.ds(k * QUART + half * (QUART // 2), QUART // 2)]

    def second_steps(k):
        return (1, 3) if k in RELAYED else NEAR

    own = [
        pltpu.make_async_copy(p_in, m.praw.at[pl.ds(row0(yi, xi), BLK), :], m.own.at[0]),
        pltpu.make_async_copy(t_in, m.traw.at[pl.ds(pl.multiple_of(pi * BLK, BLK), BLK), :], m.own.at[1]),
        pltpu.make_async_copy(s_in, m.sraw.at[pl.ds(pl.multiple_of(pi * BLK, BLK), BLK), :], m.own.at[2]),
    ]

    for k in range(4):
        i1, i2 = pos[k % 2]
        for d in NEAR:
            to = batch_dev(*where(k % 2, i1 + d, i2))
            send(p_in.at[:, pl.ds(k * QUART, QUART)], piece(k, yi, xi), m.ag1_s.at[k, d - 1], m.ag1_r.at[k, d - 1], to)
    for k in range(4):
        i1, i2 = pos[k % 2]
        for d in second_steps(k):
            to = batch_dev(*where(k % 2, i1, i2 + d))
            send(p_in.at[:, pl.ds(k * QUART, QUART)], piece(k, yi, xi), m.ag2_s.at[k, 0, d - 1], m.ag2_r.at[k, 0, d - 1], to)

    def ts_rows(ref, p):
        return ref.at[pl.ds(pl.multiple_of(p * BLK, BLK), BLK), :]

    sibling = zi * 2 + 1 - ci
    embeddings = ((t_in, m.traw), (s_in, m.sraw))
    for a, (src, ref) in enumerate(embeddings):
        for d in (4, 3, 5, 2, 6, 1, 7):
            peer = ((zi + d) % 8) * 2 + ci
            send(src, ts_rows(ref, pi), m.ts_s.at[a, d - 1], m.ts_r.at[a, d - 1], proto_dev(peer))
        send(src, ts_rows(ref, pi), m.ts_s.at[a, 7], m.ts_r.at[a, 7], proto_dev(sibling))
    for copy in own:
        copy.start()

    for k in range(4):
        h = k % 2
        i1, i2 = pos[h]
        for d in (1, 3, 2):
            y, x = where(h, i1 - d, i2)
            block = piece(k, y, x)
            arrived(block, m.ag1_s.at[k, d - 1], m.ag1_r.at[k, d - 1], batch_dev(y, x))
            for d2 in second_steps(k):
                send(block, block, m.ag2_s.at[k, d, d2 - 1], m.ag2_r.at[k, d, d2 - 1], batch_dev(*where(h, i1, i2 + d2)))

    def ts_forward(a):
        ref = embeddings[a][1]
        for d in (1, 7, 2, 6, 3, 5, 4):
            peer = ((zi + 8 - d) % 8) * 2 + ci
            rows = ts_rows(ref, peer)
            arrived(rows, m.ts_s.at[a, d - 1], m.ts_r.at[a, d - 1], proto_dev(peer))
            send(rows, rows, m.ts_s.at[a, 7 + d], m.ts_r.at[a, 7 + d], proto_dev(sibling))

    def ts_finish(a):
        ref = embeddings[a][1]
        own[1 + a].wait()
        arrived(ts_rows(ref, sibling), m.ts_s.at[a, 7], m.ts_r.at[a, 7], proto_dev(sibling))
        for d in range(1, 8):
            rows = ts_rows(ref, ((zi + 8 - d) % 8) * 2 + 1 - ci)
            arrived(rows, m.ts_s.at[a, 7 + d], m.ts_r.at[a, 7 + d], proto_dev(sibling))

    ts_forward(0)
    for k in RELAYED:
        h = k % 2
        i1, i2 = pos[h]
        for r in (0, 1, 3, 2):
            for half, d in enumerate((1, 3)):
                y, x = where(h, i1 - r, i2 - d)
                block = piece(k, y, x)
                arrived(block, m.ag2_s.at[k, r, d - 1], m.ag2_r.at[k, r, d - 1], batch_dev(y, x))
                block = half_piece(k, y, x, half)
                slot = 1 + 2 * half
                send(block, block, m.ag2_s.at[k, r, slot], m.ag2_r.at[k, r, slot], batch_dev(*where(h, i1, i2 + d)))
    ts_forward(1)

    def unit(values):
        values = values.astype(F32)
        factor = lax.rsqrt(jnp.sum(values * values, axis=0, keepdims=True) + EPS)
        return values * factor, factor

    ts_finish(0)
    teacher, unused = unit(m.traw[...])
    m.tt[...] = jnp.transpose(teacher).astype(BF16)
    ts_finish(1)
    student, factor = unit(m.sraw[...])
    m.sscale[...] = factor
    m.su[...] = student.astype(BF16)
    m.st[...] = jnp.transpose(student).astype(BF16)
    own[0].wait()

    def cols_of(j):
        return pl.ds(j * CHUNK if isinstance(j, int) else pl.multiple_of(j * CHUNK, CHUNK), CHUNK)

    def teacher_chunk(j, carry):
        cols = cols_of(j)
        proto, factor = unit(m.praw[:, cols])
        proto = proto.astype(BF16)
        m.pu[:, cols] = proto
        m.pscale[:, cols] = factor
        c = jnp.dot(m.tt[...], proto, preferred_element_type=F32)
        e = jnp.exp2(c * (LOG2E / TEACHER_TEMP))
        m.expo[:, cols] = e
        m.colacc[:, cols] = jnp.sum(e.reshape(ROWS // 8, 8, CHUNK), axis=0)
        return carry

    def to_message(ref):
        for j in range(NCHUNK):
            ref[j : j + 1, pl.ds(0, CHUNK)] = jnp.sum(m.colacc[:, j * CHUNK : (j + 1) * CHUNK], axis=0, keepdims=True)

    for k in range(4):
        h = k % 2
        i1, i2 = pos[h]
        for r in range(4):
            if k in RELAYED:
                y, x = where(h, i1 - r, i2 - 2)
                for half in range(2):
                    slot = 1 + 2 * half
                    arrived(half_piece(k, y, x, half), m.ag2_s.at[k, r, slot], m.ag2_r.at[k, r, slot], batch_dev(y, x))
                continue
            for d in (1, 3, 2):
                y, x = where(h, i1 - r, i2 - d)
                arrived(piece(k, y, x), m.ag2_s.at[k, r, d - 1], m.ag2_r.at[k, r, d - 1], batch_dev(y, x))
        lax.fori_loop(2 * k, 2 * k + 2, teacher_chunk, 0)
    to_message(m.cx.at[0, bi])

    def all_send(buf, ss, rs):
        for n, step in enumerate(BATCH_STEPS):
            send(buf.at[bi], buf.at[bi], ss.at[n], rs.at[n], (batch_peer(step, 1), pi))

    def all_sum(buf, ss, rs):
        for n, step in reversed(list(enumerate(BATCH_STEPS))):
            frm = batch_peer(step, -1)
            arrived(buf.at[frm], ss.at[n], rs.at[n], (frm, pi))
        return jnp.sum(buf[...], axis=0)

    def message(e):
        return m.cx.at[e] if e == 1 else m.cx.at[e, :, :, pl.ds(0, CHUNK)]

    def col_start(e):
        all_send(message(e), m.cx_s.at[e], m.cx_r.at[e])

    def col_finish(e):
        return all_sum(message(e), m.cx_s.at[e], m.cx_r.at[e])

    def ring_send(buf, me, dev, ss, rs):
        for d in NEAR:
            send(buf.at[me], buf.at[me], ss.at[d - 1], rs.at[d - 1], dev((me + d) % SIDE))

    def ring_sum(buf, me, dev, ss, rs):
        for d in range(1, SIDE):
            frm = (me + SIDE - d) % SIDE
            arrived(buf.at[frm], ss.at[d - 1], rs.at[d - 1], dev(frm))
        return (buf[0] + buf[1]) + (buf[2] + buf[3])

    def along_x(x):
        return batch_dev(yi, x)

    def along_y(y):
        return batch_dev(y, xi)

    def row_start(e):
        for n, step in enumerate(PROTO_STEPS):
            send(m.rx.at[e, pi], m.rx.at[e, pi], m.rx_s.at[e, n], m.rx_r.at[e, n], proto_dev(proto_peer(step, 1)))

    def row_finish(e):
        for n, step in reversed(list(enumerate(PROTO_STEPS))):
            frm = proto_peer(step, -1)
            arrived(m.rx.at[e, frm], m.rx_s.at[e, n], m.rx_r.at[e, n], proto_dev(frm))
        return jnp.sum(m.rx[e], axis=0)

    def to_rows(acc_ref, e, first):
        for q in range(4):
            block = jnp.transpose(acc_ref[q * 128 : (q + 1) * 128, :])
            m.rx[e, pi, pl.ds(first + q, 1), :] = jnp.sum(block, axis=0, keepdims=True)

    def to_columns(ref, rows):
        for q in range(4):
            ref[q * 128 : (q + 1) * 128, :] = jnp.transpose(jnp.broadcast_to(rows[q : q + 1], (128, 128)))

    col_start(0)

    m.rowacc[...] = jnp.zeros_like(m.rowacc)
    m.smax[...] = jnp.zeros_like(m.smax)

    def student_chunk(j, carry):
        cols = cols_of(j)
        c = jnp.dot(m.st[...], m.pu[:, cols], preferred_element_type=F32)
        m.cos[:, cols] = c
        e = jnp.exp2(c * (LOG2E / STUDENT_TEMP))
        m.smax[...] = jnp.maximum(m.smax[...], jnp.sum(e.reshape(ROWS // 8, 8, CHUNK), axis=0))
        m.rowacc[...] += (e[:, 0:128] + e[:, 128:256]) + (e[:, 256:384] + e[:, 384:512])
        return carry

    lax.fori_loop(0, NCHUNK, student_chunk, 0)
    to_rows(m.rowacc, 0, 4)
    drain(len(started) - 15)

    def row_pass(e):
        def step(r, carry):
            rows = pl.ds(pl.multiple_of(r * 64, 64), 64)
            acc = jnp.zeros((8, 8, 128), F32)
            for q in range(COLS // 128):
                cols = slice(q * 128, (q + 1) * 128)
                acc = acc + m.expo[rows, cols].reshape(8, 8, 128) * m.pinv[:, cols]
            m.rowacc[rows, :] = acc.reshape(64, 128)
            return carry

        lax.fori_loop(0, ROWS // 64, step, 0)
        to_rows(m.rowacc, e, 0)

    def col_pass(e):
        m.colacc[...] = jnp.zeros_like(m.colacc)

        def step(r, carry):
            rows = pl.ds(pl.multiple_of(r * 64, 64), 64)
            weights = m.csb[rows, :]
            for q in range(COLS // 128):
                cols = slice(q * 128, (q + 1) * 128)
                m.colacc[:, cols] += jnp.sum((m.expo[rows, cols] * weights).reshape(8, 8, 128), axis=0)
            return carry

        lax.fori_loop(0, ROWS // 64, step, 0)
        to_message(m.cx.at[e, bi])

    log_total = None
    for e in range(3):
        if e:
            col_pass(e)
            col_start(e)
            drain(len(started) - 15)
        sums = col_finish(e)
        total = sums[:, :CHUNK]
        if e == 1:
            mass = sums[0:2, CHUNK:]
        if e == 2:
            growth = jnp.max(total * inverse)
        inverse = 1.0 / total
        for j in range(NCHUNK):
            m.pinv[:, j * CHUNK : (j + 1) * CHUNK] = jnp.broadcast_to(inverse[j : j + 1], (8, CHUNK))
        if e == 1:
            m.rx[1, pi, 4:8, :] = jnp.zeros((4, 128), F32)
        if e == 2:
            m.rx[2, pi, 4:6, :] = jnp.zeros((2, 128), F32) + growth
            m.rx[2, pi, 6:8, :] = mass
        row_pass(e)
        row_start(e)
        drain(len(started) - 15)
        rows = row_finish(e)
        to_columns(m.csb, 1.0 / rows[0:4])
        if e == 0:
            to_columns(m.itot, 1.0 / rows[4:8])
            log_total = jnp.sum(jnp.log(rows[4:8]), axis=0, keepdims=True)
            bound = jnp.max(jnp.sum(m.smax[...], axis=0, keepdims=True)) * jnp.max(1.0 / rows[4:8])
            m.cx[1, bi, :, pl.ds(CHUNK, 128)] = jnp.zeros((NCHUNK, 128), F32) + bound

    bound = (jnp.max(m.rx[2][:, 4:6, :]) + jnp.max(m.rx[2][:, 6:8, :])) * (1.05 / (CROPS * STUDENT_TEMP))
    wire_scale, wire_unscale = WIRE_TOP / bound, bound * (1.0 / WIRE_TOP)

    def encode(values, scale):
        values = values * scale
        square = values * values
        e8 = square * square
        return (values * (e8 * e8)).astype(BF16)

    def decode(coded, unscale):
        coded = coded.astype(F32)
        root = jnp.exp2(jnp.log(jnp.maximum(jnp.abs(coded), 1e-37)) * (-8.0 / 9.0 * LOG2E))
        return (coded * root) * unscale

    m.tlacc[...] = jnp.zeros_like(m.tlacc)
    m.cg[...] = jnp.zeros_like(m.cg)

    def grad_chunk(j, carry):
        cols = cols_of(j)

        def rows_step(r, inner):
            rows = pl.ds(pl.multiple_of(r * 64, 64), 64)
            weights, inv = m.csb[rows, :], m.itot[rows, :]
            tl = jnp.zeros((64, 128), F32)
            for i in range(4):
                sub = pl.ds(j * CHUNK + i * 128, 128)
                target = (m.expo[rows, sub].reshape(8, 8, 128) * m.pinv[:, sub]).reshape(64, 128) * weights
                c = m.cos[rows, sub]
                prob = jnp.exp2(c * (LOG2E / STUDENT_TEMP)) * inv
                tl = tl + target * c
                m.gl[rows, i * 128 : (i + 1) * 128] = ((prob - target) * (1.0 / (CROPS * STUDENT_TEMP))).astype(BF16)
            m.tlacc[...] += jnp.sum(tl.reshape(8, 8, 128), axis=0)
            return inner

        lax.fori_loop(0, ROWS // 64, rows_step, 0)
        g = m.gl[...]
        proto = m.pu[:, cols]
        part = jnp.dot(m.su[...], g, preferred_element_type=F32)
        m.gp[:, cols] = part
        m.cg[...] += lax.dot_general(proto, g, (((1,), (1,)), ((), ())), preferred_element_type=F32)
        m.colacc[:, cols] = jnp.sum((proto.astype(F32) * part).reshape(K // 8, 8, CHUNK), axis=0)
        return carry

    def first_rows(h, c, cols):
        c = (c + SIDE) % SIDE
        blocks = []
        for u in range(SIDE):
            y, x = (c, u) if h else (u, c)
            blocks.append(m.gp[pl.ds(row0(y, x), BLK), cols])
        return jnp.concatenate(blocks, axis=0)

    def second_rows(j, c):
        return m.t1[j, pl.ds(pl.multiple_of(((c + SIDE) % SIDE) * BLK, BLK), BLK), :]

    def first_send(j):
        h = j % 2
        i1, i2 = pos[h]
        for d in NEAR:
            m.s1[j, d - 1] = encode(first_rows(h, i1 + d, slice(j * CHUNK, (j + 1) * CHUNK)), wire_scale)
            to = batch_dev(*where(h, i1 + d, i2))
            send(m.s1.at[j, d - 1], m.r1.at[j, d - 1], m.rs1_s.at[j, d - 1], m.rs1_r.at[j, d - 1], to)

    def second_send(j):
        h = j % 2
        i1, i2 = pos[h]
        total = first_rows(h, i1, slice(j * CHUNK, (j + 1) * CHUNK))
        for d in range(1, SIDE):
            arrived(m.r1.at[j, d - 1], m.rs1_s.at[j, d - 1], m.rs1_r.at[j, d - 1], batch_dev(*where(h, i1 - d, i2)))
            total = total + decode(m.r1[j, d - 1], wire_unscale)
        m.t1[j] = total
        for d in NEAR:
            m.s2[j, d - 1] = encode(second_rows(j, i2 + d), wire_scale)
            to = batch_dev(*where(h, i1, i2 + d))
            send(m.s2.at[j, d - 1], m.r2.at[j, d - 1], m.rs2_s.at[j, d - 1], m.rs2_r.at[j, d - 1], to)

    def reduced(j):
        h = j % 2
        i1, i2 = pos[h]
        total = second_rows(j, i2)
        for d in range(1, SIDE):
            arrived(m.r2.at[j, d - 1], m.rs2_s.at[j, d - 1], m.rs2_r.at[j, d - 1], batch_dev(*where(h, i1, i2 - d)))
            total = total + decode(m.r2[j, d - 1], wire_unscale)
        return total

    for j in range(NCHUNK):
        grad_chunk(j, 0)
        first_send(j)
        if j >= LAG:
            second_send(j - LAG)
    for p in range(NP):
        m.cgb[p % 2, p // 2] = m.cg[p * BLK : (p + 1) * BLK, :]
    send(m.cgb.at[1 - ci], m.cgr, m.cg_s.at[7], m.cg_r.at[7], proto_dev(sibling))
    dot_rows = jnp.sum(m.su[...].astype(F32) * m.cg[...], axis=0, keepdims=True)
    for q in range(4):
        m.rx[3, pi, q : q + 1, :] = dot_rows[:, q * 128 : (q + 1) * 128]
    m.rx[3, pi, 4:8, :] = jnp.zeros((4, 128), F32)
    m.rx[3, pi, 4:5, :] = jnp.sum(m.tlacc[...], axis=0, keepdims=True)
    row_start(3)
    to_message(m.dx.at[xi])
    ring_send(m.dx, xi, along_x, m.d_s.at[0], m.d_r.at[0])

    arrived(m.cgr, m.cg_s.at[7], m.cg_r.at[7], proto_dev(sibling))
    m.cgm[...] = m.cgb[ci] + m.cgr[...]
    m.cgs[...] = encode(m.cgm[...], CROP_SCALE)
    for d in range(1, 8):
        to = (zi + d) % 8
        send(m.cgs.at[to], m.cgz.at[zi], m.cg_s.at[d - 1], m.cg_r.at[d - 1], proto_dev(to * 2 + ci))

    second_send(NCHUNK - LAG)
    m.dy[yi] = ring_sum(m.dx, xi, along_x, m.d_s.at[0], m.d_r.at[0])
    ring_send(m.dy, yi, along_y, m.d_s.at[1], m.d_r.at[1])
    second_send(NCHUNK - LAG + 1)

    rows = row_finish(3)
    loss_rows = rows[4:5] * (1.0 / STUDENT_TEMP) - log_total
    m.lx[bi] = jnp.broadcast_to(loss_rows, (8, 128))
    all_send(m.lx, m.l_s, m.l_r)
    for j in range(NCHUNK - LAG + 2, NCHUNK):
        second_send(j)
    drain(len(started) - 12)
    dots = ring_sum(m.dy, yi, along_y, m.d_s.at[1], m.d_r.at[1])

    loss_out[0, 0] = jnp.sum(all_sum(m.lx, m.l_s, m.l_r)[0:1]) * (-1.0 / CROPS)
    crop_part = m.cgm[zi]
    for d in range(1, 8):
        frm = (zi + 8 - d) % 8
        arrived(m.cgz.at[frm], m.cg_s.at[d - 1], m.cg_r.at[d - 1], proto_dev(frm * 2 + ci))
        crop_part = crop_part + decode(m.cgz[frm], 1.0 / CROP_SCALE)
    student_own = m.su[pl.ds(pl.multiple_of(pi * BLK, BLK), BLK), :].astype(F32)
    for q in range(4):
        cols = slice(q * 128, (q + 1) * 128)
        gs_out[:, cols] = (crop_part[:, cols] - student_own[:, cols] * rows[q : q + 1]) * m.sscale[:, cols]

    proto_rows = pl.ds(row0(yi, xi), BLK)
    for j in range(NCHUNK):
        cols = slice(j * CHUNK, (j + 1) * CHUNK)
        proto_own = m.pu[proto_rows, cols].astype(F32)
        gp_out[:, cols] = (reduced(j) - proto_own * dots[j : j + 1]) * m.pscale[:, cols]

    drain(len(started))


def shards(teacher_emb, student_emb, prototypes):
    hbm = pl.BlockSpec(memory_space=pl.ANY)
    vmem = pl.BlockSpec(memory_space=pltpu.VMEM)
    grad_proto, grad_student, loss = pl.pallas_call(
        body,
        out_shape=(
            pltpu.VMEM((BLK, COLS), F32),
            pltpu.VMEM((BLK, ROWS), F32),
            jax.ShapeDtypeStruct((1, 1), F32),
        ),
        in_specs=[hbm] * 3,
        out_specs=(vmem, vmem, pl.BlockSpec(memory_space=pltpu.SMEM)),
        scratch_shapes=[pltpu.VMEM(shape, dtype) for shape, dtype in SCRATCH.values()]
        + [pltpu.SemaphoreType.DMA(shape) for shape in SEMS.values()],
        compiler_params=pltpu.CompilerParams(
            collective_id=0, has_side_effects=True, vmem_limit_bytes=58 * 1024 * 1024
        ),
    )(teacher_emb, student_emb, prototypes)
    return grad_proto, grad_student, loss.reshape(())


def solution(mesh):
    in_specs = (P("proto", "batch"), P("proto", "batch"), P("batch", "proto"))
    out_specs = (P("batch", "proto"), P("proto", "batch"), P())
    return jax.shard_map(shards, mesh=mesh, in_specs=in_specs, out_specs=out_specs, check_vma=False)
```

```python
import types

import jax
import jax.numpy as jnp
from jax import lax
from jax.experimental import pallas as pl
from jax.experimental.pallas import tpu as pltpu
from jax.sharding import PartitionSpec as P

F32, BF16 = jnp.float32, jnp.bfloat16
MESH = pl.DeviceIdType.MESH
LOG2E = 1.4426950408889634
TEACHER_TEMP, STUDENT_TEMP, EPS = 0.07, 0.1, 1e-6
K, ROWS, COLS = 256, 512, 4096
CHUNK = 512
NCHUNK = COLS // CHUNK
SIDE = 4
NP = 16
BLK = K // 16
QUART = COLS // 4
NEAR = (2, 1, 3)
LAG = 5
RELAYED = (0, 1, 2)
CROPS = ROWS * SIDE * SIDE
WIRE_TOP = 8192.0
CROP_SCALE = WIRE_TOP * (CROPS * STUDENT_TEMP) / 2.1
MSGW = CHUNK + 128


def hops(step, size):
    return min(step, size - step)


BATCH_STEPS = sorted(
    ((dy, dx) for dy in range(SIDE) for dx in range(SIDE) if dy or dx), key=lambda s: -hops(s[0], SIDE) - hops(s[1], SIDE)
)
PROTO_STEPS = sorted(((dz, dc) for dz in range(8) for dc in range(2) if dz or dc), key=lambda s: -2 * hops(s[0], 8) - s[1])

SCRATCH = dict(
    praw=((K, COLS), BF16),
    traw=((K, ROWS), BF16),
    sraw=((K, ROWS), BF16),
    tt=((ROWS, K), BF16),
    st=((ROWS, K), BF16),
    su=((K, ROWS), BF16),
    pu=((K, COLS), BF16),
    pscale=((1, COLS), F32),
    sscale=((1, ROWS), F32),
    expo=((ROWS, COLS), F32),
    cos=((ROWS, COLS), F32),
    rowacc=((ROWS, 128), F32),
    colacc=((8, COLS), F32),
    pinv=((8, COLS), F32),
    csb=((ROWS, 128), F32),
    itot=((ROWS, 128), F32),
    tlacc=((8, 128), F32),
    gl=((ROWS, CHUNK), BF16),
    gp=((K, COLS), F32),
    cg=((K, ROWS), F32),
    cgb=((2, 8, BLK, ROWS), F32),
    cgr=((8, BLK, ROWS), F32),
    cgz=((8, BLK, ROWS), BF16),
    cgs=((8, BLK, ROWS), BF16),
    cgm=((8, BLK, ROWS), F32),
    cx=((3, SIDE * SIDE, NCHUNK, MSGW), F32),
    dx=((SIDE, NCHUNK, CHUNK), F32),
    dy=((SIDE, NCHUNK, CHUNK), F32),
    rx=((4, NP, 8, 128), F32),
    lx=((SIDE * SIDE, 8, 128), F32),
    s1=((NCHUNK, 3, SIDE * BLK, CHUNK), BF16),
    r1=((NCHUNK, 3, SIDE * BLK, CHUNK), BF16),
    t1=((NCHUNK, SIDE * BLK, CHUNK), F32),
    s2=((NCHUNK, 3, BLK, CHUNK), BF16),
    r2=((NCHUNK, 3, BLK, CHUNK), BF16),
    smax=((8, CHUNK), F32),
)
SEMS = dict(
    own=(3,),
    ag1_s=(4, 3),
    ag1_r=(4, 3),
    ag2_s=(4, 4, 4),
    ag2_r=(4, 4, 4),
    ts_s=(2, 16),
    ts_r=(2, 16),
    cx_s=(3, 15),
    cx_r=(3, 15),
    d_s=(2, 3),
    d_r=(2, 3),
    rx_s=(4, 15),
    rx_r=(4, 15),
    l_s=(15,),
    l_r=(15,),
    rs1_s=(NCHUNK, 3),
    rs1_r=(NCHUNK, 3),
    rs2_s=(NCHUNK, 3),
    rs2_r=(NCHUNK, 3),
    cg_s=(8,),
    cg_r=(8,),
)


def body(t_in, s_in, p_in, gp_out, gs_out, loss_out, *scratch):
    m = types.SimpleNamespace(**dict(zip(list(SCRATCH) + list(SEMS), scratch)))
    bi, pi = lax.axis_index("batch"), lax.axis_index("proto")
    yi, xi = bi // SIDE, bi % SIDE
    zi, ci = pi // 2, pi % 2
    started = []

    def batch_dev(y, x):
        return (y * SIDE + x, pi)

    def proto_dev(p):
        return (bi, p)

    def batch_peer(step, sign):
        return (yi + SIDE + sign * step[0]) % SIDE * SIDE + (xi + SIDE + sign * step[1]) % SIDE

    def proto_peer(step, sign):
        return (zi + 8 + sign * step[0]) % 8 * 2 + (ci + step[1]) % 2

    def rdma(src, dst, ssem, rsem, dev):
        return pltpu.make_async_remote_copy(
            src_ref=src, dst_ref=dst, send_sem=ssem, recv_sem=rsem, device_id=dev, device_id_type=MESH
        )

    def send(src, dst, ssem, rsem, dev):
        copy = rdma(src, dst, ssem, rsem, dev)
        copy.start()
        started.append(copy)

    def drain(count):
        for copy in started[:count]:
            copy.wait_send()
        del started[:count]

    def arrived(dst, ssem, rsem, dev):
        rdma(dst, dst, ssem, rsem, dev).wait_recv()

    barrier = pltpu.get_barrier_semaphore()
    peers = []
    for step in PROTO_STEPS:
        if step[1] == 0 or step[0] == 0:
            peers.append(proto_dev(proto_peer(step, 1)))
    for step in BATCH_STEPS:
        if step[0] == 0 or step[1] == 0:
            peers.append((batch_peer(step, 1), pi))
    for peer in peers:
        pl.semaphore_signal(barrier, inc=1, device_id=peer, device_id_type=MESH)
    pl.semaphore_wait(barrier, len(peers))

    def where(h, c1, c2):
        c1, c2 = (c1 + SIDE) % SIDE, (c2 + SIDE) % SIDE
        return (c2, c1) if h == 0 else (c1, c2)

    pos = ((xi, yi), (yi, xi))

    def row0(y, x):
        return pl.multiple_of((y * SIDE + x) * BLK, BLK)

    def piece(k, y, x):
        return m.praw.at[pl.ds(row0(y, x), BLK), pl.ds(k * QUART, QUART)]

    def half_piece(k, y, x, half):
        return m.praw.at[pl.ds(row0(y, x), BLK), pl.ds(k * QUART + half * (QUART // 2), QUART // 2)]

    def second_steps(k):
        return (1, 3) if k in RELAYED else NEAR

    own = [
        pltpu.make_async_copy(p_in, m.praw.at[pl.ds(row0(yi, xi), BLK), :], m.own.at[0]),
        pltpu.make_async_copy(t_in, m.traw.at[pl.ds(pl.multiple_of(pi * BLK, BLK), BLK), :], m.own.at[1]),
        pltpu.make_async_copy(s_in, m.sraw.at[pl.ds(pl.multiple_of(pi * BLK, BLK), BLK), :], m.own.at[2]),
    ]

    for k in range(4):
        i1, i2 = pos[k % 2]
        for d in NEAR:
            to = batch_dev(*where(k % 2, i1 + d, i2))
            send(p_in.at[:, pl.ds(k * QUART, QUART)], piece(k, yi, xi), m.ag1_s.at[k, d - 1], m.ag1_r.at[k, d - 1], to)
    for k in range(4):
        i1, i2 = pos[k % 2]
        for d in second_steps(k):
            to = batch_dev(*where(k % 2, i1, i2 + d))
            send(p_in.at[:, pl.ds(k * QUART, QUART)], piece(k, yi, xi), m.ag2_s.at[k, 0, d - 1], m.ag2_r.at[k, 0, d - 1], to)

    def ts_rows(ref, p):
        return ref.at[pl.ds(pl.multiple_of(p * BLK, BLK), BLK), :]

    sibling = zi * 2 + 1 - ci
    embeddings = ((t_in, m.traw), (s_in, m.sraw))
    for a, (src, ref) in enumerate(embeddings):
        for d in (4, 3, 5, 2, 6, 1, 7):
            peer = ((zi + d) % 8) * 2 + ci
            send(src, ts_rows(ref, pi), m.ts_s.at[a, d - 1], m.ts_r.at[a, d - 1], proto_dev(peer))
        send(src, ts_rows(ref, pi), m.ts_s.at[a, 7], m.ts_r.at[a, 7], proto_dev(sibling))
    for copy in own:
        copy.start()

    for k in range(4):
        h = k % 2
        i1, i2 = pos[h]
        for d in (1, 3, 2):
            y, x = where(h, i1 - d, i2)
            block = piece(k, y, x)
            arrived(block, m.ag1_s.at[k, d - 1], m.ag1_r.at[k, d - 1], batch_dev(y, x))
            for d2 in second_steps(k):
                send(block, block, m.ag2_s.at[k, d, d2 - 1], m.ag2_r.at[k, d, d2 - 1], batch_dev(*where(h, i1, i2 + d2)))

    def ts_forward(a):
        ref = embeddings[a][1]
        for d in (1, 7, 2, 6, 3, 5, 4):
            peer = ((zi + 8 - d) % 8) * 2 + ci
            rows = ts_rows(ref, peer)
            arrived(rows, m.ts_s.at[a, d - 1], m.ts_r.at[a, d - 1], proto_dev(peer))
            send(rows, rows, m.ts_s.at[a, 7 + d], m.ts_r.at[a, 7 + d], proto_dev(sibling))

    def ts_finish(a):
        ref = embeddings[a][1]
        own[1 + a].wait()
        arrived(ts_rows(ref, sibling), m.ts_s.at[a, 7], m.ts_r.at[a, 7], proto_dev(sibling))
        for d in range(1, 8):
            rows = ts_rows(ref, ((zi + 8 - d) % 8) * 2 + 1 - ci)
            arrived(rows, m.ts_s.at[a, 7 + d], m.ts_r.at[a, 7 + d], proto_dev(sibling))

    ts_forward(0)
    for k in RELAYED:
        h = k % 2
        i1, i2 = pos[h]
        for r in (0, 1, 3, 2):
            for half, d in enumerate((1, 3)):
                y, x = where(h, i1 - r, i2 - d)
                block = piece(k, y, x)
                arrived(block, m.ag2_s.at[k, r, d - 1], m.ag2_r.at[k, r, d - 1], batch_dev(y, x))
                block = half_piece(k, y, x, half)
                slot = 1 + 2 * half
                send(block, block, m.ag2_s.at[k, r, slot], m.ag2_r.at[k, r, slot], batch_dev(*where(h, i1, i2 + d)))
    ts_forward(1)

    def unit(values):
        values = values.astype(F32)
        factor = lax.rsqrt(jnp.sum(values * values, axis=0, keepdims=True) + EPS)
        return values * factor, factor

    ts_finish(0)
    teacher, unused = unit(m.traw[...])
    m.tt[...] = jnp.transpose(teacher).astype(BF16)
    ts_finish(1)
    student, factor = unit(m.sraw[...])
    m.sscale[...] = factor
    m.su[...] = student.astype(BF16)
    m.st[...] = jnp.transpose(student).astype(BF16)
    own[0].wait()

    def cols_of(j):
        return pl.ds(j * CHUNK if isinstance(j, int) else pl.multiple_of(j * CHUNK, CHUNK), CHUNK)

    def teacher_chunk(j, carry):
        cols = cols_of(j)
        proto, factor = unit(m.praw[:, cols])
        proto = proto.astype(BF16)
        m.pu[:, cols] = proto
        m.pscale[:, cols] = factor
        c = jnp.dot(m.tt[...], proto, preferred_element_type=F32)
        e = jnp.exp2(c * (LOG2E / TEACHER_TEMP))
        m.expo[:, cols] = e
        m.colacc[:, cols] = jnp.sum(e.reshape(ROWS // 8, 8, CHUNK), axis=0)
        return carry

    def to_message(ref):
        for j in range(NCHUNK):
            ref[j : j + 1, pl.ds(0, CHUNK)] = jnp.sum(m.colacc[:, j * CHUNK : (j + 1) * CHUNK], axis=0, keepdims=True)

    for k in range(4):
        h = k % 2
        i1, i2 = pos[h]
        for r in range(4):
            if k in RELAYED:
                y, x = where(h, i1 - r, i2 - 2)
                for half in range(2):
                    slot = 1 + 2 * half
                    arrived(half_piece(k, y, x, half), m.ag2_s.at[k, r, slot], m.ag2_r.at[k, r, slot], batch_dev(y, x))
                continue
            for d in (1, 3, 2):
                y, x = where(h, i1 - r, i2 - d)
                arrived(piece(k, y, x), m.ag2_s.at[k, r, d - 1], m.ag2_r.at[k, r, d - 1], batch_dev(y, x))
        lax.fori_loop(2 * k, 2 * k + 2, teacher_chunk, 0)
    to_message(m.cx.at[0, bi])

    def all_send(buf, ss, rs):
        for n, step in enumerate(BATCH_STEPS):
            send(buf.at[bi], buf.at[bi], ss.at[n], rs.at[n], (batch_peer(step, 1), pi))

    def all_sum(buf, ss, rs):
        for n, step in reversed(list(enumerate(BATCH_STEPS))):
            frm = batch_peer(step, -1)
            arrived(buf.at[frm], ss.at[n], rs.at[n], (frm, pi))
        return jnp.sum(buf[...], axis=0)

    def message(e):
        return m.cx.at[e] if e == 1 else m.cx.at[e, :, :, pl.ds(0, CHUNK)]

    def col_start(e):
        all_send(message(e), m.cx_s.at[e], m.cx_r.at[e])

    def col_finish(e):
        return all_sum(message(e), m.cx_s.at[e], m.cx_r.at[e])

    def ring_send(buf, me, dev, ss, rs):
        for d in NEAR:
            send(buf.at[me], buf.at[me], ss.at[d - 1], rs.at[d - 1], dev((me + d) % SIDE))

    def ring_sum(buf, me, dev, ss, rs):
        for d in range(1, SIDE):
            frm = (me + SIDE - d) % SIDE
            arrived(buf.at[frm], ss.at[d - 1], rs.at[d - 1], dev(frm))
        return (buf[0] + buf[1]) + (buf[2] + buf[3])

    def along_x(x):
        return batch_dev(yi, x)

    def along_y(y):
        return batch_dev(y, xi)

    def row_start(e):
        for n, step in enumerate(PROTO_STEPS):
            send(m.rx.at[e, pi], m.rx.at[e, pi], m.rx_s.at[e, n], m.rx_r.at[e, n], proto_dev(proto_peer(step, 1)))

    def row_finish(e):
        for n, step in reversed(list(enumerate(PROTO_STEPS))):
            frm = proto_peer(step, -1)
            arrived(m.rx.at[e, frm], m.rx_s.at[e, n], m.rx_r.at[e, n], proto_dev(frm))
        return jnp.sum(m.rx[e], axis=0)

    def to_rows(acc_ref, e, first):
        for q in range(4):
            block = jnp.transpose(acc_ref[q * 128 : (q + 1) * 128, :])
            m.rx[e, pi, pl.ds(first + q, 1), :] = jnp.sum(block, axis=0, keepdims=True)

    def to_columns(ref, rows):
        for q in range(4):
            ref[q * 128 : (q + 1) * 128, :] = jnp.transpose(jnp.broadcast_to(rows[q : q + 1], (128, 128)))

    col_start(0)

    m.rowacc[...] = jnp.zeros_like(m.rowacc)
    m.smax[...] = jnp.zeros_like(m.smax)

    def student_chunk(j, carry):
        cols = cols_of(j)
        c = jnp.dot(m.st[...], m.pu[:, cols], preferred_element_type=F32)
        m.cos[:, cols] = c
        e = jnp.exp2(c * (LOG2E / STUDENT_TEMP))
        m.smax[...] = jnp.maximum(m.smax[...], jnp.sum(e.reshape(ROWS // 8, 8, CHUNK), axis=0))
        m.rowacc[...] += (e[:, 0:128] + e[:, 128:256]) + (e[:, 256:384] + e[:, 384:512])
        return carry

    lax.fori_loop(0, NCHUNK, student_chunk, 0)
    to_rows(m.rowacc, 0, 4)
    drain(len(started) - 15)

    def row_pass(e):
        def step(r, carry):
            rows = pl.ds(pl.multiple_of(r * 64, 64), 64)
            acc = jnp.zeros((8, 8, 128), F32)
            for q in range(COLS // 128):
                cols = slice(q * 128, (q + 1) * 128)
                acc = acc + m.expo[rows, cols].reshape(8, 8, 128) * m.pinv[:, cols]
            m.rowacc[rows, :] = acc.reshape(64, 128)
            return carry

        lax.fori_loop(0, ROWS // 64, step, 0)
        to_rows(m.rowacc, e, 0)

    def col_pass(e):
        m.colacc[...] = jnp.zeros_like(m.colacc)

        def step(r, carry):
            rows = pl.ds(pl.multiple_of(r * 64, 64), 64)
            weights = m.csb[rows, :]
            for q in range(COLS // 128):
                cols = slice(q * 128, (q + 1) * 128)
                m.colacc[:, cols] += jnp.sum((m.expo[rows, cols] * weights).reshape(8, 8, 128), axis=0)
            return carry

        lax.fori_loop(0, ROWS // 64, step, 0)
        to_message(m.cx.at[e, bi])

    log_total = None
    for e in range(3):
        if e:
            col_pass(e)
            col_start(e)
            drain(len(started) - 15)
        sums = col_finish(e)
        total = sums[:, :CHUNK]
        if e == 1:
            mass = sums[0:2, CHUNK:]
        if e == 2:
            growth = jnp.max(total * inverse)
        inverse = 1.0 / total
        for j in range(NCHUNK):
            m.pinv[:, j * CHUNK : (j + 1) * CHUNK] = jnp.broadcast_to(inverse[j : j + 1], (8, CHUNK))
        if e == 1:
            m.rx[1, pi, 4:8, :] = jnp.zeros((4, 128), F32)
        if e == 2:
            m.rx[2, pi, 4:6, :] = jnp.zeros((2, 128), F32) + growth
            m.rx[2, pi, 6:8, :] = mass
        row_pass(e)
        row_start(e)
        drain(len(started) - 15)
        rows = row_finish(e)
        to_columns(m.csb, 1.0 / rows[0:4])
        if e == 0:
            to_columns(m.itot, 1.0 / rows[4:8])
            log_total = jnp.sum(jnp.log(rows[4:8]), axis=0, keepdims=True)
            bound = jnp.max(jnp.sum(m.smax[...], axis=0, keepdims=True)) * jnp.max(1.0 / rows[4:8])
            m.cx[1, bi, :, pl.ds(CHUNK, 128)] = jnp.zeros((NCHUNK, 128), F32) + bound

    bound = (jnp.max(m.rx[2][:, 4:6, :]) + jnp.max(m.rx[2][:, 6:8, :])) * (1.05 / (CROPS * STUDENT_TEMP))
    wire_scale, wire_unscale = WIRE_TOP / bound, bound * (1.0 / WIRE_TOP)

    def encode(values, scale):
        values = values * scale
        square = values * values
        e8 = square * square
        return (values * (e8 * e8)).astype(BF16)

    def decode(coded, unscale):
        coded = coded.astype(F32)
        root = jnp.exp2(jnp.log(jnp.maximum(jnp.abs(coded), 1e-37)) * (-8.0 / 9.0 * LOG2E))
        return (coded * root) * unscale

    m.tlacc[...] = jnp.zeros_like(m.tlacc)
    m.cg[...] = jnp.zeros_like(m.cg)

    def grad_chunk(j, carry):
        cols = cols_of(j)

        def rows_step(r, inner):
            rows = pl.ds(pl.multiple_of(r * 64, 64), 64)
            weights, inv = m.csb[rows, :], m.itot[rows, :]
            tl = jnp.zeros((64, 128), F32)
            for i in range(4):
                sub = pl.ds(j * CHUNK + i * 128, 128)
                target = (m.expo[rows, sub].reshape(8, 8, 128) * m.pinv[:, sub]).reshape(64, 128) * weights
                c = m.cos[rows, sub]
                prob = jnp.exp2(c * (LOG2E / STUDENT_TEMP)) * inv
                tl = tl + target * c
                m.gl[rows, i * 128 : (i + 1) * 128] = ((prob - target) * (1.0 / (CROPS * STUDENT_TEMP))).astype(BF16)
            m.tlacc[...] += jnp.sum(tl.reshape(8, 8, 128), axis=0)
            return inner

        lax.fori_loop(0, ROWS // 64, rows_step, 0)
        g = m.gl[...]
        proto = m.pu[:, cols]
        part = jnp.dot(m.su[...], g, preferred_element_type=F32)
        m.gp[:, cols] = part
        m.cg[...] += lax.dot_general(proto, g, (((1,), (1,)), ((), ())), preferred_element_type=F32)
        m.colacc[:, cols] = jnp.sum((proto.astype(F32) * part).reshape(K // 8, 8, CHUNK), axis=0)
        return carry

    def first_rows(h, c, cols):
        c = (c + SIDE) % SIDE
        blocks = []
        for u in range(SIDE):
            y, x = (c, u) if h else (u, c)
            blocks.append(m.gp[pl.ds(row0(y, x), BLK), cols])
        return jnp.concatenate(blocks, axis=0)

    def second_rows(j, c):
        return m.t1[j, pl.ds(pl.multiple_of(((c + SIDE) % SIDE) * BLK, BLK), BLK), :]

    def first_send(j):
        h = j % 2
        i1, i2 = pos[h]
        for d in NEAR:
            m.s1[j, d - 1] = encode(first_rows(h, i1 + d, slice(j * CHUNK, (j + 1) * CHUNK)), wire_scale)
            to = batch_dev(*where(h, i1 + d, i2))
            send(m.s1.at[j, d - 1], m.r1.at[j, d - 1], m.rs1_s.at[j, d - 1], m.rs1_r.at[j, d - 1], to)

    def second_send(j):
        h = j % 2
        i1, i2 = pos[h]
        total = first_rows(h, i1, slice(j * CHUNK, (j + 1) * CHUNK))
        for d in range(1, SIDE):
            arrived(m.r1.at[j, d - 1], m.rs1_s.at[j, d - 1], m.rs1_r.at[j, d - 1], batch_dev(*where(h, i1 - d, i2)))
            total = total + decode(m.r1[j, d - 1], wire_unscale)
        m.t1[j] = total
        for d in NEAR:
            m.s2[j, d - 1] = encode(second_rows(j, i2 + d), wire_scale)
            to = batch_dev(*where(h, i1, i2 + d))
            send(m.s2.at[j, d - 1], m.r2.at[j, d - 1], m.rs2_s.at[j, d - 1], m.rs2_r.at[j, d - 1], to)

    def reduced(j):
        h = j % 2
        i1, i2 = pos[h]
        total = second_rows(j, i2)
        for d in range(1, SIDE):
            arrived(m.r2.at[j, d - 1], m.rs2_s.at[j, d - 1], m.rs2_r.at[j, d - 1], batch_dev(*where(h, i1, i2 - d)))
            total = total + decode(m.r2[j, d - 1], wire_unscale)
        return total

    for j in range(NCHUNK):
        grad_chunk(j, 0)
        first_send(j)
        if j >= LAG:
            second_send(j - LAG)
    for p in range(NP):
        m.cgb[p % 2, p // 2] = m.cg[p * BLK : (p + 1) * BLK, :]
    send(m.cgb.at[1 - ci], m.cgr, m.cg_s.at[7], m.cg_r.at[7], proto_dev(sibling))
    dot_rows = jnp.sum(m.su[...].astype(F32) * m.cg[...], axis=0, keepdims=True)
    for q in range(4):
        m.rx[3, pi, q : q + 1, :] = dot_rows[:, q * 128 : (q + 1) * 128]
    m.rx[3, pi, 4:8, :] = jnp.zeros((4, 128), F32)
    m.rx[3, pi, 4:5, :] = jnp.sum(m.tlacc[...], axis=0, keepdims=True)
    row_start(3)
    to_message(m.dx.at[xi])
    ring_send(m.dx, xi, along_x, m.d_s.at[0], m.d_r.at[0])

    arrived(m.cgr, m.cg_s.at[7], m.cg_r.at[7], proto_dev(sibling))
    m.cgm[...] = m.cgb[ci] + m.cgr[...]
    m.cgs[...] = encode(m.cgm[...], CROP_SCALE)
    for d in range(1, 8):
        to = (zi + d) % 8
        send(m.cgs.at[to], m.cgz.at[zi], m.cg_s.at[d - 1], m.cg_r.at[d - 1], proto_dev(to * 2 + ci))

    second_send(NCHUNK - LAG)
    m.dy[yi] = ring_sum(m.dx, xi, along_x, m.d_s.at[0], m.d_r.at[0])
    ring_send(m.dy, yi, along_y, m.d_s.at[1], m.d_r.at[1])
    second_send(NCHUNK - LAG + 1)

    rows = row_finish(3)
    loss_rows = rows[4:5] * (1.0 / STUDENT_TEMP) - log_total
    m.lx[bi] = jnp.broadcast_to(loss_rows, (8, 128))
    all_send(m.lx, m.l_s, m.l_r)
    for j in range(NCHUNK - LAG + 2, NCHUNK):
        second_send(j)
    drain(len(started) - 12)
    dots = ring_sum(m.dy, yi, along_y, m.d_s.at[1], m.d_r.at[1])

    loss_out[0, 0] = jnp.sum(all_sum(m.lx, m.l_s, m.l_r)[0:1]) * (-1.0 / CROPS)
    crop_part = m.cgm[zi]
    for d in range(1, 8):
        frm = (zi + 8 - d) % 8
        arrived(m.cgz.at[frm], m.cg_s.at[d - 1], m.cg_r.at[d - 1], proto_dev(frm * 2 + ci))
        crop_part = crop_part + decode(m.cgz[frm], 1.0 / CROP_SCALE)
    student_own = m.su[pl.ds(pl.multiple_of(pi * BLK, BLK), BLK), :].astype(F32)
    for q in range(4):
        cols = slice(q * 128, (q + 1) * 128)
        gs_out[:, cols] = (crop_part[:, cols] - student_own[:, cols] * rows[q : q + 1]) * m.sscale[:, cols]

    proto_rows = pl.ds(row0(yi, xi), BLK)
    for j in range(NCHUNK):
        cols = slice(j * CHUNK, (j + 1) * CHUNK)
        proto_own = m.pu[proto_rows, cols].astype(F32)
        gp_out[:, cols] = (reduced(j) - proto_own * dots[j : j + 1]) * m.pscale[:, cols]

    drain(len(started))


def shards(teacher_emb, student_emb, prototypes):
    hbm = pl.BlockSpec(memory_space=pl.ANY)
    vmem = pl.BlockSpec(memory_space=pltpu.VMEM)
    grad_proto, grad_student, loss = pl.pallas_call(
        body,
        out_shape=(
            pltpu.VMEM((BLK, COLS), F32),
            pltpu.VMEM((BLK, ROWS), F32),
            jax.ShapeDtypeStruct((1, 1), F32),
        ),
        in_specs=[hbm] * 3,
        out_specs=(vmem, vmem, pl.BlockSpec(memory_space=pltpu.SMEM)),
        scratch_shapes=[pltpu.VMEM(shape, dtype) for shape, dtype in SCRATCH.values()]
        + [pltpu.SemaphoreType.DMA(shape) for shape in SEMS.values()],
        compiler_params=pltpu.CompilerParams(
            collective_id=0, has_side_effects=True, vmem_limit_bytes=58 * 1024 * 1024
        ),
    )(teacher_emb, student_emb, prototypes)
    return grad_proto, grad_student, loss.reshape(())


def solution(mesh):
    in_specs = (P("proto", "batch"), P("proto", "batch"), P("batch", "proto"))
    out_specs = (P("batch", "proto"), P("proto", "batch"), P())
    return jax.shard_map(shards, mesh=mesh, in_specs=in_specs, out_specs=out_specs, check_vma=False)
```

```python
import types

import jax
import jax.numpy as jnp
from jax import lax
from jax.experimental import pallas as pl
from jax.experimental.pallas import tpu as pltpu
from jax.sharding import PartitionSpec as P

F32, BF16 = jnp.float32, jnp.bfloat16
MESH = pl.DeviceIdType.MESH
LOG2E = 1.4426950408889634
TEACHER_TEMP, STUDENT_TEMP, EPS = 0.07, 0.1, 1e-6
K, ROWS, COLS = 256, 512, 4096
CHUNK = 512
NCHUNK = COLS // CHUNK
SIDE = 4
NP = 16
BLK = K // 16
QUART = COLS // 4
NEAR = (2, 1, 3)
LAG = 5
RELAYED = (0, 1, 2)
CROPS = ROWS * SIDE * SIDE
WIRE_TOP = 8192.0
CROP_SCALE = WIRE_TOP * (CROPS * STUDENT_TEMP) / 2.1
MSGW = CHUNK + 128


def hops(step, size):
    return min(step, size - step)


BATCH_STEPS = sorted(
    ((dy, dx) for dy in range(SIDE) for dx in range(SIDE) if dy or dx), key=lambda s: -hops(s[0], SIDE) - hops(s[1], SIDE)
)
PROTO_STEPS = sorted(((dz, dc) for dz in range(8) for dc in range(2) if dz or dc), key=lambda s: -2 * hops(s[0], 8) - s[1])

SCRATCH = dict(
    praw=((K, COLS), BF16),
    traw=((K, ROWS), BF16),
    sraw=((K, ROWS), BF16),
    tt=((ROWS, K), BF16),
    st=((ROWS, K), BF16),
    su=((K, ROWS), BF16),
    pu=((K, COLS), BF16),
    pscale=((1, COLS), F32),
    sscale=((1, ROWS), F32),
    expo=((ROWS, COLS), F32),
    cos=((ROWS, COLS), F32),
    rowacc=((ROWS, 128), F32),
    colacc=((8, COLS), F32),
    pinv=((8, COLS), F32),
    csb=((ROWS, 128), F32),
    itot=((ROWS, 128), F32),
    tlacc=((8, 128), F32),
    gl=((ROWS, CHUNK), BF16),
    gp=((K, COLS), F32),
    cg=((K, ROWS), F32),
    cgb=((2, 8, BLK, ROWS), F32),
    cgr=((8, BLK, ROWS), F32),
    cgz=((8, BLK, ROWS), BF16),
    cgs=((8, BLK, ROWS), BF16),
    cgm=((8, BLK, ROWS), F32),
    cx=((3, SIDE * SIDE, NCHUNK, MSGW), F32),
    dx=((SIDE, NCHUNK, CHUNK), F32),
    dy=((SIDE, NCHUNK, CHUNK), F32),
    rx=((4, NP, 8, 128), F32),
    lx=((SIDE * SIDE, 8, 128), F32),
    s1=((NCHUNK, 3, SIDE * BLK, CHUNK), BF16),
    r1=((NCHUNK, 3, SIDE * BLK, CHUNK), BF16),
    t1=((NCHUNK, SIDE * BLK, CHUNK), F32),
    s2=((NCHUNK, 3, BLK, CHUNK), BF16),
    r2=((NCHUNK, 3, BLK, CHUNK), BF16),
    smax=((8, CHUNK), F32),
    prob=((ROWS, COLS), F32),
)
SEMS = dict(
    own=(3,),
    ag1_s=(4, 3),
    ag1_r=(4, 3),
    ag2_s=(4, 4, 4),
    ag2_r=(4, 4, 4),
    ts_s=(2, 16),
    ts_r=(2, 16),
    cx_s=(3, 15),
    cx_r=(3, 15),
    d_s=(2, 3),
    d_r=(2, 3),
    rx_s=(4, 15),
    rx_r=(4, 15),
    l_s=(15,),
    l_r=(15,),
    rs1_s=(NCHUNK, 3),
    rs1_r=(NCHUNK, 3),
    rs2_s=(NCHUNK, 3),
    rs2_r=(NCHUNK, 3),
    cg_s=(8,),
    cg_r=(8,),
)


def body(t_in, s_in, p_in, gp_out, gs_out, loss_out, *scratch):
    m = types.SimpleNamespace(**dict(zip(list(SCRATCH) + list(SEMS), scratch)))
    bi, pi = lax.axis_index("batch"), lax.axis_index("proto")
    yi, xi = bi // SIDE, bi % SIDE
    zi, ci = pi // 2, pi % 2
    started = []

    def batch_dev(y, x):
        return (y * SIDE + x, pi)

    def proto_dev(p):
        return (bi, p)

    def batch_peer(step, sign):
        return (yi + SIDE + sign * step[0]) % SIDE * SIDE + (xi + SIDE + sign * step[1]) % SIDE

    def proto_peer(step, sign):
        return (zi + 8 + sign * step[0]) % 8 * 2 + (ci + step[1]) % 2

    def rdma(src, dst, ssem, rsem, dev):
        return pltpu.make_async_remote_copy(
            src_ref=src, dst_ref=dst, send_sem=ssem, recv_sem=rsem, device_id=dev, device_id_type=MESH
        )

    def send(src, dst, ssem, rsem, dev):
        copy = rdma(src, dst, ssem, rsem, dev)
        copy.start()
        started.append(copy)

    def drain(count):
        for copy in started[:count]:
            copy.wait_send()
        del started[:count]

    def arrived(dst, ssem, rsem, dev):
        rdma(dst, dst, ssem, rsem, dev).wait_recv()

    barrier = pltpu.get_barrier_semaphore()
    peers = []
    for step in PROTO_STEPS:
        if step[1] == 0 or step[0] == 0:
            peers.append(proto_dev(proto_peer(step, 1)))
    for step in BATCH_STEPS:
        if step[0] == 0 or step[1] == 0:
            peers.append((batch_peer(step, 1), pi))
    for peer in peers:
        pl.semaphore_signal(barrier, inc=1, device_id=peer, device_id_type=MESH)
    pl.semaphore_wait(barrier, len(peers))

    def where(h, c1, c2):
        c1, c2 = (c1 + SIDE) % SIDE, (c2 + SIDE) % SIDE
        return (c2, c1) if h == 0 else (c1, c2)

    pos = ((xi, yi), (yi, xi))

    def row0(y, x):
        return pl.multiple_of((y * SIDE + x) * BLK, BLK)

    def piece(k, y, x):
        return m.praw.at[pl.ds(row0(y, x), BLK), pl.ds(k * QUART, QUART)]

    def half_piece(k, y, x, half):
        return m.praw.at[pl.ds(row0(y, x), BLK), pl.ds(k * QUART + half * (QUART // 2), QUART // 2)]

    def second_steps(k):
        return (1, 3) if k in RELAYED else NEAR

    own = [
        pltpu.make_async_copy(p_in, m.praw.at[pl.ds(row0(yi, xi), BLK), :], m.own.at[0]),
        pltpu.make_async_copy(t_in, m.traw.at[pl.ds(pl.multiple_of(pi * BLK, BLK), BLK), :], m.own.at[1]),
        pltpu.make_async_copy(s_in, m.sraw.at[pl.ds(pl.multiple_of(pi * BLK, BLK), BLK), :], m.own.at[2]),
    ]

    for k in range(4):
        i1, i2 = pos[k % 2]
        for d in NEAR:
            to = batch_dev(*where(k % 2, i1 + d, i2))
            send(p_in.at[:, pl.ds(k * QUART, QUART)], piece(k, yi, xi), m.ag1_s.at[k, d - 1], m.ag1_r.at[k, d - 1], to)
    for k in range(4):
        i1, i2 = pos[k % 2]
        for d in second_steps(k):
            to = batch_dev(*where(k % 2, i1, i2 + d))
            send(p_in.at[:, pl.ds(k * QUART, QUART)], piece(k, yi, xi), m.ag2_s.at[k, 0, d - 1], m.ag2_r.at[k, 0, d - 1], to)

    def ts_rows(ref, p):
        return ref.at[pl.ds(pl.multiple_of(p * BLK, BLK), BLK), :]

    sibling = zi * 2 + 1 - ci
    embeddings = ((t_in, m.traw), (s_in, m.sraw))
    for a, (src, ref) in enumerate(embeddings):
        for d in (4, 3, 5, 2, 6, 1, 7):
            peer = ((zi + d) % 8) * 2 + ci
            send(src, ts_rows(ref, pi), m.ts_s.at[a, d - 1], m.ts_r.at[a, d - 1], proto_dev(peer))
        send(src, ts_rows(ref, pi), m.ts_s.at[a, 7], m.ts_r.at[a, 7], proto_dev(sibling))
    for copy in own:
        copy.start()

    for k in range(4):
        h = k % 2
        i1, i2 = pos[h]
        for d in (1, 3, 2):
            y, x = where(h, i1 - d, i2)
            block = piece(k, y, x)
            arrived(block, m.ag1_s.at[k, d - 1], m.ag1_r.at[k, d - 1], batch_dev(y, x))
            for d2 in second_steps(k):
                send(block, block, m.ag2_s.at[k, d, d2 - 1], m.ag2_r.at[k, d, d2 - 1], batch_dev(*where(h, i1, i2 + d2)))

    def ts_forward(a):
        ref = embeddings[a][1]
        for d in (1, 7, 2, 6, 3, 5, 4):
            peer = ((zi + 8 - d) % 8) * 2 + ci
            rows = ts_rows(ref, peer)
            arrived(rows, m.ts_s.at[a, d - 1], m.ts_r.at[a, d - 1], proto_dev(peer))
            send(rows, rows, m.ts_s.at[a, 7 + d], m.ts_r.at[a, 7 + d], proto_dev(sibling))

    def ts_finish(a):
        ref = embeddings[a][1]
        own[1 + a].wait()
        arrived(ts_rows(ref, sibling), m.ts_s.at[a, 7], m.ts_r.at[a, 7], proto_dev(sibling))
        for d in range(1, 8):
            rows = ts_rows(ref, ((zi + 8 - d) % 8) * 2 + 1 - ci)
            arrived(rows, m.ts_s.at[a, 7 + d], m.ts_r.at[a, 7 + d], proto_dev(sibling))

    ts_forward(0)
    for k in RELAYED:
        h = k % 2
        i1, i2 = pos[h]
        for r in (0, 1, 3, 2):
            for half, d in enumerate((1, 3)):
                y, x = where(h, i1 - r, i2 - d)
                block = piece(k, y, x)
                arrived(block, m.ag2_s.at[k, r, d - 1], m.ag2_r.at[k, r, d - 1], batch_dev(y, x))
                block = half_piece(k, y, x, half)
                slot = 1 + 2 * half
                send(block, block, m.ag2_s.at[k, r, slot], m.ag2_r.at[k, r, slot], batch_dev(*where(h, i1, i2 + d)))
    ts_forward(1)

    def unit(values):
        values = values.astype(F32)
        factor = lax.rsqrt(jnp.sum(values * values, axis=0, keepdims=True) + EPS)
        return values * factor, factor

    ts_finish(0)
    teacher, unused = unit(m.traw[...])
    m.tt[...] = jnp.transpose(teacher).astype(BF16)
    ts_finish(1)
    student, factor = unit(m.sraw[...])
    m.sscale[...] = factor
    m.su[...] = student.astype(BF16)
    m.st[...] = jnp.transpose(student).astype(BF16)
    own[0].wait()

    def cols_of(j):
        return pl.ds(j * CHUNK if isinstance(j, int) else pl.multiple_of(j * CHUNK, CHUNK), CHUNK)

    def teacher_chunk(j, carry):
        cols = cols_of(j)
        proto, factor = unit(m.praw[:, cols])
        proto = proto.astype(BF16)
        m.pu[:, cols] = proto
        m.pscale[:, cols] = factor
        c = jnp.dot(m.tt[...], proto, preferred_element_type=F32)
        e = jnp.exp2(c * (LOG2E / TEACHER_TEMP))
        m.expo[:, cols] = e
        m.colacc[:, cols] = jnp.sum(e.reshape(ROWS // 8, 8, CHUNK), axis=0)
        return carry

    def to_message(ref):
        for j in range(NCHUNK):
            ref[j : j + 1, pl.ds(0, CHUNK)] = jnp.sum(m.colacc[:, j * CHUNK : (j + 1) * CHUNK], axis=0, keepdims=True)

    for k in range(4):
        h = k % 2
        i1, i2 = pos[h]
        for r in range(4):
            if k in RELAYED:
                y, x = where(h, i1 - r, i2 - 2)
                for half in range(2):
                    slot = 1 + 2 * half
                    arrived(half_piece(k, y, x, half), m.ag2_s.at[k, r, slot], m.ag2_r.at[k, r, slot], batch_dev(y, x))
                continue
            for d in (1, 3, 2):
                y, x = where(h, i1 - r, i2 - d)
                arrived(piece(k, y, x), m.ag2_s.at[k, r, d - 1], m.ag2_r.at[k, r, d - 1], batch_dev(y, x))
        lax.fori_loop(2 * k, 2 * k + 2, teacher_chunk, 0)
    to_message(m.cx.at[0, bi])

    def all_send(buf, ss, rs):
        for n, step in enumerate(BATCH_STEPS):
            send(buf.at[bi], buf.at[bi], ss.at[n], rs.at[n], (batch_peer(step, 1), pi))

    def all_sum(buf, ss, rs):
        for n, step in reversed(list(enumerate(BATCH_STEPS))):
            frm = batch_peer(step, -1)
            arrived(buf.at[frm], ss.at[n], rs.at[n], (frm, pi))
        return jnp.sum(buf[...], axis=0)

    def message(e):
        return m.cx.at[e] if e == 1 else m.cx.at[e, :, :, pl.ds(0, CHUNK)]

    def col_start(e):
        all_send(message(e), m.cx_s.at[e], m.cx_r.at[e])

    def col_finish(e):
        return all_sum(message(e), m.cx_s.at[e], m.cx_r.at[e])

    def ring_send(buf, me, dev, ss, rs):
        for d in NEAR:
            send(buf.at[me], buf.at[me], ss.at[d - 1], rs.at[d - 1], dev((me + d) % SIDE))

    def ring_sum(buf, me, dev, ss, rs):
        for d in range(1, SIDE):
            frm = (me + SIDE - d) % SIDE
            arrived(buf.at[frm], ss.at[d - 1], rs.at[d - 1], dev(frm))
        return (buf[0] + buf[1]) + (buf[2] + buf[3])

    def along_x(x):
        return batch_dev(yi, x)

    def along_y(y):
        return batch_dev(y, xi)

    def row_start(e):
        for n, step in enumerate(PROTO_STEPS):
            send(m.rx.at[e, pi], m.rx.at[e, pi], m.rx_s.at[e, n], m.rx_r.at[e, n], proto_dev(proto_peer(step, 1)))

    def row_finish(e):
        for n, step in reversed(list(enumerate(PROTO_STEPS))):
            frm = proto_peer(step, -1)
            arrived(m.rx.at[e, frm], m.rx_s.at[e, n], m.rx_r.at[e, n], proto_dev(frm))
        return jnp.sum(m.rx[e], axis=0)

    def to_rows(acc_ref, e, first):
        for q in range(4):
            block = jnp.transpose(acc_ref[q * 128 : (q + 1) * 128, :])
            m.rx[e, pi, pl.ds(first + q, 1), :] = jnp.sum(block, axis=0, keepdims=True)

    def to_columns(ref, rows):
        for q in range(4):
            ref[q * 128 : (q + 1) * 128, :] = jnp.transpose(jnp.broadcast_to(rows[q : q + 1], (128, 128)))

    col_start(0)

    m.rowacc[...] = jnp.zeros_like(m.rowacc)
    m.smax[...] = jnp.zeros_like(m.smax)

    def student_chunk(j, carry):
        cols = cols_of(j)
        c = jnp.dot(m.st[...], m.pu[:, cols], preferred_element_type=F32)
        m.cos[:, cols] = c
        e = jnp.exp2(c * (LOG2E / STUDENT_TEMP))
        m.smax[...] = jnp.maximum(m.smax[...], jnp.sum(e.reshape(ROWS // 8, 8, CHUNK), axis=0))
        m.rowacc[...] += (e[:, 0:128] + e[:, 128:256]) + (e[:, 256:384] + e[:, 384:512])
        return carry

    lax.fori_loop(0, NCHUNK, student_chunk, 0)
    to_rows(m.rowacc, 0, 4)
    drain(len(started) - 15)

    def row_pass(e):
        def step(r, carry):
            rows = pl.ds(pl.multiple_of(r * 64, 64), 64)
            acc = jnp.zeros((8, 8, 128), F32)
            for q in range(COLS // 128):
                cols = slice(q * 128, (q + 1) * 128)
                product = m.expo[rows, cols].reshape(8, 8, 128) * m.pinv[:, cols]
                if e == 2:
                    m.expo[rows, cols] = product.reshape(64, 128)
                acc = acc + product
            m.rowacc[rows, :] = acc.reshape(64, 128)
            return carry

        lax.fori_loop(0, ROWS // 64, step, 0)
        to_rows(m.rowacc, e, 0)

    def col_pass(e):
        m.colacc[...] = jnp.zeros_like(m.colacc)

        def step(r, carry):
            rows = pl.ds(pl.multiple_of(r * 64, 64), 64)
            weights = m.csb[rows, :]
            for q in range(COLS // 128):
                cols = slice(q * 128, (q + 1) * 128)
                m.colacc[:, cols] += jnp.sum((m.expo[rows, cols] * weights).reshape(8, 8, 128), axis=0)
            return carry

        lax.fori_loop(0, ROWS // 64, step, 0)
        to_message(m.cx.at[e, bi])

    log_total = None
    for e in range(3):
        if e:
            col_pass(e)
            col_start(e)
            drain(len(started) - 15)
            if e == 2:
                def softmax_step(r, carry):
                    rows = pl.ds(pl.multiple_of(r * 64, 64), 64)
                    inv = m.itot[rows, :]
                    for q in range(COLS // 128):
                        cols = slice(q * 128, (q + 1) * 128)
                        m.prob[rows, cols] = jnp.exp2(m.cos[rows, cols] * (LOG2E / STUDENT_TEMP)) * inv
                    return carry

                lax.fori_loop(0, ROWS // 64, softmax_step, 0)
        sums = col_finish(e)
        total = sums[:, :CHUNK]
        if e == 1:
            mass = sums[0:2, CHUNK:]
        if e == 2:
            growth = jnp.max(total * inverse)
        inverse = 1.0 / total
        for j in range(NCHUNK):
            m.pinv[:, j * CHUNK : (j + 1) * CHUNK] = jnp.broadcast_to(inverse[j : j + 1], (8, CHUNK))
        if e == 1:
            m.rx[1, pi, 4:8, :] = jnp.zeros((4, 128), F32)
        if e == 2:
            m.rx[2, pi, 4:6, :] = jnp.zeros((2, 128), F32) + growth
            m.rx[2, pi, 6:8, :] = mass
        row_pass(e)
        row_start(e)
        drain(len(started) - 15)
        rows = row_finish(e)
        to_columns(m.csb, 1.0 / rows[0:4])
        if e == 0:
            to_columns(m.itot, 1.0 / rows[4:8])
            log_total = jnp.sum(jnp.log(rows[4:8]), axis=0, keepdims=True)
            bound = jnp.max(jnp.sum(m.smax[...], axis=0, keepdims=True)) * jnp.max(1.0 / rows[4:8])
            m.cx[1, bi, :, pl.ds(CHUNK, 128)] = jnp.zeros((NCHUNK, 128), F32) + bound

    bound = (jnp.max(m.rx[2][:, 4:6, :]) + jnp.max(m.rx[2][:, 6:8, :])) * (1.05 / (CROPS * STUDENT_TEMP))
    wire_scale, wire_unscale = WIRE_TOP / bound, bound * (1.0 / WIRE_TOP)

    def encode(values, scale):
        values = values * scale
        square = values * values
        e8 = square * square
        return (values * (e8 * e8)).astype(BF16)

    def decode(coded, unscale):
        coded = coded.astype(F32)
        root = jnp.exp2(jnp.log(jnp.maximum(jnp.abs(coded), 1e-37)) * (-8.0 / 9.0 * LOG2E))
        return (coded * root) * unscale

    m.tlacc[...] = jnp.zeros_like(m.tlacc)
    m.cg[...] = jnp.zeros_like(m.cg)

    def grad_chunk(j, carry):
        cols = cols_of(j)

        def rows_step(r, inner):
            rows = pl.ds(pl.multiple_of(r * 64, 64), 64)
            weights = m.csb[rows, :]
            tl = jnp.zeros((64, 128), F32)
            for i in range(4):
                sub = pl.ds(j * CHUNK + i * 128, 128)
                target = m.expo[rows, sub] * weights
                c = m.cos[rows, sub]
                prob = m.prob[rows, sub]
                tl = tl + target * c
                m.gl[rows, i * 128 : (i + 1) * 128] = ((prob - target) * (1.0 / (CROPS * STUDENT_TEMP))).astype(BF16)
            m.tlacc[...] += jnp.sum(tl.reshape(8, 8, 128), axis=0)
            return inner

        lax.fori_loop(0, ROWS // 64, rows_step, 0)
        g = m.gl[...]
        proto = m.pu[:, cols]
        part = jnp.dot(m.su[...], g, preferred_element_type=F32)
        m.gp[:, cols] = part
        m.cg[...] += lax.dot_general(proto, g, (((1,), (1,)), ((), ())), preferred_element_type=F32)
        m.colacc[:, cols] = jnp.sum((proto.astype(F32) * part).reshape(K // 8, 8, CHUNK), axis=0)
        return carry

    def first_rows(h, c, cols):
        c = (c + SIDE) % SIDE
        blocks = []
        for u in range(SIDE):
            y, x = (c, u) if h else (u, c)
            blocks.append(m.gp[pl.ds(row0(y, x), BLK), cols])
        return jnp.concatenate(blocks, axis=0)

    def second_rows(j, c):
        return m.t1[j, pl.ds(pl.multiple_of(((c + SIDE) % SIDE) * BLK, BLK), BLK), :]

    def first_send(j):
        h = j % 2
        i1, i2 = pos[h]
        for d in NEAR:
            m.s1[j, d - 1] = encode(first_rows(h, i1 + d, slice(j * CHUNK, (j + 1) * CHUNK)), wire_scale)
            to = batch_dev(*where(h, i1 + d, i2))
            send(m.s1.at[j, d - 1], m.r1.at[j, d - 1], m.rs1_s.at[j, d - 1], m.rs1_r.at[j, d - 1], to)

    def second_send(j):
        h = j % 2
        i1, i2 = pos[h]
        total = first_rows(h, i1, slice(j * CHUNK, (j + 1) * CHUNK))
        for d in range(1, SIDE):
            arrived(m.r1.at[j, d - 1], m.rs1_s.at[j, d - 1], m.rs1_r.at[j, d - 1], batch_dev(*where(h, i1 - d, i2)))
            total = total + decode(m.r1[j, d - 1], wire_unscale)
        m.t1[j] = total
        for d in NEAR:
            m.s2[j, d - 1] = encode(second_rows(j, i2 + d), wire_scale)
            to = batch_dev(*where(h, i1, i2 + d))
            send(m.s2.at[j, d - 1], m.r2.at[j, d - 1], m.rs2_s.at[j, d - 1], m.rs2_r.at[j, d - 1], to)

    def reduced(j):
        h = j % 2
        i1, i2 = pos[h]
        total = second_rows(j, i2)
        for d in range(1, SIDE):
            arrived(m.r2.at[j, d - 1], m.rs2_s.at[j, d - 1], m.rs2_r.at[j, d - 1], batch_dev(*where(h, i1, i2 - d)))
            total = total + decode(m.r2[j, d - 1], wire_unscale)
        return total

    for j in range(NCHUNK):
        grad_chunk(j, 0)
        first_send(j)
        if j >= LAG:
            second_send(j - LAG)
    for p in range(NP):
        m.cgb[p % 2, p // 2] = m.cg[p * BLK : (p + 1) * BLK, :]
    send(m.cgb.at[1 - ci], m.cgr, m.cg_s.at[7], m.cg_r.at[7], proto_dev(sibling))
    dot_rows = jnp.sum(m.su[...].astype(F32) * m.cg[...], axis=0, keepdims=True)
    for q in range(4):
        m.rx[3, pi, q : q + 1, :] = dot_rows[:, q * 128 : (q + 1) * 128]
    m.rx[3, pi, 4:8, :] = jnp.zeros((4, 128), F32)
    m.rx[3, pi, 4:5, :] = jnp.sum(m.tlacc[...], axis=0, keepdims=True)
    row_start(3)
    to_message(m.dx.at[xi])
    ring_send(m.dx, xi, along_x, m.d_s.at[0], m.d_r.at[0])

    arrived(m.cgr, m.cg_s.at[7], m.cg_r.at[7], proto_dev(sibling))
    m.cgm[...] = m.cgb[ci] + m.cgr[...]
    m.cgs[...] = encode(m.cgm[...], CROP_SCALE)
    for d in range(1, 8):
        to = (zi + d) % 8
        send(m.cgs.at[to], m.cgz.at[zi], m.cg_s.at[d - 1], m.cg_r.at[d - 1], proto_dev(to * 2 + ci))

    second_send(NCHUNK - LAG)
    m.dy[yi] = ring_sum(m.dx, xi, along_x, m.d_s.at[0], m.d_r.at[0])
    ring_send(m.dy, yi, along_y, m.d_s.at[1], m.d_r.at[1])
    second_send(NCHUNK - LAG + 1)

    rows = row_finish(3)
    loss_rows = rows[4:5] * (1.0 / STUDENT_TEMP) - log_total
    m.lx[bi] = jnp.broadcast_to(loss_rows, (8, 128))
    all_send(m.lx, m.l_s, m.l_r)
    for j in range(NCHUNK - LAG + 2, NCHUNK):
        second_send(j)
    drain(len(started) - 12)
    dots = ring_sum(m.dy, yi, along_y, m.d_s.at[1], m.d_r.at[1])

    loss_out[0, 0] = jnp.sum(all_sum(m.lx, m.l_s, m.l_r)[0:1]) * (-1.0 / CROPS)
    crop_part = m.cgm[zi]
    for d in range(1, 8):
        frm = (zi + 8 - d) % 8
        arrived(m.cgz.at[frm], m.cg_s.at[d - 1], m.cg_r.at[d - 1], proto_dev(frm * 2 + ci))
        crop_part = crop_part + decode(m.cgz[frm], 1.0 / CROP_SCALE)
    student_own = m.su[pl.ds(pl.multiple_of(pi * BLK, BLK), BLK), :].astype(F32)
    for q in range(4):
        cols = slice(q * 128, (q + 1) * 128)
        gs_out[:, cols] = (crop_part[:, cols] - student_own[:, cols] * rows[q : q + 1]) * m.sscale[:, cols]

    proto_rows = pl.ds(row0(yi, xi), BLK)
    for j in range(NCHUNK):
        cols = slice(j * CHUNK, (j + 1) * CHUNK)
        proto_own = m.pu[proto_rows, cols].astype(F32)
        gp_out[:, cols] = (reduced(j) - proto_own * dots[j : j + 1]) * m.pscale[:, cols]

    drain(len(started))


def shards(teacher_emb, student_emb, prototypes):
    hbm = pl.BlockSpec(memory_space=pl.ANY)
    vmem = pl.BlockSpec(memory_space=pltpu.VMEM)
    grad_proto, grad_student, loss = pl.pallas_call(
        body,
        out_shape=(
            pltpu.VMEM((BLK, COLS), F32),
            pltpu.VMEM((BLK, ROWS), F32),
            jax.ShapeDtypeStruct((1, 1), F32),
        ),
        in_specs=[hbm] * 3,
        out_specs=(vmem, vmem, pl.BlockSpec(memory_space=pltpu.SMEM)),
        scratch_shapes=[pltpu.VMEM(shape, dtype) for shape, dtype in SCRATCH.values()]
        + [pltpu.SemaphoreType.DMA(shape) for shape in SEMS.values()],
        compiler_params=pltpu.CompilerParams(
            collective_id=0, has_side_effects=True, vmem_limit_bytes=58 * 1024 * 1024
        ),
    )(teacher_emb, student_emb, prototypes)
    return grad_proto, grad_student, loss.reshape(())


def solution(mesh):
    in_specs = (P("proto", "batch"), P("proto", "batch"), P("batch", "proto"))
    out_specs = (P("batch", "proto"), P("proto", "batch"), P())
    return jax.shard_map(shards, mesh=mesh, in_specs=in_specs, out_specs=out_specs, check_vma=False)
```

```python
import types

import jax
import jax.numpy as jnp
from jax import lax
from jax.experimental import pallas as pl
from jax.experimental.pallas import tpu as pltpu
from jax.sharding import PartitionSpec as P

F32, BF16 = jnp.float32, jnp.bfloat16
MESH = pl.DeviceIdType.MESH
LOG2E = 1.4426950408889634
TEACHER_TEMP, STUDENT_TEMP, EPS = 0.07, 0.1, 1e-6
K, ROWS, COLS = 256, 512, 4096
CHUNK = 512
NCHUNK = COLS // CHUNK
SIDE = 4
NP = 16
BLK = K // 16
QUART = COLS // 4
NEAR = (2, 1, 3)
LAG = 5
RELAYED = (0, 1, 2)
CROPS = ROWS * SIDE * SIDE
WIRE_TOP = 8192.0
CROP_SCALE = WIRE_TOP * (CROPS * STUDENT_TEMP) / 2.1
MSGW = CHUNK + 128


def hops(step, size):
    return min(step, size - step)


BATCH_STEPS = sorted(
    ((dy, dx) for dy in range(SIDE) for dx in range(SIDE) if dy or dx), key=lambda s: -hops(s[0], SIDE) - hops(s[1], SIDE)
)
PROTO_STEPS = sorted(((dz, dc) for dz in range(8) for dc in range(2) if dz or dc), key=lambda s: -2 * hops(s[0], 8) - s[1])

SCRATCH = dict(
    praw=((K, COLS), BF16),
    traw=((K, ROWS), BF16),
    sraw=((K, ROWS), BF16),
    tt=((ROWS, K), BF16),
    st=((ROWS, K), BF16),
    su=((K, ROWS), BF16),
    pu=((K, COLS), BF16),
    pscale=((1, COLS), F32),
    sscale=((1, ROWS), F32),
    expo=((ROWS, COLS), F32),
    cos=((ROWS, COLS), F32),
    rowacc=((ROWS, 128), F32),
    colacc=((8, COLS), F32),
    pinv=((8, COLS), F32),
    csb=((ROWS, 128), F32),
    itot=((ROWS, 128), F32),
    gl=((ROWS, CHUNK), BF16),
    gp=((K, COLS), F32),
    cg=((K, ROWS), F32),
    cgb=((2, 8, BLK, ROWS), F32),
    cgr=((8, BLK, ROWS), F32),
    cgz=((8, BLK, ROWS), BF16),
    cgs=((8, BLK, ROWS), BF16),
    cgm=((8, BLK, ROWS), F32),
    cx=((3, SIDE * SIDE, NCHUNK, MSGW), F32),
    dx=((SIDE, NCHUNK, CHUNK), F32),
    dy=((SIDE, NCHUNK, CHUNK), F32),
    rx=((4, NP, 8, 128), F32),
    lx=((SIDE * SIDE, 8, 128), F32),
    s1=((NCHUNK, 3, SIDE * BLK, CHUNK), BF16),
    r1=((NCHUNK, 3, SIDE * BLK, CHUNK), BF16),
    t1=((NCHUNK, SIDE * BLK, CHUNK), F32),
    s2=((NCHUNK, 3, BLK, CHUNK), BF16),
    r2=((NCHUNK, 3, BLK, CHUNK), BF16),
    smax=((8, CHUNK), F32),
    prob=((ROWS, COLS), F32),
)
SEMS = dict(
    own=(3,),
    ag1_s=(4, 3),
    ag1_r=(4, 3),
    ag2_s=(4, 4, 4),
    ag2_r=(4, 4, 4),
    ts_s=(2, 16),
    ts_r=(2, 16),
    cx_s=(3, 15),
    cx_r=(3, 15),
    d_s=(2, 3),
    d_r=(2, 3),
    rx_s=(4, 15),
    rx_r=(4, 15),
    l_s=(15,),
    l_r=(15,),
    rs1_s=(NCHUNK, 3),
    rs1_r=(NCHUNK, 3),
    rs2_s=(NCHUNK, 3),
    rs2_r=(NCHUNK, 3),
    cg_s=(8,),
    cg_r=(8,),
)


def body(t_in, s_in, p_in, gp_out, gs_out, loss_out, *scratch):
    m = types.SimpleNamespace(**dict(zip(list(SCRATCH) + list(SEMS), scratch)))
    bi, pi = lax.axis_index("batch"), lax.axis_index("proto")
    yi, xi = bi // SIDE, bi % SIDE
    zi, ci = pi // 2, pi % 2
    started = []

    def batch_dev(y, x):
        return (y * SIDE + x, pi)

    def proto_dev(p):
        return (bi, p)

    def batch_peer(step, sign):
        return (yi + SIDE + sign * step[0]) % SIDE * SIDE + (xi + SIDE + sign * step[1]) % SIDE

    def proto_peer(step, sign):
        return (zi + 8 + sign * step[0]) % 8 * 2 + (ci + step[1]) % 2

    def rdma(src, dst, ssem, rsem, dev):
        return pltpu.make_async_remote_copy(
            src_ref=src, dst_ref=dst, send_sem=ssem, recv_sem=rsem, device_id=dev, device_id_type=MESH
        )

    def send(src, dst, ssem, rsem, dev):
        copy = rdma(src, dst, ssem, rsem, dev)
        copy.start()
        started.append(copy)

    def drain(count):
        for copy in started[:count]:
            copy.wait_send()
        del started[:count]

    def arrived(dst, ssem, rsem, dev):
        rdma(dst, dst, ssem, rsem, dev).wait_recv()

    barrier = pltpu.get_barrier_semaphore()
    peers = []
    for step in PROTO_STEPS:
        if step[1] == 0 or step[0] == 0:
            peers.append(proto_dev(proto_peer(step, 1)))
    for step in BATCH_STEPS:
        if step[0] == 0 or step[1] == 0:
            peers.append((batch_peer(step, 1), pi))
    for peer in peers:
        pl.semaphore_signal(barrier, inc=1, device_id=peer, device_id_type=MESH)
    pl.semaphore_wait(barrier, len(peers))

    def where(h, c1, c2):
        c1, c2 = (c1 + SIDE) % SIDE, (c2 + SIDE) % SIDE
        return (c2, c1) if h == 0 else (c1, c2)

    pos = ((xi, yi), (yi, xi))

    def row0(y, x):
        return pl.multiple_of((y * SIDE + x) * BLK, BLK)

    def piece(k, y, x):
        return m.praw.at[pl.ds(row0(y, x), BLK), pl.ds(k * QUART, QUART)]

    def half_piece(k, y, x, half):
        return m.praw.at[pl.ds(row0(y, x), BLK), pl.ds(k * QUART + half * (QUART // 2), QUART // 2)]

    def second_steps(k):
        return (1, 3) if k in RELAYED else NEAR

    own = [
        pltpu.make_async_copy(p_in, m.praw.at[pl.ds(row0(yi, xi), BLK), :], m.own.at[0]),
        pltpu.make_async_copy(t_in, m.traw.at[pl.ds(pl.multiple_of(pi * BLK, BLK), BLK), :], m.own.at[1]),
        pltpu.make_async_copy(s_in, m.sraw.at[pl.ds(pl.multiple_of(pi * BLK, BLK), BLK), :], m.own.at[2]),
    ]

    for k in range(4):
        i1, i2 = pos[k % 2]
        for d in NEAR:
            to = batch_dev(*where(k % 2, i1 + d, i2))
            send(p_in.at[:, pl.ds(k * QUART, QUART)], piece(k, yi, xi), m.ag1_s.at[k, d - 1], m.ag1_r.at[k, d - 1], to)
    for k in range(4):
        i1, i2 = pos[k % 2]
        for d in second_steps(k):
            to = batch_dev(*where(k % 2, i1, i2 + d))
            send(p_in.at[:, pl.ds(k * QUART, QUART)], piece(k, yi, xi), m.ag2_s.at[k, 0, d - 1], m.ag2_r.at[k, 0, d - 1], to)

    def ts_rows(ref, p):
        return ref.at[pl.ds(pl.multiple_of(p * BLK, BLK), BLK), :]

    sibling = zi * 2 + 1 - ci
    embeddings = ((t_in, m.traw), (s_in, m.sraw))
    for a, (src, ref) in enumerate(embeddings):
        for d in (4, 3, 5, 2, 6, 1, 7):
            peer = ((zi + d) % 8) * 2 + ci
            send(src, ts_rows(ref, pi), m.ts_s.at[a, d - 1], m.ts_r.at[a, d - 1], proto_dev(peer))
        send(src, ts_rows(ref, pi), m.ts_s.at[a, 7], m.ts_r.at[a, 7], proto_dev(sibling))
    for copy in own:
        copy.start()

    for k in range(4):
        h = k % 2
        i1, i2 = pos[h]
        for d in (1, 3, 2):
            y, x = where(h, i1 - d, i2)
            block = piece(k, y, x)
            arrived(block, m.ag1_s.at[k, d - 1], m.ag1_r.at[k, d - 1], batch_dev(y, x))
            for d2 in second_steps(k):
                send(block, block, m.ag2_s.at[k, d, d2 - 1], m.ag2_r.at[k, d, d2 - 1], batch_dev(*where(h, i1, i2 + d2)))

    def ts_forward(a):
        ref = embeddings[a][1]
        for d in (1, 7, 2, 6, 3, 5, 4):
            peer = ((zi + 8 - d) % 8) * 2 + ci
            rows = ts_rows(ref, peer)
            arrived(rows, m.ts_s.at[a, d - 1], m.ts_r.at[a, d - 1], proto_dev(peer))
            send(rows, rows, m.ts_s.at[a, 7 + d], m.ts_r.at[a, 7 + d], proto_dev(sibling))

    def ts_finish(a):
        ref = embeddings[a][1]
        own[1 + a].wait()
        arrived(ts_rows(ref, sibling), m.ts_s.at[a, 7], m.ts_r.at[a, 7], proto_dev(sibling))
        for d in range(1, 8):
            rows = ts_rows(ref, ((zi + 8 - d) % 8) * 2 + 1 - ci)
            arrived(rows, m.ts_s.at[a, 7 + d], m.ts_r.at[a, 7 + d], proto_dev(sibling))

    ts_forward(0)
    for k in RELAYED:
        h = k % 2
        i1, i2 = pos[h]
        for r in (0, 1, 3, 2):
            for half, d in enumerate((1, 3)):
                y, x = where(h, i1 - r, i2 - d)
                block = piece(k, y, x)
                arrived(block, m.ag2_s.at[k, r, d - 1], m.ag2_r.at[k, r, d - 1], batch_dev(y, x))
                block = half_piece(k, y, x, half)
                slot = 1 + 2 * half
                send(block, block, m.ag2_s.at[k, r, slot], m.ag2_r.at[k, r, slot], batch_dev(*where(h, i1, i2 + d)))
    ts_forward(1)

    def unit(values):
        values = values.astype(F32)
        factor = lax.rsqrt(jnp.sum(values * values, axis=0, keepdims=True) + EPS)
        return values * factor, factor

    ts_finish(0)
    teacher, unused = unit(m.traw[...])
    m.tt[...] = jnp.transpose(teacher).astype(BF16)
    ts_finish(1)
    student, factor = unit(m.sraw[...])
    m.sscale[...] = factor
    m.su[...] = student.astype(BF16)
    m.st[...] = jnp.transpose(student).astype(BF16)
    own[0].wait()

    def cols_of(j):
        return pl.ds(j * CHUNK if isinstance(j, int) else pl.multiple_of(j * CHUNK, CHUNK), CHUNK)

    def teacher_chunk(j, carry):
        cols = cols_of(j)
        proto, factor = unit(m.praw[:, cols])
        proto = proto.astype(BF16)
        m.pu[:, cols] = proto
        m.pscale[:, cols] = factor
        c = jnp.dot(m.tt[...], proto, preferred_element_type=F32)
        e = jnp.exp2(c * (LOG2E / TEACHER_TEMP))
        m.expo[:, cols] = e
        m.colacc[:, cols] = jnp.sum(e.reshape(ROWS // 8, 8, CHUNK), axis=0)
        return carry

    def to_message(ref):
        for j in range(NCHUNK):
            ref[j : j + 1, pl.ds(0, CHUNK)] = jnp.sum(m.colacc[:, j * CHUNK : (j + 1) * CHUNK], axis=0, keepdims=True)

    for k in range(4):
        h = k % 2
        i1, i2 = pos[h]
        for r in range(4):
            if k in RELAYED:
                y, x = where(h, i1 - r, i2 - 2)
                for half in range(2):
                    slot = 1 + 2 * half
                    arrived(half_piece(k, y, x, half), m.ag2_s.at[k, r, slot], m.ag2_r.at[k, r, slot], batch_dev(y, x))
                continue
            for d in (1, 3, 2):
                y, x = where(h, i1 - r, i2 - d)
                arrived(piece(k, y, x), m.ag2_s.at[k, r, d - 1], m.ag2_r.at[k, r, d - 1], batch_dev(y, x))
        lax.fori_loop(2 * k, 2 * k + 2, teacher_chunk, 0)
    to_message(m.cx.at[0, bi])

    def all_send(buf, ss, rs):
        for n, step in enumerate(BATCH_STEPS):
            send(buf.at[bi], buf.at[bi], ss.at[n], rs.at[n], (batch_peer(step, 1), pi))

    def all_sum(buf, ss, rs):
        for n, step in reversed(list(enumerate(BATCH_STEPS))):
            frm = batch_peer(step, -1)
            arrived(buf.at[frm], ss.at[n], rs.at[n], (frm, pi))
        return jnp.sum(buf[...], axis=0)

    def message(e):
        return m.cx.at[e] if e == 1 else m.cx.at[e, :, :, pl.ds(0, CHUNK)]

    def col_start(e):
        all_send(message(e), m.cx_s.at[e], m.cx_r.at[e])

    def col_finish(e):
        return all_sum(message(e), m.cx_s.at[e], m.cx_r.at[e])

    def ring_send(buf, me, dev, ss, rs):
        for d in NEAR:
            send(buf.at[me], buf.at[me], ss.at[d - 1], rs.at[d - 1], dev((me + d) % SIDE))

    def ring_sum(buf, me, dev, ss, rs):
        for d in range(1, SIDE):
            frm = (me + SIDE - d) % SIDE
            arrived(buf.at[frm], ss.at[d - 1], rs.at[d - 1], dev(frm))
        return (buf[0] + buf[1]) + (buf[2] + buf[3])

    def along_x(x):
        return batch_dev(yi, x)

    def along_y(y):
        return batch_dev(y, xi)

    def row_start(e):
        for n, step in enumerate(PROTO_STEPS):
            send(m.rx.at[e, pi], m.rx.at[e, pi], m.rx_s.at[e, n], m.rx_r.at[e, n], proto_dev(proto_peer(step, 1)))

    def row_finish(e):
        for n, step in reversed(list(enumerate(PROTO_STEPS))):
            frm = proto_peer(step, -1)
            arrived(m.rx.at[e, frm], m.rx_s.at[e, n], m.rx_r.at[e, n], proto_dev(frm))
        return jnp.sum(m.rx[e], axis=0)

    def to_rows(acc_ref, e, first):
        for q in range(4):
            block = jnp.transpose(acc_ref[q * 128 : (q + 1) * 128, :])
            m.rx[e, pi, pl.ds(first + q, 1), :] = jnp.sum(block, axis=0, keepdims=True)

    def to_columns(ref, rows):
        for q in range(4):
            ref[q * 128 : (q + 1) * 128, :] = jnp.transpose(jnp.broadcast_to(rows[q : q + 1], (128, 128)))

    col_start(0)

    m.rowacc[...] = jnp.zeros_like(m.rowacc)
    m.smax[...] = jnp.zeros_like(m.smax)

    def student_chunk(j, carry):
        cols = cols_of(j)
        c = jnp.dot(m.st[...], m.pu[:, cols], preferred_element_type=F32)
        m.cos[:, cols] = c
        e = jnp.exp2(c * (LOG2E / STUDENT_TEMP))
        m.smax[...] = jnp.maximum(m.smax[...], jnp.sum(e.reshape(ROWS // 8, 8, CHUNK), axis=0))
        m.rowacc[...] += (e[:, 0:128] + e[:, 128:256]) + (e[:, 256:384] + e[:, 384:512])
        return carry

    lax.fori_loop(0, NCHUNK, student_chunk, 0)
    to_rows(m.rowacc, 0, 4)
    drain(len(started) - 15)

    def row_pass(e):
        def step(r, carry):
            rows = pl.ds(pl.multiple_of(r * 64, 64), 64)
            acc = jnp.zeros((8, 8, 128), F32)
            for q in range(COLS // 128):
                cols = slice(q * 128, (q + 1) * 128)
                product = m.expo[rows, cols].reshape(8, 8, 128) * m.pinv[:, cols]
                if e == 2:
                    m.expo[rows, cols] = product.reshape(64, 128)
                acc = acc + product
            m.rowacc[rows, :] = acc.reshape(64, 128)
            return carry

        lax.fori_loop(0, ROWS // 64, step, 0)
        to_rows(m.rowacc, e, 0)

    def col_pass(e):
        m.colacc[...] = jnp.zeros_like(m.colacc)

        def step(r, carry):
            rows = pl.ds(pl.multiple_of(r * 64, 64), 64)
            weights = m.csb[rows, :]
            for q in range(COLS // 128):
                cols = slice(q * 128, (q + 1) * 128)
                m.colacc[:, cols] += jnp.sum((m.expo[rows, cols] * weights).reshape(8, 8, 128), axis=0)
            return carry

        lax.fori_loop(0, ROWS // 64, step, 0)
        to_message(m.cx.at[e, bi])

    log_total = None
    for e in range(3):
        if e:
            col_pass(e)
            col_start(e)
            drain(len(started) - 15)
            if e == 2:
                def softmax_step(r, carry):
                    rows = pl.ds(pl.multiple_of(r * 64, 64), 64)
                    inv = m.itot[rows, :]
                    for q in range(COLS // 128):
                        cols = slice(q * 128, (q + 1) * 128)
                        m.prob[rows, cols] = jnp.exp2(m.cos[rows, cols] * (LOG2E / STUDENT_TEMP)) * inv
                    return carry

                lax.fori_loop(0, ROWS // 64, softmax_step, 0)
        sums = col_finish(e)
        total = sums[:, :CHUNK]
        if e == 1:
            mass = sums[0:2, CHUNK:]
        if e == 2:
            growth = jnp.max(total * inverse)
        inverse = 1.0 / total
        for j in range(NCHUNK):
            m.pinv[:, j * CHUNK : (j + 1) * CHUNK] = jnp.broadcast_to(inverse[j : j + 1], (8, CHUNK))
        if e == 1:
            m.rx[1, pi, 4:8, :] = jnp.zeros((4, 128), F32)
        if e == 2:
            m.rx[2, pi, 4:6, :] = jnp.zeros((2, 128), F32) + growth
            m.rx[2, pi, 6:8, :] = mass
        row_pass(e)
        row_start(e)
        drain(len(started) - 15)
        if e == 2:
            def loss_step(r, carry):
                rows = pl.ds(pl.multiple_of(r * 64, 64), 64)
                acc = jnp.zeros((64, 128), F32)
                for q in range(COLS // 128):
                    cols = slice(q * 128, (q + 1) * 128)
                    acc = acc + m.expo[rows, cols] * m.cos[rows, cols]
                m.rowacc[rows, :] = acc
                return carry

            lax.fori_loop(0, ROWS // 64, loss_step, 0)
        rows = row_finish(e)
        to_columns(m.csb, 1.0 / rows[0:4])
        if e == 0:
            to_columns(m.itot, 1.0 / rows[4:8])
            log_total = jnp.sum(jnp.log(rows[4:8]), axis=0, keepdims=True)
            bound = jnp.max(jnp.sum(m.smax[...], axis=0, keepdims=True)) * jnp.max(1.0 / rows[4:8])
            m.cx[1, bi, :, pl.ds(CHUNK, 128)] = jnp.zeros((NCHUNK, 128), F32) + bound

    bound = (jnp.max(m.rx[2][:, 4:6, :]) + jnp.max(m.rx[2][:, 6:8, :])) * (1.05 / (CROPS * STUDENT_TEMP))
    wire_scale, wire_unscale = WIRE_TOP / bound, bound * (1.0 / WIRE_TOP)

    def encode(values, scale):
        values = values * scale
        square = values * values
        e8 = square * square
        return (values * (e8 * e8)).astype(BF16)

    def decode(coded, unscale):
        coded = coded.astype(F32)
        root = jnp.exp2(jnp.log(jnp.maximum(jnp.abs(coded), 1e-37)) * (-8.0 / 9.0 * LOG2E))
        return (coded * root) * unscale

    loss_rows = jnp.sum(m.csb[...] * m.rowacc[...], axis=0, keepdims=True) * (1.0 / STUDENT_TEMP)
    m.lx[bi] = jnp.broadcast_to(loss_rows - log_total * (1.0 / NP), (8, 128))

    m.cg[...] = jnp.zeros_like(m.cg)

    def grad_chunk(j, carry):
        cols = cols_of(j)

        def rows_step(r, inner):
            rows = pl.ds(pl.multiple_of(r * 64, 64), 64)
            weights = m.csb[rows, :]
            for i in range(4):
                sub = pl.ds(j * CHUNK + i * 128, 128)
                target = m.expo[rows, sub] * weights
                prob = m.prob[rows, sub]
                m.gl[rows, i * 128 : (i + 1) * 128] = ((prob - target) * (1.0 / (CROPS * STUDENT_TEMP))).astype(BF16)
            return inner

        lax.fori_loop(0, ROWS // 64, rows_step, 0)
        g = m.gl[...]
        proto = m.pu[:, cols]
        part = jnp.dot(m.su[...], g, preferred_element_type=F32)
        m.gp[:, cols] = part
        m.cg[...] += lax.dot_general(proto, g, (((1,), (1,)), ((), ())), preferred_element_type=F32)
        m.colacc[:, cols] = jnp.sum((proto.astype(F32) * part).reshape(K // 8, 8, CHUNK), axis=0)
        return carry

    def first_rows(h, c, cols):
        c = (c + SIDE) % SIDE
        blocks = []
        for u in range(SIDE):
            y, x = (c, u) if h else (u, c)
            blocks.append(m.gp[pl.ds(row0(y, x), BLK), cols])
        return jnp.concatenate(blocks, axis=0)

    def second_rows(j, c):
        return m.t1[j, pl.ds(pl.multiple_of(((c + SIDE) % SIDE) * BLK, BLK), BLK), :]

    def first_send(j):
        h = j % 2
        i1, i2 = pos[h]
        for d in NEAR:
            m.s1[j, d - 1] = encode(first_rows(h, i1 + d, slice(j * CHUNK, (j + 1) * CHUNK)), wire_scale)
            to = batch_dev(*where(h, i1 + d, i2))
            send(m.s1.at[j, d - 1], m.r1.at[j, d - 1], m.rs1_s.at[j, d - 1], m.rs1_r.at[j, d - 1], to)

    def second_send(j):
        h = j % 2
        i1, i2 = pos[h]
        total = first_rows(h, i1, slice(j * CHUNK, (j + 1) * CHUNK))
        for d in range(1, SIDE):
            arrived(m.r1.at[j, d - 1], m.rs1_s.at[j, d - 1], m.rs1_r.at[j, d - 1], batch_dev(*where(h, i1 - d, i2)))
            total = total + decode(m.r1[j, d - 1], wire_unscale)
        m.t1[j] = total
        for d in NEAR:
            m.s2[j, d - 1] = encode(second_rows(j, i2 + d), wire_scale)
            to = batch_dev(*where(h, i1, i2 + d))
            send(m.s2.at[j, d - 1], m.r2.at[j, d - 1], m.rs2_s.at[j, d - 1], m.rs2_r.at[j, d - 1], to)

    def reduced(j):
        h = j % 2
        i1, i2 = pos[h]
        total = second_rows(j, i2)
        for d in range(1, SIDE):
            arrived(m.r2.at[j, d - 1], m.rs2_s.at[j, d - 1], m.rs2_r.at[j, d - 1], batch_dev(*where(h, i1, i2 - d)))
            total = total + decode(m.r2[j, d - 1], wire_unscale)
        return total

    for j in range(NCHUNK):
        grad_chunk(j, 0)
        first_send(j)
        if j == 0:
            all_send(m.lx, m.l_s, m.l_r)
        if j >= LAG:
            second_send(j - LAG)
    for p in range(NP):
        m.cgb[p % 2, p // 2] = m.cg[p * BLK : (p + 1) * BLK, :]
    send(m.cgb.at[1 - ci], m.cgr, m.cg_s.at[7], m.cg_r.at[7], proto_dev(sibling))
    dot_rows = jnp.sum(m.su[...].astype(F32) * m.cg[...], axis=0, keepdims=True)
    for q in range(4):
        m.rx[3, pi, q : q + 1, :] = dot_rows[:, q * 128 : (q + 1) * 128]
    m.rx[3, pi, 4:8, :] = jnp.zeros((4, 128), F32)
    m.rx[3, pi, 4:5, :] = all_sum(m.lx, m.l_s, m.l_r)[0:1]
    row_start(3)
    to_message(m.dx.at[xi])
    ring_send(m.dx, xi, along_x, m.d_s.at[0], m.d_r.at[0])

    arrived(m.cgr, m.cg_s.at[7], m.cg_r.at[7], proto_dev(sibling))
    m.cgm[...] = m.cgb[ci] + m.cgr[...]
    m.cgs[...] = encode(m.cgm[...], CROP_SCALE)
    for d in range(1, 8):
        to = (zi + d) % 8
        send(m.cgs.at[to], m.cgz.at[zi], m.cg_s.at[d - 1], m.cg_r.at[d - 1], proto_dev(to * 2 + ci))

    second_send(NCHUNK - LAG)
    m.dy[yi] = ring_sum(m.dx, xi, along_x, m.d_s.at[0], m.d_r.at[0])
    ring_send(m.dy, yi, along_y, m.d_s.at[1], m.d_r.at[1])
    second_send(NCHUNK - LAG + 1)

    for j in range(NCHUNK - LAG + 2, NCHUNK):
        second_send(j)
    drain(len(started) - 12)
    dots = ring_sum(m.dy, yi, along_y, m.d_s.at[1], m.d_r.at[1])

    rows = row_finish(3)
    loss_out[0, 0] = jnp.sum(rows[4:5]) * (-1.0 / CROPS)
    crop_part = m.cgm[zi]
    for d in range(1, 8):
        frm = (zi + 8 - d) % 8
        arrived(m.cgz.at[frm], m.cg_s.at[d - 1], m.cg_r.at[d - 1], proto_dev(frm * 2 + ci))
        crop_part = crop_part + decode(m.cgz[frm], 1.0 / CROP_SCALE)
    student_own = m.su[pl.ds(pl.multiple_of(pi * BLK, BLK), BLK), :].astype(F32)
    for q in range(4):
        cols = slice(q * 128, (q + 1) * 128)
        gs_out[:, cols] = (crop_part[:, cols] - student_own[:, cols] * rows[q : q + 1]) * m.sscale[:, cols]

    proto_rows = pl.ds(row0(yi, xi), BLK)
    for j in range(NCHUNK):
        cols = slice(j * CHUNK, (j + 1) * CHUNK)
        proto_own = m.pu[proto_rows, cols].astype(F32)
        gp_out[:, cols] = (reduced(j) - proto_own * dots[j : j + 1]) * m.pscale[:, cols]

    drain(len(started))


def shards(teacher_emb, student_emb, prototypes):
    hbm = pl.BlockSpec(memory_space=pl.ANY)
    vmem = pl.BlockSpec(memory_space=pltpu.VMEM)
    grad_proto, grad_student, loss = pl.pallas_call(
        body,
        out_shape=(
            pltpu.VMEM((BLK, COLS), F32),
            pltpu.VMEM((BLK, ROWS), F32),
            jax.ShapeDtypeStruct((1, 1), F32),
        ),
        in_specs=[hbm] * 3,
        out_specs=(vmem, vmem, pl.BlockSpec(memory_space=pltpu.SMEM)),
        scratch_shapes=[pltpu.VMEM(shape, dtype) for shape, dtype in SCRATCH.values()]
        + [pltpu.SemaphoreType.DMA(shape) for shape in SEMS.values()],
        compiler_params=pltpu.CompilerParams(
            collective_id=0, has_side_effects=True, vmem_limit_bytes=58 * 1024 * 1024
        ),
    )(teacher_emb, student_emb, prototypes)
    return grad_proto, grad_student, loss.reshape(())


def solution(mesh):
    in_specs = (P("proto", "batch"), P("proto", "batch"), P("batch", "proto"))
    out_specs = (P("batch", "proto"), P("proto", "batch"), P())
    return jax.shard_map(shards, mesh=mesh, in_specs=in_specs, out_specs=out_specs, check_vma=False)
```
